128 devices in a mesh: expert: 8 (over z, x_hi), replica: 16 (over y, x_lo, core).
Axes of the slice: x: 4 (x_hi: 2, x_lo: 2; x = x_hi * 2 + x_lo), y: 4, z: 4, core: 2. Of those that a mesh axis runs over, the one named last changes fastest.
Arguments:
- tokens: bfloat16 [32768, 512], P(('expert', 'replica')), may hold values from -6 to 6
- expert_ids: int32 [32768, 2], P(('expert', 'replica')), may hold values from 0 to 23, all different within a row; in each aligned block of 256 rows (0 to 255, 256 to 511, ...) at most 48 rows name the same one
- gates: float32 [32768, 2], P(('expert', 'replica')), may hold values from 0.2 to 1
- cotangent: bfloat16 [32768, 512], P(('expert', 'replica')), may hold values from -3 to 3
- w_gate: bfloat16 [24, 512, 2048], P('expert'), may hold values from -0.25 to 0.25
- w_up: bfloat16 [24, 512, 2048], P('expert'), may hold values from -0.25 to 0.25
- w_down: bfloat16 [24, 2048, 512], P('expert'), may hold values from -0.125 to 0.125
Outputs:
- mixed: bfloat16 [32768, 512], P(('expert', 'replica'))
- token_grad: bfloat16 [32768, 512], P(('expert', 'replica'))
- gate_grad: bfloat16 [24, 512, 2048], P('expert', None, 'replica')
- up_grad: bfloat16 [24, 512, 2048], P('expert', None, 'replica')
- down_grad: bfloat16 [24, 2048, 512], P('expert', 'replica')
The draws below stay inside these ranges and needn't reach their ends.
Inputs may be any that keep to these rules, and one draw needn't show every extreme that they name: `expert_ids`: each token names two different experts. Among the 512 entries of one device's tokens, no expert is named more than 48 times, and in some devices some expert is named exactly 48 times.
All inputs are finite; a program needn't handle non-finite values.
Results may differ from the reference program's by a relative error of at most 0.022.
Values may be sent and summed in bfloat16 or wider, within the bound.
No kernel may reach another device: no remote copies, remote signals or barrier semaphores. Data moves between devices by JAX's collectives and lax.ppermute only.
A program may use at most 128 MiB of HBM per device.

```python
import math
import jax
import jax.numpy as jnp
import numpy as np
from jax import lax

D = 512
FF = 2048
TOK_DEV = 256
EXPERTS = 24
CAP = 48
TOKENS = 32768
N_EXPERT = 8
N_REPLICA = 16


def block_scale(stream_key, dims, shards, least, high):
    loudness = 1.0
    for position, parts in shards:
        heights = jax.random.uniform(jax.random.fold_in(jax.random.fold_in(stream_key, 6), position), (parts,), jnp.float32, least / len(shards), high / len(shards))
        loudness = loudness * jnp.repeat(jnp.exp(heights), dims[position] // parts).reshape((-1,) + (1,) * (len(dims) - 1 - position))
    return loudness


def deal_out(key, own, number, rows, number_of, top, reach, lean):
    order = jax.random.permutation(key, number_of)
    packed, ordinary = load_shares(number_of, rows * top, reach, lean, True), load_shares(number_of, rows * top, reach, lean, False)
    places = jnp.arange(number_of)

    def named(lengths, turn):
        used = int((lengths > 0).sum())
        fixed = max(1, used // 4)
        passed = fixed + (places - fixed + turn * (used - fixed)) % max(1, number_of - fixed)
        return jnp.zeros((number_of,), jnp.int32).at[order[jnp.where(places < fixed, places, passed)]].set(jnp.asarray(lengths, jnp.int32))

    lengths = jnp.where(number % 4 == 0, named(packed, number // 4), named(ordinary, number - number // 4 - 1))
    mixed = jax.random.permutation(jax.random.fold_in(own, 3), number_of)
    source_of, receiver = mixed[0:number_of // 2 * 2:2], mixed[1:number_of // 2 * 2:2]
    room = jnp.minimum(lengths[source_of] - 1, reach - lengths[receiver]) // 2
    room = jnp.where((source_of == order[0]) | (receiver == order[0]) | (lengths[receiver] == 0), 0, jnp.maximum(room, 0))
    passed = jax.random.randint(jax.random.fold_in(own, 4), (number_of // 2,), 0, 1 << 20) % (room + 1)
    lengths = lengths.at[source_of].add(-passed).at[receiver].add(passed)
    items = jnp.searchsorted(jnp.cumsum(lengths), jnp.arange(rows * top), side="right").astype(jnp.int32)
    table = items.reshape(top, rows).T
    table = table[jax.random.permutation(jax.random.fold_in(own, 1), rows)]
    turn = jax.random.randint(jax.random.fold_in(own, 2), (rows, 1), 0, top)
    return jnp.take_along_axis(table, (jnp.arange(top)[None, :] + turn) % top, axis=1)


def load_shares(number_of, total, most, skew, full):
    portions = [(1 << 20) // math.isqrt(rank ** skew) + 1 for rank in range(1, number_of + 1)]
    largest = most if full else min(most, max(-(-total // number_of), total * portions[0] // sum(portions)))
    least = 1 if total - largest >= number_of - 1 else 0
    counts, surplus = [largest] + [least] * (number_of - 1), total - largest - least * (number_of - 1)
    while surplus > 0:
        movable = [i for i in range(1, number_of) if counts[i] < largest] or [i for i in range(1, number_of) if counts[i] < most]
        whole, budget = sum([portions[i] for i in movable]), surplus
        for i in movable:
            addition = min(most - counts[i], max(1, budget * portions[i] // whole), surplus)
            counts[i] = counts[i] + addition
            surplus = surplus - addition
    return np.array(counts)


def scatter_about(key, dims, width, most, split=(), kind=jnp.bfloat16):
    entries = width * jax.random.normal(key, dims, jnp.float32)
    if split:
        entries = entries * block_scale(key, dims, split, -0.22, 0.18)
    return jnp.clip(entries, -most, most).astype(kind)


def setup_inputs(seed: int = 0) -> dict:
    key_list = jax.random.split(jax.random.key(seed), 8)
    tokens = scatter_about(key_list[0], (TOKENS, D), 1.0, 6.0, ((0, 128),))
    expert_ids_keys = jax.random.split(jax.random.fold_in(key_list[1], 1), TOKENS // TOK_DEV)
    expert_ids_turns = jax.random.permutation(jax.random.fold_in(key_list[1], 3), TOKENS // TOK_DEV)
    expert_ids = jax.vmap(lambda own, number: deal_out(jax.random.fold_in(key_list[1], 2), own, number, TOK_DEV, EXPERTS, 2, CAP, 2))(expert_ids_keys, expert_ids_turns).reshape((TOKENS, 2))
    gates = jnp.clip(0.2 + 0.8 * jax.random.uniform(key_list[2], (TOKENS, 2), jnp.float32) ** block_scale(key_list[2], (TOKENS, 2), ((0, 128),), -0.2, 0.2), 0.2, 1.0)
    cotangent = scatter_about(key_list[3], (TOKENS, D), 0.5, 3.0, ((0, 128),))
    w_gate = scatter_about(key_list[4], (EXPERTS, D, FF), D ** -0.5, 0.25, ((0, 8),))
    w_up = scatter_about(key_list[5], (EXPERTS, D, FF), D ** -0.5, 0.25, ((0, 8),))
    w_down = scatter_about(key_list[6], (EXPERTS, FF, D), FF ** -0.5, 0.125, ((0, 8),))
    return {"tokens": tokens, "expert_ids": expert_ids, "gates": gates, "cotangent": cotangent, "w_gate": w_gate, "w_up": w_up, "w_down": w_down}


def slot_of(flat_ids, experts, capacity):
    onehot = (flat_ids[:, None] == jnp.arange(experts, dtype=jnp.int32)[None, :]).astype(jnp.int32)
    before = jnp.cumsum(onehot, axis=0) - onehot
    return (flat_ids * capacity + jnp.sum(before * onehot, axis=1)).astype(jnp.int32)


def summed_parts(partial_value):
    rounded = lax.optimization_barrier(partial_value.astype(jnp.bfloat16))
    return jnp.sum(rounded.astype(jnp.float32), axis=0).astype(jnp.bfloat16)


def per_expert(operands):
    slot_rows, slot_grads, weight_gate, weight_up, weight_down = operands
    high = lax.Precision.HIGHEST
    rows_wide = slot_rows.astype(jnp.float32)
    grads_wide = slot_grads.astype(jnp.float32)
    gate_wide = weight_gate.astype(jnp.float32)
    up_wide = weight_up.astype(jnp.float32)
    down_wide = weight_down.astype(jnp.float32)
    pre_gate = jnp.einsum('rsd,df->rsf', rows_wide, gate_wide, precision=high)
    pre_up = jnp.einsum('rsd,df->rsf', rows_wide, up_wide, precision=high)
    hidden = (jax.nn.silu(pre_gate) * pre_up).astype(jnp.bfloat16)
    hidden_wide = hidden.astype(jnp.float32)
    expert_out = jnp.einsum('rsf,fd->rsd', hidden_wide, down_wide, precision=high).astype(jnp.bfloat16)
    grad_hidden = jnp.einsum('rsd,fd->rsf', grads_wide, down_wide, precision=high)
    sigmoid_gate = jax.nn.sigmoid(pre_gate)
    grad_pre_gate = (grad_hidden * pre_up * sigmoid_gate * (1.0 + pre_gate * (1.0 - sigmoid_gate))).astype(jnp.bfloat16)
    grad_pre_up = (grad_hidden * jax.nn.silu(pre_gate)).astype(jnp.bfloat16)
    pg_wide = grad_pre_gate.astype(jnp.float32)
    pu_wide = grad_pre_up.astype(jnp.float32)
    in_grad = (jnp.einsum('rsf,df->rsd', pg_wide, gate_wide, precision=high)
               + jnp.einsum('rsf,df->rsd', pu_wide, up_wide, precision=high)).astype(jnp.bfloat16)
    gate_part = jnp.einsum('rsd,rsf->rdf', rows_wide, pg_wide, precision=high)
    up_part = jnp.einsum('rsd,rsf->rdf', rows_wide, pu_wide, precision=high)
    down_part = jnp.einsum('rsf,rsd->rfd', hidden_wide, grads_wide, precision=high)
    return expert_out, in_grad, summed_parts(gate_part), summed_parts(up_part), summed_parts(down_part)


def reference(tokens, expert_ids, gates, cotangent, w_gate, w_up, w_down):
    blocks = N_EXPERT * N_REPLICA
    tok_blocks = tokens.reshape(blocks, TOK_DEV, D)
    cot_blocks = cotangent.reshape(blocks, TOK_DEV, D)
    id_blocks = expert_ids.reshape(blocks, 2 * TOK_DEV)
    gate_blocks = gates.reshape(blocks, 2 * TOK_DEV)
    slot_table = jax.vmap(lambda flat_ids: slot_of(flat_ids, EXPERTS, CAP))(id_blocks)
    owner_token = jnp.arange(2 * TOK_DEV, dtype=jnp.int32) // 2
    entry_rows = tok_blocks[:, owner_token]
    entry_grads = (gate_blocks[:, :, None] * cot_blocks[:, owner_token].astype(jnp.float32)).astype(jnp.bfloat16)

    def place(values, slot_list):
        return jnp.zeros((EXPERTS * CAP, D), jnp.bfloat16).at[slot_list].set(values)

    sent_rows = jax.vmap(place)(entry_rows, slot_table)
    sent_grads = jax.vmap(place)(entry_grads, slot_table)

    def by_expert(buffer):
        shaped = buffer.reshape(N_EXPERT, N_REPLICA, EXPERTS, CAP, D).transpose(2, 1, 0, 3, 4)
        return shaped.reshape(EXPERTS, N_REPLICA, N_EXPERT * CAP, D)

    results = lax.map(per_expert, (by_expert(sent_rows), by_expert(sent_grads), w_gate, w_up, w_down))

    def by_source(stacked):
        shaped = stacked.reshape(EXPERTS, N_REPLICA, N_EXPERT, CAP, D).transpose(2, 1, 0, 3, 4)
        return shaped.reshape(blocks, EXPERTS * CAP, D)

    pick_rows = jax.vmap(lambda buffer, slot_list: buffer[slot_list])
    back_out = pick_rows(by_source(results[0]), slot_table).reshape(blocks, TOK_DEV, 2, D)
    back_grad = pick_rows(by_source(results[1]), slot_table).reshape(blocks, TOK_DEV, 2, D)
    weights_two = gates.reshape(blocks, TOK_DEV, 2)[:, :, :, None]
    mixed = jnp.sum(weights_two * back_out.astype(jnp.float32), axis=2).astype(jnp.bfloat16).reshape(TOKENS, D)
    token_grad = jnp.sum(back_grad.astype(jnp.float32), axis=2).astype(jnp.bfloat16).reshape(TOKENS, D)
    return mixed, token_grad, results[2], results[3], results[4]
```

```python
import functools

import jax
import jax.numpy as jnp
from jax import lax
from jax.experimental import pallas as pl
from jax.experimental.pallas import tpu as pltpu
from jax.sharding import PartitionSpec as P

CAP = 48
N_EXPERT = 8
LOCAL = 3
ROWS = N_EXPERT * CAP
D = 512
BLK = 128
STEPS = (2, 1, 3, 0)
F32 = jnp.float32
BF16 = jnp.bfloat16
VMEM_LIMIT = 48 * 1024 * 1024


def dot(a, b, ca=1, cb=0):
    return lax.dot_general(a, b, (((ca,), (cb,)), ((), ())), preferred_element_type=F32)


def expert_of(me, rel, j):
    dest = ((((me >> 1) + (rel >> 1)) & 3) << 1) | ((me ^ rel) & 1)
    return dest * LOCAL + j


def over_expert(rel, back):
    dz, dh = rel >> 1, rel & 1
    pairs = []
    for z in range(4):
        for h in range(2):
            a, b = z * 2 + h, ((z + dz) % 4) * 2 + (h ^ dh)
            pairs.append((b, a) if back else (a, b))
    return pairs


def over_replica(dy, flip_x, flip_core):
    pairs = []
    for y in range(4):
        for x in range(2):
            for c in range(2):
                pairs.append(
                    ((y * 2 + x) * 2 + c, (((y + dy) % 4) * 2 + (x ^ flip_x)) * 2 + (c ^ flip_core))
                )
    return pairs


CORE = over_replica(0, 0, 1)
UP = over_replica(1, 0, 0)
DOWN = over_replica(3, 0, 0)
ACROSS = over_replica(0, 1, 0)


def dispatch_kernel(j, me_ref, ids_ref, gates_ref, tokens_ref, cot_ref, *out_refs):
    me = me_ref[0]
    tok = ids_ref.shape[1]
    rel = lax.broadcasted_iota(jnp.int32, (N_EXPERT, tok), 0)
    want = expert_of(me, rel, j)
    hit0 = ids_ref[0:1, :] == want
    hit1 = ids_ref[1:2, :] == want
    hit = jnp.where(hit0 | hit1, 1.0, 0.0).astype(F32)
    gate = jnp.where(hit0, gates_ref[0:1, :], jnp.where(hit1, gates_ref[1:2, :], 0.0))
    earlier = lax.broadcasted_iota(jnp.int32, (tok, tok), 0) < lax.broadcasted_iota(
        jnp.int32, (tok, tok), 1
    )
    before = dot(hit.astype(BF16), jnp.where(earlier, 1.0, 0.0).astype(BF16))
    place = jnp.where(hit > 0.0, before, -1.0).astype(jnp.int32)
    slot = lax.broadcasted_iota(jnp.int32, (CAP, tok), 0)
    picks, weights = [], []
    for r in range(N_EXPERT):
        sel = slot == place[r : r + 1, :]
        picks.append(jnp.where(sel, 1.0, 0.0).astype(BF16))
        weights.append(
            jnp.sum(jnp.where(sel, gate[r : r + 1, :], 0.0), axis=1, keepdims=True)
        )
    pick = jnp.concatenate(picks, axis=0)
    weight = jnp.concatenate(weights, axis=0)
    rows = dot(pick, tokens_ref[...]).astype(BF16)
    grads = (weight * dot(pick, cot_ref[...])).astype(BF16)
    for r in range(N_EXPERT):
        out_refs[r][0] = rows[r * CAP : (r + 1) * CAP]
        out_refs[r][1] = grads[r * CAP : (r + 1) * CAP]


def dispatch(j, me, ids_t, gates_t, tokens, cot):
    vmem = pl.BlockSpec(memory_space=pltpu.VMEM)
    return pl.pallas_call(
        functools.partial(dispatch_kernel, j),
        in_specs=[pl.BlockSpec(memory_space=pltpu.SMEM)] + [vmem] * 4,
        out_specs=[vmem] * N_EXPERT,
        out_shape=[jax.ShapeDtypeStruct((2, CAP, D), BF16)] * N_EXPERT,
        compiler_params=pltpu.CompilerParams(vmem_limit_bytes=VMEM_LIMIT),
        cost_estimate=pl.CostEstimate(flops=2 * 10**9, bytes_accessed=2 * 10**6, transcendentals=0),
        name=f"dispatch{j}",
    )(me, ids_t, gates_t, tokens, cot)


def expert_kernel(
    tbl_ref, own_ref, oth_ref, wg0, wg1, wu0, wu1, wd0, wd1,
    s2a, s2b, s1a, s1b, s3a, s3b, s0a, s0b, ret_own, ret_oth,
    x_s, g_s, xt_s, gt_s, eo_s, ig_s,
):
    i = pl.program_id(0)

    @pl.when(i == 0)
    def _():
        for k, ref in enumerate((own_ref, oth_ref)):
            x_s[k * ROWS : (k + 1) * ROWS, :] = ref[:, 0].reshape(ROWS, D)
            g_s[k * ROWS : (k + 1) * ROWS, :] = ref[:, 1].reshape(ROWS, D)
        xt_s[...] = x_s[...].T
        gt_s[...] = g_s[...].T
        eo_s[...] = jnp.zeros_like(eo_s)
        ig_s[...] = jnp.zeros_like(ig_s)

    wg = jnp.concatenate([wg0[...], wg1[...]], axis=1)
    wu = jnp.concatenate([wu0[...], wu1[...]], axis=1)
    wd = jnp.concatenate([wd0[...], wd1[...]], axis=0)
    x = x_s[...]
    g = g_s[...]
    pre_gate = dot(x, wg)
    pre_up = dot(x, wu)
    grad_hidden = dot(g, wd, 1, 1)
    sig = jax.nn.sigmoid(pre_gate)
    silu = pre_gate * sig
    hidden = (silu * pre_up).astype(BF16)
    grad_gate = (grad_hidden * pre_up * sig * (1.0 + pre_gate * (1.0 - sig))).astype(BF16)
    grad_up = (grad_hidden * silu).astype(BF16)
    part_gate = dot(xt_s[...], grad_gate).astype(BF16)
    part_up = dot(xt_s[...], grad_up).astype(BF16)
    part_down = dot(gt_s[...], hidden).astype(BF16)

    def keep(ref, lane):
        for k, part in enumerate((part_gate, part_up, part_down)):
            ref[k * D : (k + 1) * D, :] = part[:, lane * BLK : (lane + 1) * BLK]

    for step, (a, b) in enumerate(((s2a, s2b), (s1a, s1b), (s3a, s3b), (s0a, s0b))):

        @pl.when(i == step)
        def _(a=a, b=b):
            keep(a, 0)
            keep(b, 1)

    eo_s[...] += dot(hidden, wd)
    ig_s[...] += dot(grad_gate, wg, 1, 1) + dot(grad_up, wu, 1, 1)

    @pl.when(i == 3)
    def _():
        for k, ref in enumerate((ret_own, ret_oth)):
            ref[0] = eo_s[k * ROWS : (k + 1) * ROWS, :].astype(BF16)
            ref[1] = ig_s[k * ROWS : (k + 1) * ROWS, :].astype(BF16)


def expert(j, tbl, own, oth, w_gate, w_up, w_down):
    rows = 2 * ROWS

    def fixed(shape):
        return pl.BlockSpec(shape, lambda i, tbl: (0,) * len(shape))

    def columns(k):
        return pl.BlockSpec((None, D, BLK), lambda i, tbl: (j, 0, tbl[2 * i + k]))

    def lines(k):
        return pl.BlockSpec((None, BLK, D), lambda i, tbl: (j, tbl[2 * i + k], 0))

    chunk, ret = (3 * D, BLK), (2, ROWS, D)
    out_shapes = [chunk] * 8 + [ret] * 2
    return pl.pallas_call(
        expert_kernel,
        grid_spec=pltpu.PrefetchScalarGridSpec(
            num_scalar_prefetch=1,
            grid=(4,),
            in_specs=[fixed(own.shape), fixed(oth.shape)]
            + [columns(0), columns(1), columns(0), columns(1), lines(0), lines(1)],
            out_specs=[fixed(s) for s in out_shapes],
            scratch_shapes=[
                pltpu.VMEM((rows, D), BF16),
                pltpu.VMEM((rows, D), BF16),
                pltpu.VMEM((D, rows), BF16),
                pltpu.VMEM((D, rows), BF16),
                pltpu.VMEM((rows, D), F32),
                pltpu.VMEM((rows, D), F32),
            ],
        ),
        out_shape=[jax.ShapeDtypeStruct(s, BF16) for s in out_shapes],
        compiler_params=pltpu.CompilerParams(
            dimension_semantics=("arbitrary",), vmem_limit_bytes=VMEM_LIMIT
        ),
        cost_estimate=pl.CostEstimate(
            flops=9 * 2 * rows * D * 1024, bytes_accessed=9 * 10**6, transcendentals=rows * 1024
        ),
        name=f"expert{j}",
    )(tbl, own, oth, w_gate, w_gate, w_up, w_up, w_down, w_down)


def back_kernel(own_ref, oth_ref, *out_refs):
    for r in range(N_EXPERT):
        for k in range(2):
            rows = pl.ds(r * CAP, CAP)
            out_refs[r][k] = (own_ref[k, rows].astype(F32) + oth_ref[k, rows].astype(F32)).astype(BF16)


def back(j, own, oth):
    vmem = pl.BlockSpec(memory_space=pltpu.VMEM)
    return pl.pallas_call(
        back_kernel,
        in_specs=[vmem] * 2,
        out_specs=[vmem] * N_EXPERT,
        out_shape=[jax.ShapeDtypeStruct((2, CAP, D), BF16)] * N_EXPERT,
        compiler_params=pltpu.CompilerParams(vmem_limit_bytes=VMEM_LIMIT),
        cost_estimate=pl.CostEstimate(flops=10**6, bytes_accessed=3 * 10**6, transcendentals=0),
        name=f"back{j}",
    )(own, oth)


def combine_kernel(me_ref, ids_ref, gates_ref, *refs):
    rows, (mixed_ref, grad_ref, out_s, in_s) = refs[:-4], refs[-4:]
    me = me_ref[0]
    tok = ids_ref.shape[0]
    for n, ref in enumerate(rows):
        out_s[n * CAP : (n + 1) * CAP, :] = ref[0]
        in_s[n * CAP : (n + 1) * CAP, :] = ref[1]
    lane = lax.broadcasted_iota(jnp.int32, (tok, 128), 1)
    want = jnp.where(lane < N_EXPERT * LOCAL, expert_of(me, lane & 7, lane >> 3), -1)
    hits = [(ids_ref[:, k : k + 1] == want) for k in range(2)]
    both = jnp.where(hits[0] | hits[1], 1.0, 0.0).astype(BF16)
    earlier = lax.broadcasted_iota(jnp.int32, (tok, tok), 1) < lax.broadcasted_iota(
        jnp.int32, (tok, tok), 0
    )
    before = dot(jnp.where(earlier, 1.0, 0.0).astype(BF16), both)
    code = before + (lane * CAP).astype(F32)
    slots = lax.broadcasted_iota(jnp.int32, (tok, len(rows) * CAP), 1)
    picks = []
    for k in range(2):
        slot = jnp.sum(jnp.where(hits[k], code, 0.0), axis=1, keepdims=True).astype(jnp.int32)
        picks.append(jnp.where(slots == slot, 1.0, 0.0).astype(BF16))
    mixed = gates_ref[:, 0:1] * dot(picks[0], out_s[...])
    mixed = mixed + gates_ref[:, 1:2] * dot(picks[1], out_s[...])
    mixed_ref[...] = mixed.astype(BF16)
    grad_ref[...] = dot(picks[0] + picks[1], in_s[...]).astype(BF16)


def combine(me, ids, gates, rows):
    vmem = pl.BlockSpec(memory_space=pltpu.VMEM)
    tok = ids.shape[0]
    return pl.pallas_call(
        combine_kernel,
        in_specs=[pl.BlockSpec(memory_space=pltpu.SMEM)] + [vmem] * (2 + len(rows)),
        out_specs=[vmem] * 2,
        out_shape=[jax.ShapeDtypeStruct((tok, D), BF16)] * 2,
        scratch_shapes=[pltpu.VMEM((len(rows) * CAP, D), BF16)] * 2,
        compiler_params=pltpu.CompilerParams(vmem_limit_bytes=VMEM_LIMIT),
        cost_estimate=pl.CostEstimate(flops=10**9, bytes_accessed=4 * 10**6, transcendentals=0),
        name="combine",
    )(me, ids, gates, *rows)


def finish_kernel(*refs):
    ins, outs = refs[: 2 * LOCAL], refs[2 * LOCAL :]
    for j in range(LOCAL):
        total = (ins[2 * j][...].astype(F32) + ins[2 * j + 1][...].astype(F32)).astype(BF16)
        outs[0][j] = total[0:D]
        outs[1][j] = total[D : 2 * D]
        outs[2][j] = total[2 * D :].T


def finish(parts):
    vmem = pl.BlockSpec(memory_space=pltpu.VMEM)
    shapes = [(LOCAL, D, BLK), (LOCAL, D, BLK), (LOCAL, BLK, D)]
    return pl.pallas_call(
        finish_kernel,
        in_specs=[vmem] * len(parts),
        out_specs=[vmem] * 3,
        out_shape=[jax.ShapeDtypeStruct(s, BF16) for s in shapes],
        compiler_params=pltpu.CompilerParams(vmem_limit_bytes=VMEM_LIMIT),
        cost_estimate=pl.CostEstimate(flops=10**6, bytes_accessed=4 * 10**6, transcendentals=0),
        name="finish",
    )(*parts)


def add(*terms):
    return functools.reduce(lambda a, b: a + b, [t.astype(F32) for t in terms]).astype(BF16)


def local(tokens, expert_ids, gates, cotangent, w_gate, w_up, w_down):
    me = lax.axis_index("expert").astype(jnp.int32).reshape(1)
    rep = lax.axis_index("replica").astype(jnp.int32)
    y, x, core = rep >> 2, (rep >> 1) & 1, rep & 1
    tbl = jnp.stack(
        [((y + d) & 3) * 4 + (x ^ flip) * 2 + core for d in STEPS for flip in range(2)]
    )
    ids_t, gates_t = expert_ids.T, gates.T
    send = functools.partial(lax.ppermute, axis_name="replica")

    received = []
    for j in range(LOCAL):
        sent = dispatch(j, me, ids_t, gates_t, tokens, cotangent)
        got = [sent[0]] + [
            lax.ppermute(sent[r], "expert", over_expert(r, False)) for r in range(1, N_EXPERT)
        ]
        received.append(jnp.stack(got))

    rows, parts = [], []
    for j in range(LOCAL):
        own = received[j]
        oth = send(own, perm=CORE)
        s2a, s2b, s1a, s1b, s3a, s3b, s0a, s0b, ret_own, ret_oth = expert(
            j, tbl, own, oth, w_gate, w_up, w_down
        )
        r1a, r1b = send(s2a, perm=UP), send(s2b, perm=DOWN)
        from_down_b = send(s1b, perm=UP)
        from_up_a = send(s3a, perm=DOWN)
        from_down_a = send(add(s1a, r1a), perm=UP)
        from_up_b = send(add(s3b, r1b), perm=DOWN)
        across = send(add(s0b, from_down_b, from_up_b), perm=ACROSS)
        parts += [add(s0a, from_down_a, from_up_a), across]
        sums = back(j, ret_own, send(ret_oth, perm=CORE))
        rows += [sums[0]] + [
            lax.ppermute(sums[r], "expert", over_expert(r, True)) for r in range(1, N_EXPERT)
        ]
    mixed, token_grad = combine(me, expert_ids, gates, rows)
    gate_grad, up_grad, down_grad = finish(parts)
    return mixed, token_grad, gate_grad, up_grad, down_grad


def solution(mesh):
    tokens = P(("expert", "replica"), None)
    return jax.shard_map(
        local,
        mesh=mesh,
        in_specs=(tokens,) * 4 + (P("expert", None, None),) * 3,
        out_specs=(tokens,) * 2
        + (P("expert", None, "replica"), P("expert", None, "replica"), P("expert", "replica", None)),
        check_vma=False,
    )
```

```python
import functools

import jax
import jax.numpy as jnp
from jax import lax
from jax.experimental import pallas as pl
from jax.experimental.pallas import tpu as pltpu
from jax.sharding import PartitionSpec as P

CAP = 48
LOCAL = 3
SOURCES = 8
ROWS = SOURCES * CAP
D = 512
TOK = 256
BLK = 128
META = 16
F32 = jnp.float32
BF16 = jnp.bfloat16
VMEM_LIMIT = 48 * 1024 * 1024
VMEM = pl.BlockSpec(memory_space=pltpu.VMEM)
SMEM = pl.BlockSpec(memory_space=pltpu.SMEM)


def dot(a, b, ca=1, cb=0):
    return lax.dot_general(a, b, (((ca,), (cb,)), ((), ())), preferred_element_type=F32)


def bf16_like(*shape):
    return jax.ShapeDtypeStruct(shape, BF16)


def call(kernel, name, in_specs, out_shape, args, nbytes=10**6, scratch=()):
    return pl.pallas_call(
        kernel,
        in_specs=in_specs,
        out_specs=jax.tree.map(lambda _: VMEM, out_shape),
        out_shape=out_shape,
        scratch_shapes=list(scratch),
        compiler_params=pltpu.CompilerParams(vmem_limit_bytes=VMEM_LIMIT),
        cost_estimate=pl.CostEstimate(flops=0, bytes_accessed=nbytes, transcendentals=0),
        name=name,
    )(*args)


def along_z(dz):
    return [(z * 2 + h, ((z + dz) % 4) * 2 + h) for z in range(4) for h in range(2)]


PARTNER = [(e, e ^ 1) for e in range(8)]
CORE = [(r, r ^ 1) for r in range(16)]
ACROSS = [(r, r ^ 2) for r in range(16)]
RING = [(r, (r + (4 if r % 2 == 0 else 12)) % 16) for r in range(16)]


def pack_kernel(tokens_ref, cot_ref, ids_ref, gates_ref, out_ref):
    out_ref[0:TOK] = tokens_ref[...]
    out_ref[TOK : 2 * TOK] = cot_ref[...]
    gates = gates_ref[...]
    high = gates.astype(BF16).astype(F32)
    middle = (gates - high).astype(BF16).astype(F32)
    low = gates - high - middle
    meta = jnp.concatenate(
        [ids_ref[...].astype(F32), high, middle, low, jnp.zeros((META - 8, TOK), F32)], axis=0
    )
    out_ref[2 * TOK :] = jnp.concatenate([meta, jnp.zeros_like(meta)], axis=1).astype(BF16)


def read_meta(packed_ref):
    meta = packed_ref[2 * TOK :, 0:TOK].astype(F32)
    gates = meta[2:4] + meta[4:6] + meta[6:8]
    return meta[0:2], gates


def dispatch_kernel(me_ref, packed_ref, *out_refs):
    z, h = me_ref[0] >> 1, me_ref[0] & 1
    ids, gates = read_meta(packed_ref)
    count = 4 * LOCAL
    index = lax.broadcasted_iota(jnp.int32, (16, TOK), 0)
    want = (((z + (index & 3)) & 3) * 2 + h) * LOCAL + (index >> 2)
    want = jnp.where(index < count, want, -1).astype(F32)
    hit0 = ids[0:1] == want
    hit1 = ids[1:2] == want
    hit = jnp.where(hit0 | hit1, 1.0, 0.0).astype(F32)
    gate = jnp.where(hit0, gates[0:1], jnp.where(hit1, gates[1:2], 0.0))
    earlier = lax.broadcasted_iota(jnp.int32, (TOK, TOK), 0) < lax.broadcasted_iota(
        jnp.int32, (TOK, TOK), 1
    )
    before = dot(hit.astype(BF16), jnp.where(earlier, 1.0, 0.0).astype(BF16))
    place = jnp.where(hit > 0.0, before, -1.0).astype(jnp.int32)
    slot = lax.broadcasted_iota(jnp.int32, (CAP, TOK), 0)
    for j in range(LOCAL):
        picks, weights = [], []
        for n in range(j * 4, j * 4 + 4):
            sel = slot == place[n : n + 1]
            picks.append(jnp.where(sel, 1.0, 0.0).astype(BF16))
            weights.append(jnp.sum(jnp.where(sel, gate[n : n + 1], 0.0), axis=1, keepdims=True))
        pick = jnp.concatenate(picks, axis=0)
        weight = jnp.concatenate(weights, axis=0)
        rows = dot(pick, packed_ref[0:TOK]).astype(BF16)
        grads = (weight * dot(pick, packed_ref[TOK : 2 * TOK])).astype(BF16)
        for dz in range(4):
            part = slice(dz * CAP, (dz + 1) * CAP)
            if j == 0:
                out_refs[dz][0] = rows[part]
                out_refs[dz][1] = grads[part]
            else:
                out_refs[4 + dz][j - 1, 0] = rows[part]
                out_refs[4 + dz][j - 1, 1] = grads[part]


def dispatch(name, me, packed):
    out = [bf16_like(2, CAP, D)] * 4 + [bf16_like(2, 2, CAP, D)] * 4
    return call(dispatch_kernel, name, [SMEM, VMEM], out, (me, packed), 3 * 10**6)


def join_first_kernel(*refs):
    for n, ref in enumerate(refs[:-1]):
        refs[-1][n] = ref[...]


def join_rest_kernel(*refs):
    for n, ref in enumerate(refs[:-2]):
        refs[-2][n] = ref[0]
        refs[-1][n] = ref[1]


def expert_kernel(
    tbl_ref, own_ref, oth_ref, after_ref, wg0, wg1, wu0, wu1, wd0, wd1,
    far, mid, near, home0, home1, ret_own, ret_oth,
    x_s, g_s, xt_s, gt_s, eo_s, ig_s,
):
    i = pl.program_id(0)

    @pl.when(i == 0)
    def _():
        for k, ref in enumerate((own_ref, oth_ref)):
            x_s[k * ROWS : (k + 1) * ROWS, :] = ref[:, 0].reshape(ROWS, D)
            g_s[k * ROWS : (k + 1) * ROWS, :] = ref[:, 1].reshape(ROWS, D)
        xt_s[...] = x_s[...].T
        gt_s[...] = g_s[...].T
        eo_s[...] = jnp.zeros_like(eo_s)
        ig_s[...] = jnp.zeros_like(ig_s)

    wg = jnp.concatenate([wg0[...], wg1[...]], axis=1)
    wu = jnp.concatenate([wu0[...], wu1[...]], axis=1)
    wd = jnp.concatenate([wd0[...], wd1[...]], axis=0)
    x = x_s[...]
    g = g_s[...]
    pre_gate = dot(x, wg)
    pre_up = dot(x, wu)
    grad_hidden = dot(g, wd, 1, 1)
    sig = jax.nn.sigmoid(pre_gate)
    silu = pre_gate * sig
    hidden = (silu * pre_up).astype(BF16)
    grad_gate = (grad_hidden * pre_up * sig * (1.0 + pre_gate * (1.0 - sig))).astype(BF16)
    grad_up = (grad_hidden * silu).astype(BF16)
    part_gate = dot(xt_s[...], grad_gate).astype(BF16)
    part_up = dot(xt_s[...], grad_up).astype(BF16)
    part_down = dot(gt_s[...], hidden).astype(BF16)

    def keep(ref, lane):
        for k, part in enumerate((part_gate, part_up, part_down)):
            ref[k * D : (k + 1) * D, :] = part[:, lane * BLK : (lane + 1) * BLK]

    homes = (far.at[0], far.at[1]), (mid.at[0], mid.at[1]), (near.at[0], near.at[1]), (home0, home1)
    for step, (a, b) in enumerate(homes):

        @pl.when(i == step)
        def _(a=a, b=b):
            keep(a, 0)
            keep(b, 1)

    eo_s[...] += dot(hidden, wd)
    ig_s[...] += dot(grad_gate, wg, 1, 1) + dot(grad_up, wu, 1, 1)

    @pl.when(i == 3)
    def _():
        for k, ref in enumerate((ret_own, ret_oth)):
            ref[0] = eo_s[k * ROWS : (k + 1) * ROWS, :].astype(BF16)
            ref[1] = ig_s[k * ROWS : (k + 1) * ROWS, :].astype(BF16)


def expert(j, tbl, own, oth, after, w_gate, w_up, w_down):
    rows = 2 * ROWS

    def fixed(shape):
        return pl.BlockSpec(shape, lambda i, tbl: (0,) * len(shape))

    def columns(k):
        return pl.BlockSpec((None, D, BLK), lambda i, tbl: (j, 0, tbl[2 * i + k]))

    def lines(k):
        return pl.BlockSpec((None, BLK, D), lambda i, tbl: (j, tbl[2 * i + k], 0))

    chunk, ret = (3 * D, BLK), (2, ROWS, D)
    out_shapes = [(2,) + chunk] * 3 + [chunk] * 2 + [ret] * 2
    return pl.pallas_call(
        expert_kernel,
        grid_spec=pltpu.PrefetchScalarGridSpec(
            num_scalar_prefetch=1,
            grid=(4,),
            in_specs=[fixed(own.shape), fixed(oth.shape), pl.BlockSpec(memory_space=pl.ANY)]
            + [columns(0), columns(1), columns(0), columns(1), lines(0), lines(1)],
            out_specs=[fixed(s) for s in out_shapes],
            scratch_shapes=[
                pltpu.VMEM((rows, D), BF16),
                pltpu.VMEM((rows, D), BF16),
                pltpu.VMEM((D, rows), BF16),
                pltpu.VMEM((D, rows), BF16),
                pltpu.VMEM((rows, D), F32),
                pltpu.VMEM((rows, D), F32),
            ],
        ),
        out_shape=[bf16_like(*s) for s in out_shapes],
        compiler_params=pltpu.CompilerParams(
            dimension_semantics=("arbitrary",), vmem_limit_bytes=VMEM_LIMIT
        ),
        cost_estimate=pl.CostEstimate(flops=0, bytes_accessed=2 * 10**6, transcendentals=0),
        name=f"expert{j}",
    )(tbl, own, oth, after, w_gate, w_gate, w_up, w_up, w_down, w_down)


def back_kernel(count, *refs):
    ins, outs = refs[: 2 * count], refs[2 * count :]
    for j in range(count):
        own_ref, oth_ref = ins[2 * j : 2 * j + 2]
        for n in range(SOURCES):
            for k in range(2):
                rows = slice(n * CAP, (n + 1) * CAP)
                total = own_ref[k, rows].astype(F32) + oth_ref[k, rows].astype(F32)
                outs[n & 3][j, n >> 2, k] = total.astype(BF16)


def back(name, pairs):
    count = len(pairs) // 2
    out = [bf16_like(count, 2, 2, CAP, D)] * 4
    return call(
        functools.partial(back_kernel, count), name, [VMEM] * len(pairs), out, pairs, 3 * 10**6
    )


def token_sums(side, me_ref, packed_ref, rows, out_s, in_s):
    z, h = me_ref[0] >> 1, me_ref[0] & 1
    for dz in range(4):
        first, last = rows[dz], rows[4 + dz]
        for j in range(LOCAL):
            ref, at = (first, j) if j < LOCAL - 1 else (last, 0)
            n = j * 4 + dz
            out_s[n * CAP : (n + 1) * CAP, :] = ref[at, side, 0]
            in_s[n * CAP : (n + 1) * CAP, :] = ref[at, side, 1]
    ids, gates = read_meta(packed_ref)
    columns = jnp.concatenate([ids, gates, jnp.zeros((4, TOK), F32)], axis=0).T
    lane = lax.broadcasted_iota(jnp.int32, (TOK, 128), 1)
    want = (((z + (lane & 3)) & 3) * 2 + h) * LOCAL + (lane >> 2)
    want = jnp.where(lane < 4 * LOCAL, want, -1).astype(F32)
    hits = [columns[:, k : k + 1] == want for k in range(2)]
    either = jnp.where(hits[0] | hits[1], 1.0, 0.0).astype(BF16)
    earlier = lax.broadcasted_iota(jnp.int32, (TOK, TOK), 1) < lax.broadcasted_iota(
        jnp.int32, (TOK, TOK), 0
    )
    before = dot(jnp.where(earlier, 1.0, 0.0).astype(BF16), either)
    code = before + (lane * CAP + 1).astype(F32)
    slots = lax.broadcasted_iota(jnp.int32, (TOK, 4 * LOCAL * CAP), 1)
    picks = []
    for k in range(2):
        slot = jnp.sum(jnp.where(hits[k], code, 0.0), axis=1, keepdims=True).astype(jnp.int32) - 1
        picks.append(jnp.where(slots == slot, 1.0, 0.0).astype(BF16))
    mixed = columns[:, 2:3] * dot(picks[0], out_s[...]) + columns[:, 3:4] * dot(picks[1], out_s[...])
    return mixed, dot(picks[0] + picks[1], in_s[...])


def partner_kernel(me_ref, packed_ref, *refs):
    rows, (out_ref, out_s, in_s) = refs[:-3], refs[-3:]
    mixed, grad = token_sums(1, me_ref, packed_ref, rows, out_s, in_s)
    out_ref[0] = mixed.astype(BF16)
    out_ref[1] = grad.astype(BF16)


def combine_kernel(me_ref, packed_ref, other_ref, *refs):
    rows, (mixed_ref, grad_ref, out_s, in_s) = refs[:-4], refs[-4:]
    mixed, grad = token_sums(0, me_ref, packed_ref, rows, out_s, in_s)
    mixed_ref[...] = (mixed + other_ref[0].astype(F32)).astype(BF16)
    grad_ref[...] = (grad + other_ref[1].astype(F32)).astype(BF16)


def finish_kernel(*refs):
    ins, outs = refs[: 2 * LOCAL], refs[2 * LOCAL :]
    for j in range(LOCAL):
        total = (ins[2 * j][...].astype(F32) + ins[2 * j + 1][...].astype(F32)).astype(BF16)
        outs[0][j] = total[0:D]
        outs[1][j] = total[D : 2 * D]
        outs[2][j] = total[2 * D :].T


def add(*terms):
    return functools.reduce(lambda a, b: a + b, [t.astype(F32) for t in terms]).astype(BF16)


def local(tokens, expert_ids, gates, cotangent, w_gate, w_up, w_down):
    me = lax.axis_index("expert").astype(jnp.int32).reshape(1)
    rep = lax.axis_index("replica").astype(jnp.int32)
    y, x, core = rep >> 2, (rep >> 1) & 1, rep & 1
    step = jnp.arange(8, dtype=jnp.int32)
    away = (3 - (step >> 1)) * (1 - 2 * core)
    tbl = ((y + away) & 3) * 4 + (x ^ (step & 1)) * 2 + core

    def over_replica(value, perm):
        return lax.ppermute(value, "replica", perm)

    def to_z(value, dz):
        return lax.ppermute(value, "expert", along_z(dz))

    packed = call(
        pack_kernel,
        "pack",
        [VMEM] * 4,
        bf16_like(2 * TOK + META, D),
        (tokens, cotangent, expert_ids.T, gates.T),
    )
    partner = lax.ppermute(packed, "expert", PARTNER)
    firsts, rests = [], []
    for name, source in (("own_slots", packed), ("partner_slots", partner)):
        sent = dispatch(name, me, source)
        firsts += [sent[0]] + [to_z(sent[dz], dz) for dz in range(1, 4)]
        rests += [sent[4]] + [to_z(sent[4 + dz], dz) for dz in range(1, 4)]
    joined = bf16_like(SOURCES, 2, CAP, D)
    received = [call(join_first_kernel, "join0", [VMEM] * 8, joined, firsts)]
    received += call(join_rest_kernel, "join12", [VMEM] * 8, [joined] * 2, rests)

    parts, pairs = [], []
    after = me
    for j in range(LOCAL):
        own = received[j]
        oth = over_replica(own, CORE)
        far, mid, near, home0, home1, ret_own, ret_oth = expert(
            j, tbl, own, oth, after, w_gate, w_up, w_down
        )
        after = home0
        total = over_replica(far, RING)
        total = over_replica(add(mid, total), RING)
        total = over_replica(add(near, total), RING)
        across = over_replica(add(home1, total[1]), ACROSS)
        parts += [add(home0, total[0]), across]
        pairs += [ret_own, over_replica(ret_oth, CORE)]

    rows = []
    for name, some in (("back01", pairs[:4]), ("back2", pairs[4:])):
        sums = back(name, some)
        rows += [sums[0]] + [to_z(sums[dz], 4 - dz) for dz in range(1, 4)]
    scratch = [pltpu.VMEM((4 * LOCAL * CAP, D), BF16)] * 2
    theirs = call(
        partner_kernel, "partner_sums", [SMEM] + [VMEM] * 9, bf16_like(2, TOK, D),
        (me, partner, *rows), 3 * 10**6, scratch,
    )
    mixed, token_grad = call(
        combine_kernel, "combine", [SMEM] + [VMEM] * 10, [bf16_like(TOK, D)] * 2,
        (me, packed, lax.ppermute(theirs, "expert", PARTNER), *rows), 3 * 10**6, scratch,
    )
    gate_grad, up_grad, down_grad = call(
        finish_kernel, "finish", [VMEM] * len(parts),
        [bf16_like(LOCAL, D, BLK), bf16_like(LOCAL, D, BLK), bf16_like(LOCAL, BLK, D)],
        parts, 4 * 10**6,
    )
    return mixed, token_grad, gate_grad, up_grad, down_grad


def solution(mesh):
    tokens = P(("expert", "replica"), None)
    return jax.shard_map(
        local,
        mesh=mesh,
        in_specs=(tokens,) * 4 + (P("expert", None, None),) * 3,
        out_specs=(tokens,) * 2
        + (P("expert", None, "replica"), P("expert", None, "replica"), P("expert", "replica", None)),
        check_vma=False,
    )
```

```python
import functools

import jax
import jax.numpy as jnp
from jax import lax
from jax.experimental import pallas as pl
from jax.experimental.pallas import tpu as pltpu
from jax.sharding import PartitionSpec as P

CAP = 48
LOCAL = 3
SOURCES = 8
ROWS = SOURCES * CAP
D = 512
TOK = 256
BLK = 128
META = 16
F32 = jnp.float32
BF16 = jnp.bfloat16
VMEM_LIMIT = 34 * 1024 * 1024
VMEM = pl.BlockSpec(memory_space=pltpu.VMEM)
SMEM = pl.BlockSpec(memory_space=pltpu.SMEM)


def dot(a, b, ca=1, cb=0):
    return lax.dot_general(a, b, (((ca,), (cb,)), ((), ())), preferred_element_type=F32)


def bf16_like(*shape):
    return jax.ShapeDtypeStruct(shape, BF16)


def call(kernel, name, in_specs, out_shape, args, nbytes=10**6, scratch=()):
    return pl.pallas_call(
        kernel,
        in_specs=in_specs,
        out_specs=jax.tree.map(lambda _: VMEM, out_shape),
        out_shape=out_shape,
        scratch_shapes=list(scratch),
        compiler_params=pltpu.CompilerParams(vmem_limit_bytes=VMEM_LIMIT),
        cost_estimate=pl.CostEstimate(flops=0, bytes_accessed=nbytes, transcendentals=0),
        name=name,
    )(*args)


def along_z(dz):
    return [(z * 2 + h, ((z + dz) % 4) * 2 + h) for z in range(4) for h in range(2)]


PARTNER = [(e, e ^ 1) for e in range(8)]
CORE = [(r, r ^ 1) for r in range(16)]
ACROSS = [(r, r ^ 2) for r in range(16)]
RING = [(r, (r + (4 if r % 2 == 0 else 12)) % 16) for r in range(16)]


def pack_kernel(tokens_ref, cot_ref, ids_ref, gates_ref, out_ref, ids_s, gates_s, sems):
    copies = [
        pltpu.make_async_copy(src, dst, sems.at[n])
        for n, (src, dst) in enumerate(
            (
                (ids_ref, ids_s),
                (gates_ref, gates_s),
                (tokens_ref, out_ref.at[pl.ds(0, TOK)]),
                (cot_ref, out_ref.at[pl.ds(TOK, TOK)]),
            )
        )
    ]
    for copy in copies:
        copy.start()
    copies[0].wait()
    copies[1].wait()
    gates = gates_s[...]
    high = gates.astype(BF16).astype(F32)
    middle = (gates - high).astype(BF16).astype(F32)
    low = gates - high - middle
    meta = jnp.concatenate(
        [ids_s[...].astype(F32), high, middle, low, jnp.zeros((META - 8, TOK), F32)], axis=0
    )
    out_ref[2 * TOK :] = jnp.concatenate([meta, jnp.zeros_like(meta)], axis=1).astype(BF16)
    copies[2].wait()
    copies[3].wait()


def read_meta(packed_ref):
    meta = packed_ref[2 * TOK :, 0:TOK].astype(F32)
    gates = meta[2:4] + meta[4:6] + meta[6:8]
    return meta[0:2], gates


def dispatch_kernel(split, me_ref, packed_ref, *out_refs):
    z, h = me_ref[0] >> 1, me_ref[0] & 1
    ids, gates = read_meta(packed_ref)
    count = 4 * LOCAL
    index = lax.broadcasted_iota(jnp.int32, (16, TOK), 0)
    want = (((z + (index & 3)) & 3) * 2 + h) * LOCAL + (index >> 2)
    want = jnp.where(index < count, want, -1).astype(F32)
    hit0 = ids[0:1] == want
    hit1 = ids[1:2] == want
    hit = jnp.where(hit0 | hit1, 1.0, 0.0).astype(F32)
    gate = jnp.where(hit0, gates[0:1], jnp.where(hit1, gates[1:2], 0.0))
    earlier = lax.broadcasted_iota(jnp.int32, (TOK, TOK), 0) < lax.broadcasted_iota(
        jnp.int32, (TOK, TOK), 1
    )
    before = dot(hit.astype(BF16), jnp.where(earlier, 1.0, 0.0).astype(BF16))
    place = jnp.where(hit > 0.0, before, -1.0).astype(jnp.int32)
    slot = lax.broadcasted_iota(jnp.int32, (CAP, TOK), 0)
    for j in range(LOCAL):
        picks, weights = [], []
        for n in range(j * 4, j * 4 + 4):
            sel = slot == place[n : n + 1]
            picks.append(jnp.where(sel, 1.0, 0.0).astype(BF16))
            weights.append(jnp.sum(jnp.where(sel, gate[n : n + 1], 0.0), axis=1, keepdims=True))
        pick = jnp.concatenate(picks, axis=0)
        weight = jnp.concatenate(weights, axis=0)
        rows = dot(pick, packed_ref[0:TOK]).astype(BF16)
        grads = (weight * dot(pick, packed_ref[TOK : 2 * TOK])).astype(BF16)
        for dz in range(4):
            part = slice(dz * CAP, (dz + 1) * CAP)
            ref, at = out_refs[dz], j
            if split:
                ref, at = (out_refs[dz], 0) if j == 0 else (out_refs[4 + dz], j - 1)
            ref[at, 0] = rows[part]
            ref[at, 1] = grads[part]


def dispatch(name, split, me, packed):
    out = [bf16_like(n, 2, CAP, D) for n in ((1, 2) if split else (3,)) for _ in range(4)]
    kernel = functools.partial(dispatch_kernel, split)
    return call(kernel, name, [SMEM, VMEM], out, (me, packed), 3 * 10**6)


def join_kernel(count, *refs):
    ins, out_ref = refs[:SOURCES], refs[-1]
    for n, ref in enumerate(ins):
        skip = ref.shape[0] - count
        for j in range(count):
            out_ref[j, n] = ref[skip + j if count > 1 else 0]


def join(name, count, pieces, after):
    specs = [VMEM] * SOURCES + [pl.BlockSpec(memory_space=pl.ANY)] * len(after)
    out = bf16_like(count, SOURCES, 2, CAP, D)
    return call(functools.partial(join_kernel, count), name, specs, out, (*pieces, *after), 10**6)


def share(x_s, g_s, xt_s, gt_s, eo_s, ig_s, weights, homes):
    wg = jnp.concatenate([weights[0][...], weights[1][...]], axis=1)
    wu = jnp.concatenate([weights[2][...], weights[3][...]], axis=1)
    wd = jnp.concatenate([weights[4][...], weights[5][...]], axis=0)
    x = x_s[...]
    g = g_s[...]
    pre_gate = dot(x, wg)
    pre_up = dot(x, wu)
    grad_hidden = dot(g, wd, 1, 1)
    sig = jax.nn.sigmoid(pre_gate)
    silu = pre_gate * sig
    hidden = (silu * pre_up).astype(BF16)
    grad_gate = (grad_hidden * pre_up * sig * (1.0 + pre_gate * (1.0 - sig))).astype(BF16)
    grad_up = (grad_hidden * silu).astype(BF16)
    parts = [
        dot(xt_s[...], grad_gate).astype(BF16),
        dot(xt_s[...], grad_up).astype(BF16),
        dot(gt_s[...], hidden).astype(BF16),
    ]
    i = pl.program_id(0)
    for step, pair in enumerate(homes):

        @pl.when(i == step)
        def _(pair=pair):
            for lane, ref in enumerate(pair):
                for k, part in enumerate(parts):
                    ref[k * D : (k + 1) * D, :] = part[:, lane * BLK : (lane + 1) * BLK]

    eo_s[...] += dot(hidden, wd)
    ig_s[...] += dot(grad_gate, wg, 1, 1) + dot(grad_up, wu, 1, 1)


def load_rows(own_ref, oth_ref, x_s, g_s, xt_s, gt_s):
    for k, ref in enumerate((own_ref, oth_ref)):
        x_s[k * ROWS : (k + 1) * ROWS, :] = ref[:, 0].reshape(ROWS, D)
        g_s[k * ROWS : (k + 1) * ROWS, :] = ref[:, 1].reshape(ROWS, D)
    xt_s[...] = x_s[...].T
    gt_s[...] = g_s[...].T


def first_kernel(n_after, tbl_ref, own_ref, oth_ref, *refs):
    weights, (far, eo_ref, ig_ref, x_s, g_s, xt_s, gt_s) = refs[:6], refs[6 + n_after :]
    load_rows(own_ref, oth_ref, x_s, g_s, xt_s, gt_s)
    eo_ref[...] = jnp.zeros_like(eo_ref)
    ig_ref[...] = jnp.zeros_like(ig_ref)
    share(x_s, g_s, xt_s, gt_s, eo_ref, ig_ref, weights, [(far.at[0], far.at[1])])


def rest_kernel(n_after, tbl_ref, own_ref, oth_ref, *refs):
    weights, eo_ref, ig_ref = refs[:6], refs[6], refs[7]
    mid, near, home0, home1, ret_own, ret_oth, x_s, g_s, xt_s, gt_s, eo_s, ig_s = refs[8 + n_after :]
    i = pl.program_id(0)

    @pl.when(i == 0)
    def _():
        load_rows(own_ref, oth_ref, x_s, g_s, xt_s, gt_s)
        eo_s[...] = eo_ref[...]
        ig_s[...] = ig_ref[...]

    homes = [(mid.at[0], mid.at[1]), (near.at[0], near.at[1]), (home0, home1)]
    share(x_s, g_s, xt_s, gt_s, eo_s, ig_s, weights, homes)

    @pl.when(i == 2)
    def _():
        for k, ref in enumerate((ret_own, ret_oth)):
            ref[0] = eo_s[k * ROWS : (k + 1) * ROWS, :].astype(BF16)
            ref[1] = ig_s[k * ROWS : (k + 1) * ROWS, :].astype(BF16)


def expert(j, at, tbl, own, oth, weights, sums=None, after=()):
    rows = 2 * ROWS
    steps = (0,) if sums is None else (1, 2, 3)

    def fixed(shape):
        return pl.BlockSpec(shape, lambda i, tbl: (0,) * len(shape))

    def columns(k):
        return pl.BlockSpec((None, D, BLK), lambda i, tbl: (j, 0, tbl[2 * (i + steps[0]) + k]))

    def lines(k):
        return pl.BlockSpec((None, BLK, D), lambda i, tbl: (j, tbl[2 * (i + steps[0]) + k], 0))

    joined = pl.BlockSpec((None, SOURCES, 2, CAP, D), lambda i, tbl: (at, 0, 0, 0, 0))
    chunk, ret, sum_like = (3 * D, BLK), (2, ROWS, D), jax.ShapeDtypeStruct((rows, D), F32)
    scratch = [pltpu.VMEM((rows, D), BF16)] * 2 + [pltpu.VMEM((D, rows), BF16)] * 2
    if sums is None:
        kernel, name, sums = first_kernel, f"expert{j}_first", ()
        out = [bf16_like(2, *chunk), sum_like, sum_like]
    else:
        kernel, name = rest_kernel, f"expert{j}_rest"
        out = [bf16_like(*s) for s in ((2,) + chunk, (2,) + chunk, chunk, chunk, ret, ret)]
        scratch = scratch + [pltpu.VMEM((rows, D), F32)] * 2
    w_gate, w_up, w_down = weights
    return pl.pallas_call(
        functools.partial(kernel, len(after)),
        grid_spec=pltpu.PrefetchScalarGridSpec(
            num_scalar_prefetch=1,
            grid=(len(steps),),
            in_specs=[joined, joined]
            + [columns(0), columns(1), columns(0), columns(1), lines(0), lines(1)]
            + [fixed((rows, D))] * len(sums)
            + [pl.BlockSpec(memory_space=pl.ANY)] * len(after),
            out_specs=[fixed(s.shape) for s in out],
            scratch_shapes=scratch,
        ),
        out_shape=out,
        compiler_params=pltpu.CompilerParams(
            dimension_semantics=("arbitrary",), vmem_limit_bytes=VMEM_LIMIT
        ),
        cost_estimate=pl.CostEstimate(
            flops=len(steps) * 18 * rows * D * 256, bytes_accessed=10**6, transcendentals=0
        ),
        name=name,
    )(tbl, own, oth, w_gate, w_gate, w_up, w_up, w_down, w_down, *sums, *after)


def back_kernel(count, *refs):
    ins, outs = refs[: 2 * count], refs[2 * count :]
    for j in range(count):
        own_ref, oth_ref = ins[2 * j : 2 * j + 2]
        for n in range(SOURCES):
            for k in range(2):
                rows = slice(n * CAP, (n + 1) * CAP)
                total = own_ref[k, rows].astype(F32) + oth_ref[k, rows].astype(F32)
                outs[n & 3][j, n >> 2, k] = total.astype(BF16)


def back(name, pairs):
    count = len(pairs) // 2
    out = [bf16_like(count, 2, 2, CAP, D)] * 4
    return call(
        functools.partial(back_kernel, count), name, [VMEM] * len(pairs), out, pairs, 3 * 10**6
    )


def token_sums(side, me_ref, packed_ref, rows, out_s, in_s):
    z, h = me_ref[0] >> 1, me_ref[0] & 1
    for dz in range(4):
        first, last = rows[dz], rows[4 + dz]
        for j in range(LOCAL):
            ref, at = (first, j) if j < LOCAL - 1 else (last, 0)
            n = j * 4 + dz
            out_s[n * CAP : (n + 1) * CAP, :] = ref[at, side, 0]
            in_s[n * CAP : (n + 1) * CAP, :] = ref[at, side, 1]
    ids, gates = read_meta(packed_ref)
    columns = jnp.concatenate([ids, gates, jnp.zeros((4, TOK), F32)], axis=0).T
    lane = lax.broadcasted_iota(jnp.int32, (TOK, 128), 1)
    want = (((z + (lane & 3)) & 3) * 2 + h) * LOCAL + (lane >> 2)
    want = jnp.where(lane < 4 * LOCAL, want, -1).astype(F32)
    hits = [columns[:, k : k + 1] == want for k in range(2)]
    either = jnp.where(hits[0] | hits[1], 1.0, 0.0).astype(BF16)
    earlier = lax.broadcasted_iota(jnp.int32, (TOK, TOK), 1) < lax.broadcasted_iota(
        jnp.int32, (TOK, TOK), 0
    )
    before = dot(jnp.where(earlier, 1.0, 0.0).astype(BF16), either)
    code = before + (lane * CAP + 1).astype(F32)
    slots = lax.broadcasted_iota(jnp.int32, (TOK, 4 * LOCAL * CAP), 1)
    picks = []
    for k in range(2):
        slot = jnp.sum(jnp.where(hits[k], code, 0.0), axis=1, keepdims=True).astype(jnp.int32) - 1
        picks.append(jnp.where(slots == slot, 1.0, 0.0).astype(BF16))
    mixed = columns[:, 2:3] * dot(picks[0], out_s[...]) + columns[:, 3:4] * dot(picks[1], out_s[...])
    return mixed, dot(picks[0] + picks[1], in_s[...])


def partner_kernel(me_ref, packed_ref, *refs):
    rows, (out_ref, out_s, in_s) = refs[:-3], refs[-3:]
    mixed, grad = token_sums(1, me_ref, packed_ref, rows, out_s, in_s)
    out_ref[0] = mixed.astype(BF16)
    out_ref[1] = grad.astype(BF16)


def combine_kernel(me_ref, packed_ref, other_ref, *refs):
    rows, (mixed_ref, grad_ref, out_s, in_s) = refs[:-4], refs[-4:]
    mixed, grad = token_sums(0, me_ref, packed_ref, rows, out_s, in_s)
    mixed_ref[...] = (mixed + other_ref[0].astype(F32)).astype(BF16)
    grad_ref[...] = (grad + other_ref[1].astype(F32)).astype(BF16)


def finish_kernel(*refs):
    ins, outs = refs[: 2 * LOCAL], refs[2 * LOCAL :]
    for j in range(LOCAL):
        total = (ins[2 * j][...].astype(F32) + ins[2 * j + 1][...].astype(F32)).astype(BF16)
        outs[0][j] = total[0:D]
        outs[1][j] = total[D : 2 * D]
        outs[2][j] = total[2 * D :].T


def add(*terms):
    return functools.reduce(lambda a, b: a + b, [t.astype(F32) for t in terms]).astype(BF16)


def local(tokens, expert_ids, gates, cotangent, w_gate, w_up, w_down):
    me = lax.axis_index("expert").astype(jnp.int32).reshape(1)
    rep = lax.axis_index("replica").astype(jnp.int32)
    y, x, core = rep >> 2, (rep >> 1) & 1, rep & 1
    step = jnp.arange(8, dtype=jnp.int32)
    away = (3 - (step >> 1)) * (1 - 2 * core)
    tbl = ((y + away) & 3) * 4 + (x ^ (step & 1)) * 2 + core

    def over_replica(value, perm):
        return lax.ppermute(value, "replica", perm)

    def to_z(value, dz):
        return lax.ppermute(value, "expert", along_z(dz))

    packed = call(
        pack_kernel,
        "pack",
        [pl.BlockSpec(memory_space=pltpu.HBM)] * 4,
        bf16_like(2 * TOK + META, D),
        (tokens, cotangent, expert_ids.T, gates.T),
        scratch=[
            pltpu.VMEM((2, TOK), jnp.int32),
            pltpu.VMEM((2, TOK), F32),
            pltpu.SemaphoreType.DMA((4,)),
        ],
    )
    partner = lax.ppermute(packed, "expert", PARTNER)
    sent = dispatch("own_slots", False, me, packed)
    from_own = [sent[0]] + [to_z(sent[dz], dz) for dz in range(1, 4)]
    sent = dispatch("partner_slots", True, me, partner)
    firsts = [sent[0]] + [to_z(sent[dz], dz) for dz in range(1, 4)]
    rests = [sent[4]] + [to_z(sent[4 + dz], dz) for dz in range(1, 4)]

    weights = (w_gate, w_up, w_down)
    own0 = join("join0", 1, from_own + firsts, ())
    oth0 = over_replica(own0, CORE)
    far0, eo, ig = expert(0, 0, tbl, own0, oth0, weights)
    own12 = join("join12", 2, from_own + rests, (far0,))
    oth12 = over_replica(own12, CORE)
    second0 = over_replica(far0, RING)
    mid0, near0, *kept0 = expert(0, 0, tbl, own0, oth0, weights, (eo, ig), (own12,))
    second0 = add(mid0, second0)
    third0 = over_replica(second0, RING)
    far1, eo, ig = expert(1, 0, tbl, own12, oth12, weights, None, (second0,))
    second1 = over_replica(far1, RING)
    mid1, near1, *kept1 = expert(1, 0, tbl, own12, oth12, weights, (eo, ig))
    third0 = add(near0, third0)
    home0 = over_replica(third0, RING)
    second1 = add(mid1, second1)
    third1 = over_replica(second1, RING)
    far2, eo, ig = expert(2, 1, tbl, own12, oth12, weights, None, (third0, second1))
    second2 = over_replica(far2, RING)
    mid2, near2, *kept2 = expert(2, 1, tbl, own12, oth12, weights, (eo, ig))
    second2 = add(mid2, second2)
    third2 = over_replica(second2, RING)
    home1 = over_replica(add(near1, third1), RING)
    home2 = over_replica(add(near2, third2), RING)

    parts, pairs = [], []
    for home, (mine, theirs, ret_own, ret_oth) in ((home0, kept0), (home1, kept1), (home2, kept2)):
        across = over_replica(add(theirs, home[1]), ACROSS)
        parts += [add(mine, home[0]), across]
        pairs += [ret_own, over_replica(ret_oth, CORE)]

    rows = []
    for name, some in (("back01", pairs[:4]), ("back2", pairs[4:])):
        sums = back(name, some)
        rows += [sums[0]] + [to_z(sums[dz], 4 - dz) for dz in range(1, 4)]
    scratch = [pltpu.VMEM((4 * LOCAL * CAP, D), BF16)] * 2
    theirs = call(
        partner_kernel, "partner_sums", [SMEM] + [VMEM] * 9, bf16_like(2, TOK, D),
        (me, partner, *rows), 3 * 10**6, scratch,
    )
    mixed, token_grad = call(
        combine_kernel, "combine", [SMEM] + [VMEM] * 10, [bf16_like(TOK, D)] * 2,
        (me, packed, lax.ppermute(theirs, "expert", PARTNER), *rows), 3 * 10**6, scratch,
    )
    gate_grad, up_grad, down_grad = call(
        finish_kernel, "finish", [VMEM] * len(parts),
        [bf16_like(LOCAL, D, BLK), bf16_like(LOCAL, D, BLK), bf16_like(LOCAL, BLK, D)],
        parts, 4 * 10**6,
    )
    return mixed, token_grad, gate_grad, up_grad, down_grad


def solution(mesh):
    tokens = P(("expert", "replica"), None)
    return jax.shard_map(
        local,
        mesh=mesh,
        in_specs=(tokens,) * 4 + (P("expert", None, None),) * 3,
        out_specs=(tokens,) * 2
        + (P("expert", None, "replica"), P("expert", None, "replica"), P("expert", "replica", None)),
        check_vma=False,
    )
```

```python
import functools

import jax
import jax.numpy as jnp
from jax import lax
from jax.experimental import pallas as pl
from jax.experimental.pallas import tpu as pltpu
from jax.sharding import PartitionSpec as P

CAP = 48
LOCAL = 3
SOURCES = 8
ROWS = SOURCES * CAP
D = 512
TOK = 256
BLK = 128
META = 16
F32 = jnp.float32
BF16 = jnp.bfloat16
VMEM_LIMIT = 32 * 1024 * 1024
EXPERT_LIMIT = 44 * 1024 * 1024
COST = {
    "expert0_first": 20,
    "expert0_rest": 20,
    "expert1": 20,
    "expert2_first": 20,
    "expert2_rest": 10,
}
VMEM = pl.BlockSpec(memory_space=pltpu.VMEM)
SMEM = pl.BlockSpec(memory_space=pltpu.SMEM)


def dot(a, b, ca=1, cb=0):
    return lax.dot_general(a, b, (((ca,), (cb,)), ((), ())), preferred_element_type=F32)


def bf16_like(*shape):
    return jax.ShapeDtypeStruct(shape, BF16)


def call(kernel, name, in_specs, out_shape, args, nbytes=10**6, scratch=(), limit=VMEM_LIMIT):
    return pl.pallas_call(
        kernel,
        in_specs=in_specs,
        out_specs=jax.tree.map(lambda _: VMEM, out_shape),
        out_shape=out_shape,
        scratch_shapes=list(scratch),
        compiler_params=pltpu.CompilerParams(vmem_limit_bytes=limit),
        cost_estimate=pl.CostEstimate(flops=0, bytes_accessed=nbytes, transcendentals=0),
        name=name,
    )(*args)


def along_z(dz):
    return [(z * 2 + h, ((z + dz) % 4) * 2 + h) for z in range(4) for h in range(2)]


PARTNER = [(e, e ^ 1) for e in range(8)]
CORE = [(r, r ^ 1) for r in range(16)]
ACROSS = [(r, r ^ 2) for r in range(16)]
RING = [(r, (r + (4 if r % 2 == 0 else 12)) % 16) for r in range(16)]


def pack_kernel(tokens_ref, cot_ref, ids_ref, gates_ref, out_ref, ids_s, gates_s, sems):
    copies = [
        pltpu.make_async_copy(src, dst, sems.at[n])
        for n, (src, dst) in enumerate(
            (
                (ids_ref, ids_s),
                (gates_ref, gates_s),
                (tokens_ref, out_ref.at[pl.ds(0, TOK)]),
                (cot_ref, out_ref.at[pl.ds(TOK, TOK)]),
            )
        )
    ]
    for copy in copies:
        copy.start()
    copies[0].wait()
    copies[1].wait()
    gates = gates_s[...]
    high = gates.astype(BF16).astype(F32)
    middle = (gates - high).astype(BF16).astype(F32)
    low = gates - high - middle
    meta = jnp.concatenate(
        [ids_s[...].astype(F32), high, middle, low, jnp.zeros((META - 8, TOK), F32)], axis=0
    )
    out_ref[2 * TOK :] = jnp.concatenate([meta, jnp.zeros_like(meta)], axis=1).astype(BF16)
    copies[2].wait()
    copies[3].wait()


def read_meta(packed_ref):
    meta = packed_ref[2 * TOK :, 0:TOK].astype(F32)
    gates = meta[2:4] + meta[4:6] + meta[6:8]
    return meta[0:2], gates


def dispatch_kernel(split, me_ref, packed_ref, *out_refs):
    z, h = me_ref[0] >> 1, me_ref[0] & 1
    ids, gates = read_meta(packed_ref)
    count = 4 * LOCAL
    index = lax.broadcasted_iota(jnp.int32, (16, TOK), 0)
    want = (((z + (index & 3)) & 3) * 2 + h) * LOCAL + (index >> 2)
    want = jnp.where(index < count, want, -1).astype(F32)
    hit0 = ids[0:1] == want
    hit1 = ids[1:2] == want
    hit = jnp.where(hit0 | hit1, 1.0, 0.0).astype(F32)
    gate = jnp.where(hit0, gates[0:1], jnp.where(hit1, gates[1:2], 0.0))
    earlier = lax.broadcasted_iota(jnp.int32, (TOK, TOK), 0) < lax.broadcasted_iota(
        jnp.int32, (TOK, TOK), 1
    )
    before = dot(hit.astype(BF16), jnp.where(earlier, 1.0, 0.0).astype(BF16))
    place = jnp.where(hit > 0.0, before, -1.0).astype(jnp.int32)
    slot = lax.broadcasted_iota(jnp.int32, (CAP, TOK), 0)
    for j in range(LOCAL):
        picks, weights = [], []
        for n in range(j * 4, j * 4 + 4):
            sel = slot == place[n : n + 1]
            picks.append(jnp.where(sel, 1.0, 0.0).astype(BF16))
            weights.append(jnp.sum(jnp.where(sel, gate[n : n + 1], 0.0), axis=1, keepdims=True))
        pick = jnp.concatenate(picks, axis=0)
        weight = jnp.concatenate(weights, axis=0)
        rows = dot(pick, packed_ref[0:TOK]).astype(BF16)
        grads = (weight * dot(pick, packed_ref[TOK : 2 * TOK])).astype(BF16)
        for dz in range(4):
            part = slice(dz * CAP, (dz + 1) * CAP)
            ref, at = out_refs[dz], j
            if split:
                ref, at = (out_refs[dz], 0) if j == 0 else (out_refs[4 + dz], j - 1)
            ref[at, 0] = rows[part]
            ref[at, 1] = grads[part]


def dispatch(name, split, me, packed):
    out = [bf16_like(n, 2, CAP, D) for n in ((1, 2) if split else (3,)) for _ in range(4)]
    kernel = functools.partial(dispatch_kernel, split)
    return call(kernel, name, [SMEM, VMEM], out, (me, packed), 3 * 10**6)


def join_kernel(count, *refs):
    ins, out_ref = refs[:SOURCES], refs[-1]
    for n, ref in enumerate(ins):
        skip = ref.shape[0] - count
        for j in range(count):
            out_ref[j, n] = ref[skip + j if count > 1 else 0]


def join(name, count, pieces, after):
    specs = [VMEM] * SOURCES + [pl.BlockSpec(memory_space=pl.ANY)] * len(after)
    out = bf16_like(count, SOURCES, 2, CAP, D)
    return call(functools.partial(join_kernel, count), name, specs, out, (*pieces, *after), 10**6)


def share(x_s, g_s, xt_s, gt_s, eo_s, ig_s, weights, homes):
    wg = jnp.concatenate([weights[0][...], weights[1][...]], axis=1)
    wu = jnp.concatenate([weights[2][...], weights[3][...]], axis=1)
    wd = jnp.concatenate([weights[4][...], weights[5][...]], axis=0)
    x = x_s[...]
    g = g_s[...]
    pre_gate = dot(x, wg)
    pre_up = dot(x, wu)
    grad_hidden = dot(g, wd, 1, 1)
    sig = jax.nn.sigmoid(pre_gate)
    silu = pre_gate * sig
    hidden = (silu * pre_up).astype(BF16)
    grad_gate = (grad_hidden * pre_up * sig * (1.0 + pre_gate * (1.0 - sig))).astype(BF16)
    grad_up = (grad_hidden * silu).astype(BF16)
    parts = [
        dot(xt_s[...], grad_gate).astype(BF16),
        dot(xt_s[...], grad_up).astype(BF16),
        dot(gt_s[...], hidden).astype(BF16),
    ]
    i = pl.program_id(0)
    for step, pair in enumerate(homes):

        @pl.when(i == step)
        def _(pair=pair):
            for lane, ref in enumerate(pair):
                for k, part in enumerate(parts):
                    ref[k * D : (k + 1) * D, :] = part[:, lane * BLK : (lane + 1) * BLK]

    eo_s[...] += dot(hidden, wd)
    ig_s[...] += dot(grad_gate, wg, 1, 1) + dot(grad_up, wu, 1, 1)


def expert_kernel(has_sums, ends, n_after, counts, tbl_ref, own_ref, oth_ref, *refs):
    weights, refs = refs[:6], refs[6:]
    if has_sums:
        sums, refs = refs[:2], refs[2:]
    refs = refs[n_after:]
    chunks, refs = refs[: len(counts)], refs[len(counts) :]
    results, (x_s, g_s, xt_s, gt_s, *acc) = refs[:2], refs[2:]
    eo_s, ig_s = acc if ends else results
    i = pl.program_id(0)
    flat = [ref.at[n] for ref, count in zip(chunks, counts) for n in range(count)]
    steps = len(flat) // 2

    @pl.when(i == 0)
    def _():
        for k, ref in enumerate((own_ref, oth_ref)):
            x_s[k * ROWS : (k + 1) * ROWS, :] = ref[:, 0].reshape(ROWS, D)
            g_s[k * ROWS : (k + 1) * ROWS, :] = ref[:, 1].reshape(ROWS, D)
        xt_s[...] = x_s[...].T
        gt_s[...] = g_s[...].T
        eo_s[...] = sums[0][...] if has_sums else jnp.zeros_like(eo_s)
        ig_s[...] = sums[1][...] if has_sums else jnp.zeros_like(ig_s)

    homes = [flat[2 * n : 2 * n + 2] for n in range(steps)]
    share(x_s, g_s, xt_s, gt_s, eo_s, ig_s, weights, homes)
    if ends:

        @pl.when(i == steps - 1)
        def _():
            for k, ref in enumerate(results):
                ref[0] = eo_s[k * ROWS : (k + 1) * ROWS, :].astype(BF16)
                ref[1] = ig_s[k * ROWS : (k + 1) * ROWS, :].astype(BF16)


def expert(name, j, at, tbl, base, counts, ends, own, oth, weights, sums=(), after=()):
    rows = 2 * ROWS
    steps = sum(counts) // 2

    def fixed(shape):
        return pl.BlockSpec(shape, lambda i, tbl: (0,) * len(shape))

    def columns(k):
        return pl.BlockSpec((None, D, BLK), lambda i, tbl: (j, 0, tbl[base + 2 * i + k]))

    def lines(k):
        return pl.BlockSpec((None, BLK, D), lambda i, tbl: (j, tbl[base + 2 * i + k], 0))

    joined = pl.BlockSpec((None, SOURCES, 2, CAP, D), lambda i, tbl: (at, 0, 0, 0, 0))
    out = [bf16_like(count, 3 * D, BLK) for count in counts]
    scratch = [pltpu.VMEM((rows, D), BF16)] * 2 + [pltpu.VMEM((D, rows), BF16)] * 2
    if ends:
        out += [bf16_like(2, ROWS, D)] * 2
        scratch += [pltpu.VMEM((rows, D), F32)] * 2
    else:
        out += [jax.ShapeDtypeStruct((rows, D), F32)] * 2
    w_gate, w_up, w_down = weights
    return pl.pallas_call(
        functools.partial(expert_kernel, bool(sums), ends, len(after), counts),
        grid_spec=pltpu.PrefetchScalarGridSpec(
            num_scalar_prefetch=1,
            grid=(steps,),
            in_specs=[joined, joined]
            + [columns(0), columns(1), columns(0), columns(1), lines(0), lines(1)]
            + [fixed((rows, D))] * len(sums)
            + [pl.BlockSpec(memory_space=pl.ANY)] * len(after),
            out_specs=[fixed(s.shape) for s in out],
            scratch_shapes=scratch,
        ),
        out_shape=out,
        compiler_params=pltpu.CompilerParams(
            dimension_semantics=("arbitrary",), vmem_limit_bytes=EXPERT_LIMIT
        ),
        cost_estimate=pl.CostEstimate(
            flops=COST[name] * 10**9, bytes_accessed=10**6, transcendentals=0
        ),
        name=name,
    )(tbl, own, oth, w_gate, w_gate, w_up, w_up, w_down, w_down, *sums, *after)


def back_kernel(count, n_after, *refs):
    ins, outs = refs[: 2 * count], refs[2 * count + n_after :]
    for j in range(count):
        own_ref, oth_ref = ins[2 * j : 2 * j + 2]
        for n in range(SOURCES):
            for k in range(2):
                rows = slice(n * CAP, (n + 1) * CAP)
                total = own_ref[k, rows].astype(F32) + oth_ref[k, rows].astype(F32)
                outs[n & 3][j, n >> 2, k] = total.astype(BF16)


def back(name, pairs, after=()):
    count = len(pairs) // 2
    out = [bf16_like(count, 2, 2, CAP, D)] * 4
    specs = [VMEM] * len(pairs) + [pl.BlockSpec(memory_space=pl.ANY)] * len(after)
    kernel = functools.partial(back_kernel, count, len(after))
    return call(kernel, name, specs, out, (*pairs, *after), 10**6)


def token_sums(side, me_ref, packed_ref, rows, out_s, in_s):
    z, h = me_ref[0] >> 1, me_ref[0] & 1
    for dz in range(4):
        first, last = rows[dz], rows[4 + dz]
        for j in range(LOCAL):
            ref, at = (first, j) if j < LOCAL - 1 else (last, 0)
            n = j * 4 + dz
            out_s[n * CAP : (n + 1) * CAP, :] = ref[at, side, 0]
            in_s[n * CAP : (n + 1) * CAP, :] = ref[at, side, 1]
    ids, gates = read_meta(packed_ref)
    columns = jnp.concatenate([ids, gates, jnp.zeros((4, TOK), F32)], axis=0).T
    lane = lax.broadcasted_iota(jnp.int32, (TOK, 128), 1)
    want = (((z + (lane & 3)) & 3) * 2 + h) * LOCAL + (lane >> 2)
    want = jnp.where(lane < 4 * LOCAL, want, -1).astype(F32)
    hits = [columns[:, k : k + 1] == want for k in range(2)]
    either = jnp.where(hits[0] | hits[1], 1.0, 0.0).astype(BF16)
    earlier = lax.broadcasted_iota(jnp.int32, (TOK, TOK), 1) < lax.broadcasted_iota(
        jnp.int32, (TOK, TOK), 0
    )
    before = dot(jnp.where(earlier, 1.0, 0.0).astype(BF16), either)
    code = before + (lane * CAP + 1).astype(F32)
    slots = lax.broadcasted_iota(jnp.int32, (TOK, 4 * LOCAL * CAP), 1)
    picks = []
    for k in range(2):
        slot = jnp.sum(jnp.where(hits[k], code, 0.0), axis=1, keepdims=True).astype(jnp.int32) - 1
        picks.append(jnp.where(slots == slot, 1.0, 0.0).astype(BF16))
    mixed = columns[:, 2:3] * dot(picks[0], out_s[...]) + columns[:, 3:4] * dot(picks[1], out_s[...])
    return mixed, dot(picks[0] + picks[1], in_s[...])


def partner_kernel(me_ref, packed_ref, *refs):
    rows, (out_ref, out_s, in_s) = refs[:-3], refs[-3:]
    mixed, grad = token_sums(1, me_ref, packed_ref, rows, out_s, in_s)
    out_ref[0] = mixed.astype(BF16)
    out_ref[1] = grad.astype(BF16)


def combine_kernel(me_ref, packed_ref, other_ref, *refs):
    rows, (mixed_ref, grad_ref, out_s, in_s) = refs[:-4], refs[-4:]
    mixed, grad = token_sums(0, me_ref, packed_ref, rows, out_s, in_s)
    mixed_ref[...] = (mixed + other_ref[0].astype(F32)).astype(BF16)
    grad_ref[...] = (grad + other_ref[1].astype(F32)).astype(BF16)


def finish_kernel(*refs):
    ins, outs = refs[: 2 * LOCAL], refs[2 * LOCAL :]
    for j in range(LOCAL):
        total = (ins[2 * j][...].astype(F32) + ins[2 * j + 1][...].astype(F32)).astype(BF16)
        outs[0][j] = total[0:D]
        outs[1][j] = total[D : 2 * D]
        outs[2][j] = total[2 * D :].T


def add(*terms):
    return functools.reduce(lambda a, b: a + b, [t.astype(F32) for t in terms]).astype(BF16)


def local(tokens, expert_ids, gates, cotangent, w_gate, w_up, w_down):
    me = lax.axis_index("expert").astype(jnp.int32).reshape(1)
    rep = lax.axis_index("replica").astype(jnp.int32)
    y, x, core = rep >> 2, (rep >> 1) & 1, rep & 1
    step = jnp.arange(16, dtype=jnp.int32)
    hop = jnp.where(step < 8, step >> 1, step & 3)
    flip = jnp.where(step < 8, step & 1, (step < 12).astype(jnp.int32))
    tbl = ((y + (3 - hop) * (1 - 2 * core)) & 3) * 4 + (x ^ flip) * 2 + core

    def over_replica(label, value, perm):
        with jax.named_scope(label):
            return lax.ppermute(value, "replica", perm)

    def to_z(label, value, dz):
        with jax.named_scope(label):
            return lax.ppermute(value, "expert", along_z(dz))

    packed = call(
        pack_kernel,
        "pack",
        [pl.BlockSpec(memory_space=pltpu.HBM)] * 4,
        bf16_like(2 * TOK + META, D),
        (tokens, cotangent, expert_ids.T, gates.T),
        scratch=[
            pltpu.VMEM((2, TOK), jnp.int32),
            pltpu.VMEM((2, TOK), F32),
            pltpu.SemaphoreType.DMA((4,)),
        ],
        limit=63 * 1024 * 1024,
    )
    with jax.named_scope("packed"):
        partner = lax.ppermute(packed, "expert", PARTNER)
    sent = dispatch("own_slots", False, me, packed)
    from_own = [sent[0]] + [to_z("own_rows", sent[dz], dz) for dz in range(1, 4)]
    sent = dispatch("partner_slots", True, me, partner)
    firsts = [sent[0]] + [to_z("partner_rows0", sent[dz], dz) for dz in range(1, 4)]
    rests = [sent[4]] + [to_z("partner_rows12", sent[4 + dz], dz) for dz in range(1, 4)]

    weights = (w_gate, w_up, w_down)
    own0 = join("join0", 1, from_own + firsts, ())
    oth0 = over_replica("core_rows0", own0, CORE)
    far0, *sums = expert("expert0_first", 0, 0, tbl, 0, (2,), False, own0, oth0, weights)
    second0 = over_replica("ring0_1", far0, RING)
    own12 = join("join12", 2, from_own + rests, (far0,))
    oth12 = over_replica("core_rows12", own12, CORE)
    mid0, near0, home0, ret0, swap0 = expert(
        "expert0_rest", 0, 0, tbl, 2, (2, 2, 2), True, own0, oth0, weights, sums, (own12,)
    )
    mid0, swap0, second0 = lax.optimization_barrier((mid0, swap0, second0))
    second0 = add(mid0, second0)
    third0 = over_replica("ring0_2", second0, RING)
    swap0 = over_replica("core_back0", swap0, CORE)
    cross1a, cross1b, all1, ret1, swap1 = expert(
        "expert1", 1, 0, tbl, 8, (2, 2, 4), True, own12, oth12, weights, (), (second0,)
    )
    cross1a, swap1, third0 = lax.optimization_barrier((cross1a, swap1, third0))
    third0 = add(near0, third0)
    last0 = over_replica("ring0_3", third0, RING)
    crossed1a = over_replica("cross1a", cross1a, ACROSS)
    swap1 = over_replica("core_back1", swap1, CORE)
    far2, *sums = expert(
        "expert2_first", 2, 1, tbl, 0, (2,), False, own12, oth12, weights, (), (third0, ret1)
    )
    second2 = over_replica("ring2_1", far2, RING)
    back01 = back("back01", (ret0, swap0, ret1, swap1), (far2,))
    mid2, near2, home2, ret2, swap2 = expert(
        "expert2_rest", 2, 1, tbl, 2, (2, 2, 2), True, own12, oth12, weights, sums, (back01[0],)
    )
    mid2, swap2, second2, last0, crossed1a = lax.optimization_barrier(
        (mid2, swap2, second2, last0, crossed1a)
    )
    ring1 = over_replica("ring1_1", add(all1[0], crossed1a[0]), RING)
    crossed1b = over_replica("cross1b", cross1b, ACROSS)
    second2 = add(mid2, second2)
    third2 = over_replica("ring2_2", second2, RING)
    across0 = add(home0[1], last0[1])
    across0_out = over_replica("across0", across0, ACROSS)
    swap2 = over_replica("core_back2", swap2, CORE)
    rows = [back01[0]] + [to_z("rows_back01", back01[dz], 4 - dz) for dz in range(1, 4)]
    back2 = back("back2", (ret2, swap2), (second2, across0, *rows[1:]))
    third2, ring1, local2 = lax.optimization_barrier((third2, ring1, back2[0]))
    ring1 = over_replica("ring1_2", add(all1[1], crossed1a[1], ring1), RING)
    third2 = add(near2, third2)
    last2 = over_replica("ring2_3", third2, RING)
    rows += [local2] + [to_z("rows_back2", back2[dz], 4 - dz) for dz in range(1, 4)]
    crossed1b, ring1, across0_out, last2, *rows = lax.optimization_barrier(
        (crossed1b, ring1, across0_out, last2, *rows)
    )
    ring1 = over_replica("ring1_3", add(all1[2], crossed1b[0], ring1), RING)
    across2 = over_replica("across2", add(home2[1], last2[1]), ACROSS)
    scratch = [pltpu.VMEM((4 * LOCAL * CAP, D), BF16)] * 2
    theirs = call(
        partner_kernel, "partner_sums", [SMEM] + [VMEM] * 9, bf16_like(2, TOK, D),
        (me, partner, *rows), 3 * 10**6, scratch,
    )
    parts = [add(home0[0], last0[0]), across0_out]
    parts += [add(all1[3], crossed1b[1]), ring1]
    parts += [add(home2[0], last2[0]), across2]
    with jax.named_scope("partner_out"):
        others = lax.ppermute(theirs, "expert", PARTNER)
    mixed, token_grad = call(
        combine_kernel, "combine", [SMEM] + [VMEM] * 10, [bf16_like(TOK, D)] * 2,
        (me, packed, others, *rows), 3 * 10**6, scratch,
    )
    gate_grad, up_grad, down_grad = call(
        finish_kernel, "finish", [VMEM] * len(parts),
        [bf16_like(LOCAL, D, BLK), bf16_like(LOCAL, D, BLK), bf16_like(LOCAL, BLK, D)],
        parts, 4 * 10**6,
    )
    return mixed, token_grad, gate_grad, up_grad, down_grad


def solution(mesh):
    tokens = P(("expert", "replica"), None)
    return jax.shard_map(
        local,
        mesh=mesh,
        in_specs=(tokens,) * 4 + (P("expert", None, None),) * 3,
        out_specs=(tokens,) * 2
        + (P("expert", None, "replica"), P("expert", None, "replica"), P("expert", "replica", None)),
        check_vma=False,
    )
```

```python
import functools

import jax
import jax.numpy as jnp
from jax import lax
from jax.experimental import pallas as pl
from jax.experimental.pallas import tpu as pltpu
from jax.sharding import PartitionSpec as P

CAP = 48
LOCAL = 3
SOURCES = 8
ROWS = SOURCES * CAP
D = 512
TOK = 256
BLK = 128
META = 16
F32 = jnp.float32
BF16 = jnp.bfloat16
VMEM_LIMIT = 32 * 1024 * 1024
EXPERT_LIMIT = 44 * 1024 * 1024
COST = {
    "expert0_first": 20,
    "expert0_rest": 20,
    "expert1": 20,
    "expert2_first": 20,
    "expert2_rest": 10,
}
VMEM = pl.BlockSpec(memory_space=pltpu.VMEM)
SMEM = pl.BlockSpec(memory_space=pltpu.SMEM)


def dot(a, b, ca=1, cb=0):
    return lax.dot_general(a, b, (((ca,), (cb,)), ((), ())), preferred_element_type=F32)


def bf16_like(*shape):
    return jax.ShapeDtypeStruct(shape, BF16)


def call(kernel, name, in_specs, out_shape, args, nbytes=10**6, scratch=(), limit=VMEM_LIMIT):
    return pl.pallas_call(
        kernel,
        in_specs=in_specs,
        out_specs=jax.tree.map(lambda _: VMEM, out_shape),
        out_shape=out_shape,
        scratch_shapes=list(scratch),
        compiler_params=pltpu.CompilerParams(vmem_limit_bytes=limit),
        cost_estimate=pl.CostEstimate(flops=0, bytes_accessed=nbytes, transcendentals=0),
        name=name,
    )(*args)


def along_z(dz):
    return [(z * 2 + h, ((z + dz) % 4) * 2 + h) for z in range(4) for h in range(2)]


PARTNER = [(e, e ^ 1) for e in range(8)]
CORE = [(r, r ^ 1) for r in range(16)]
ACROSS = [(r, r ^ 2) for r in range(16)]
RING = [(r, (r + (4 if r % 2 == 0 else 12)) % 16) for r in range(16)]


def pack_kernel(tokens_ref, cot_ref, ids_ref, gates_ref, out_ref, ids_s, gates_s, sems):
    copies = [
        pltpu.make_async_copy(src, dst, sems.at[n])
        for n, (src, dst) in enumerate(
            (
                (ids_ref, ids_s),
                (gates_ref, gates_s),
                (tokens_ref, out_ref.at[pl.ds(0, TOK)]),
                (cot_ref, out_ref.at[pl.ds(TOK, TOK)]),
            )
        )
    ]
    for copy in copies:
        copy.start()
    copies[0].wait()
    copies[1].wait()
    gates = gates_s[...]
    high = gates.astype(BF16).astype(F32)
    middle = (gates - high).astype(BF16).astype(F32)
    low = gates - high - middle
    meta = jnp.concatenate(
        [ids_s[...].astype(F32), high, middle, low, jnp.zeros((META - 8, TOK), F32)], axis=0
    )
    out_ref[2 * TOK :] = jnp.concatenate([meta, jnp.zeros_like(meta)], axis=1).astype(BF16)
    copies[2].wait()
    copies[3].wait()


def read_meta(packed_ref):
    meta = packed_ref[2 * TOK :, 0:TOK].astype(F32)
    gates = meta[2:4] + meta[4:6] + meta[6:8]
    return meta[0:2], gates


def dispatch_kernel(split, me_ref, packed_ref, *out_refs):
    z, h = me_ref[0] >> 1, me_ref[0] & 1
    ids, gates = read_meta(packed_ref)
    count = 4 * LOCAL
    index = lax.broadcasted_iota(jnp.int32, (16, TOK), 0)
    want = (((z + (index & 3)) & 3) * 2 + h) * LOCAL + (index >> 2)
    want = jnp.where(index < count, want, -1).astype(F32)
    hit0 = ids[0:1] == want
    hit1 = ids[1:2] == want
    hit = jnp.where(hit0 | hit1, 1.0, 0.0).astype(F32)
    gate = jnp.where(hit0, gates[0:1], jnp.where(hit1, gates[1:2], 0.0))
    earlier = lax.broadcasted_iota(jnp.int32, (TOK, TOK), 0) < lax.broadcasted_iota(
        jnp.int32, (TOK, TOK), 1
    )
    before = dot(hit.astype(BF16), jnp.where(earlier, 1.0, 0.0).astype(BF16))
    place = jnp.where(hit > 0.0, before, -1.0).astype(jnp.int32)
    slot = lax.broadcasted_iota(jnp.int32, (CAP, TOK), 0)
    for j in range(LOCAL):
        picks, weights = [], []
        for n in range(j * 4, j * 4 + 4):
            sel = slot == place[n : n + 1]
            picks.append(jnp.where(sel, 1.0, 0.0).astype(BF16))
            weights.append(jnp.sum(jnp.where(sel, gate[n : n + 1], 0.0), axis=1, keepdims=True))
        pick = jnp.concatenate(picks, axis=0)
        weight = jnp.concatenate(weights, axis=0)
        rows = dot(pick, packed_ref[0:TOK]).astype(BF16)
        grads = (weight * dot(pick, packed_ref[TOK : 2 * TOK])).astype(BF16)
        for dz in range(4):
            part = slice(dz * CAP, (dz + 1) * CAP)
            ref, at = out_refs[dz], j
            if split:
                ref, at = (out_refs[dz], 0) if j == 0 else (out_refs[4 + dz], j - 1)
            ref[at, 0] = rows[part]
            ref[at, 1] = grads[part]


def dispatch(name, split, me, packed):
    out = [bf16_like(n, 2, CAP, D) for n in ((1, 2) if split else (3,)) for _ in range(4)]
    kernel = functools.partial(dispatch_kernel, split)
    return call(kernel, name, [SMEM, VMEM], out, (me, packed), 3 * 10**6)


def join_kernel(count, *refs):
    ins, out_ref = refs[:SOURCES], refs[-1]
    for n, ref in enumerate(ins):
        skip = ref.shape[0] - count
        for j in range(count):
            out_ref[j, n] = ref[skip + j if count > 1 else 0]


def join(name, count, pieces, after):
    specs = [VMEM] * SOURCES + [pl.BlockSpec(memory_space=pl.ANY)] * len(after)
    out = bf16_like(count, SOURCES, 2, CAP, D)
    return call(functools.partial(join_kernel, count), name, specs, out, (*pieces, *after), 10**6)


def expert_kernel(j, at, base, counts, has_sums, ends, n_after, tbl_ref, own_ref, oth_ref, *refs):
    weights, refs = refs[:3], refs[3:]
    if has_sums:
        sums, refs = refs[:2], refs[2:]
    refs = refs[n_after:]
    chunks, refs = refs[: len(counts)], refs[len(counts) :]
    results, (x_s, g_s, xt_s, gt_s, wg_s, wu_s, wd_s, sems, *acc) = refs[:2], refs[2:]
    eo_s, ig_s = acc if ends else results
    flat = [ref.at[n] for ref, count in zip(chunks, counts) for n in range(count)]
    steps = len(flat) // 2

    def fetch(i):
        slot, copies = i % 2, []
        for k in range(2):
            block = pl.ds(pl.multiple_of(tbl_ref[base + 2 * i + k] * BLK, BLK), BLK)
            here = pl.ds(k * BLK, BLK)
            pairs = (
                (weights[0].at[j, :, block], wg_s.at[slot, :, here]),
                (weights[1].at[j, :, block], wu_s.at[slot, :, here]),
                (weights[2].at[j, block, :], wd_s.at[slot, here, :]),
            )
            for n, (src, dst) in enumerate(pairs):
                copies.append(pltpu.make_async_copy(src, dst, sems.at[slot, 3 * k + n]))
        return copies

    for copy in fetch(0):
        copy.start()
    for k, ref in enumerate((own_ref, oth_ref)):
        x_s[k * ROWS : (k + 1) * ROWS, :] = ref[at, :, 0].reshape(ROWS, D)
        g_s[k * ROWS : (k + 1) * ROWS, :] = ref[at, :, 1].reshape(ROWS, D)
    xt_s[...] = x_s[...].T
    gt_s[...] = g_s[...].T
    for i in range(steps):
        if i + 1 < steps:
            for copy in fetch(i + 1):
                copy.start()
        for copy in fetch(i):
            copy.wait()
        wg, wu, wd = wg_s[i % 2], wu_s[i % 2], wd_s[i % 2]
        acts = []
        for half in range(2):
            part = slice(half * ROWS, (half + 1) * ROWS)
            x, g = x_s[part], g_s[part]
            pre_gate = dot(x, wg)
            pre_up = dot(x, wu)
            grad_hidden = dot(g, wd, 1, 1)
            sig = jax.nn.sigmoid(pre_gate)
            silu = pre_gate * sig
            hidden = (silu * pre_up).astype(BF16)
            grad_gate = (grad_hidden * pre_up * sig * (1.0 + pre_gate * (1.0 - sig))).astype(BF16)
            grad_up = (grad_hidden * silu).astype(BF16)
            acts.append((grad_gate, grad_up, hidden))
            out_rows = dot(hidden, wd)
            in_rows = dot(grad_gate, wg, 1, 1) + dot(grad_up, wu, 1, 1)
            if i > 0 or has_sums:
                before = (eo_s, ig_s) if i > 0 else sums
                out_rows = before[0][part] + out_rows
                in_rows = before[1][part] + in_rows
            eo_s[part] = out_rows
            ig_s[part] = in_rows
        for k, rows_t in enumerate((xt_s, xt_s, gt_s)):
            act = jnp.concatenate([acts[0][k], acts[1][k]], axis=0)
            grad = dot(rows_t[...], act).astype(BF16)
            for lane in range(2):
                flat[2 * i + lane][k * D : (k + 1) * D, :] = grad[:, lane * BLK : (lane + 1) * BLK]
    if ends:
        for k, ref in enumerate(results):
            ref[0] = eo_s[k * ROWS : (k + 1) * ROWS, :].astype(BF16)
            ref[1] = ig_s[k * ROWS : (k + 1) * ROWS, :].astype(BF16)


def expert(name, j, at, tbl, base, counts, ends, own, oth, weights, sums=(), after=()):
    rows = 2 * ROWS
    out = [bf16_like(count, 3 * D, BLK) for count in counts]
    scratch = [pltpu.VMEM((rows, D), BF16)] * 2 + [pltpu.VMEM((D, rows), BF16)] * 2
    scratch += [pltpu.VMEM((2, D, 2 * BLK), BF16)] * 2 + [pltpu.VMEM((2, 2 * BLK, D), BF16)]
    scratch += [pltpu.SemaphoreType.DMA((2, 6))]
    if ends:
        out += [bf16_like(2, ROWS, D)] * 2
        scratch += [pltpu.VMEM((rows, D), F32)] * 2
    else:
        out += [jax.ShapeDtypeStruct((rows, D), F32)] * 2
    anywhere = pl.BlockSpec(memory_space=pl.ANY)
    kernel = functools.partial(
        expert_kernel, j, at, base, counts, bool(sums), ends, len(after)
    )
    return pl.pallas_call(
        kernel,
        in_specs=[SMEM, VMEM, VMEM] + [anywhere] * 3 + [VMEM] * len(sums) + [anywhere] * len(after),
        out_specs=[VMEM] * len(out),
        scratch_shapes=scratch,
        out_shape=out,
        compiler_params=pltpu.CompilerParams(vmem_limit_bytes=EXPERT_LIMIT),
        cost_estimate=pl.CostEstimate(
            flops=COST[name] * 10**9, bytes_accessed=10**6, transcendentals=0
        ),
        name=name,
    )(tbl, own, oth, *weights, *sums, *after)


def sums_kernel(terms, *refs):
    out_ref = refs[-1]
    for n, pairs in enumerate(terms):
        total = refs[pairs[0][0]][pairs[0][1]].astype(F32)
        for ref, index in pairs[1:]:
            total = total + refs[ref][index].astype(F32)
        out_ref[n] = total.astype(BF16)


def ring_sums(name, terms, args):
    out = bf16_like(len(terms), 3 * D, BLK)
    return call(functools.partial(sums_kernel, terms), name, [VMEM] * len(args), out, args)


def back_kernel(count, me_ref, *refs):
    ins, outs = refs[: 2 * count], refs[2 * count :]
    if count > 1:
        outs = outs[-1:]
    z = me_ref[0] >> 1
    for n in range(SOURCES):
        for j in range(count):
            for k in range(2):
                rows = slice(n * CAP, (n + 1) * CAP)
                total = ins[2 * j][k, rows].astype(F32) + ins[2 * j + 1][k, rows].astype(F32)
                if count > 1:
                    outs[0][(z + 4 - (n & 3)) & 3, j, n >> 2, k] = total.astype(BF16)
                else:
                    outs[n & 3][j, n >> 2, k] = total.astype(BF16)


def back(name, me, pairs, after=()):
    count = len(pairs) // 2
    out = bf16_like(4, count, 2, 2, CAP, D) if count > 1 else [bf16_like(1, 2, 2, CAP, D)] * 4
    specs = [SMEM] + [VMEM] * len(pairs) + [pl.BlockSpec(memory_space=pl.ANY)] * len(after)
    return call(functools.partial(back_kernel, count), name, specs, out, (me, *pairs, *after))


def token_sums(side, me_ref, packed_ref, rows, out_s, in_s):
    z, h = me_ref[0] >> 1, me_ref[0] & 1
    for dz in range(4):
        for j in range(LOCAL):
            n = j * 4 + dz
            for k, dst in enumerate((out_s, in_s)):
                if j < LOCAL - 1:
                    dst[n * CAP : (n + 1) * CAP, :] = rows[0][(z + dz) & 3, j, side, k]
                else:
                    dst[n * CAP : (n + 1) * CAP, :] = rows[1 + dz][0, side, k]
    ids, gates = read_meta(packed_ref)
    columns = jnp.concatenate([ids, gates, jnp.zeros((4, TOK), F32)], axis=0).T
    lane = lax.broadcasted_iota(jnp.int32, (TOK, 128), 1)
    want = (((z + (lane & 3)) & 3) * 2 + h) * LOCAL + (lane >> 2)
    want = jnp.where(lane < 4 * LOCAL, want, -1).astype(F32)
    hits = [columns[:, k : k + 1] == want for k in range(2)]
    either = jnp.where(hits[0] | hits[1], 1.0, 0.0).astype(BF16)
    earlier = lax.broadcasted_iota(jnp.int32, (TOK, TOK), 1) < lax.broadcasted_iota(
        jnp.int32, (TOK, TOK), 0
    )
    before = dot(jnp.where(earlier, 1.0, 0.0).astype(BF16), either)
    code = before + (lane * CAP + 1).astype(F32)
    slots = lax.broadcasted_iota(jnp.int32, (TOK, 4 * LOCAL * CAP), 1)
    picks = []
    for k in range(2):
        slot = jnp.sum(jnp.where(hits[k], code, 0.0), axis=1, keepdims=True).astype(jnp.int32) - 1
        picks.append(jnp.where(slots == slot, 1.0, 0.0).astype(BF16))
    mixed = columns[:, 2:3] * dot(picks[0], out_s[...]) + columns[:, 3:4] * dot(picks[1], out_s[...])
    return mixed, dot(picks[0] + picks[1], in_s[...])


def partner_kernel(me_ref, packed_ref, *refs):
    rows, (out_ref, out_s, in_s) = refs[:-3], refs[-3:]
    mixed, grad = token_sums(1, me_ref, packed_ref, rows, out_s, in_s)
    out_ref[0] = mixed.astype(BF16)
    out_ref[1] = grad.astype(BF16)


def combine_kernel(me_ref, packed_ref, other_ref, *refs):
    rows, (mixed_ref, grad_ref, out_s, in_s) = refs[:-4], refs[-4:]
    mixed, grad = token_sums(0, me_ref, packed_ref, rows, out_s, in_s)
    mixed_ref[...] = (mixed + other_ref[0].astype(F32)).astype(BF16)
    grad_ref[...] = (grad + other_ref[1].astype(F32)).astype(BF16)


def finish_kernel(*refs):
    ins, outs = refs[: 2 * LOCAL], refs[2 * LOCAL :]
    for j in range(LOCAL):
        total = (ins[2 * j][...].astype(F32) + ins[2 * j + 1][...].astype(F32)).astype(BF16)
        outs[0][j] = total[0:D]
        outs[1][j] = total[D : 2 * D]
        outs[2][j] = total[2 * D :].T


def add(*terms):
    return functools.reduce(lambda a, b: a + b, [t.astype(F32) for t in terms]).astype(BF16)


def local(tokens, expert_ids, gates, cotangent, w_gate, w_up, w_down):
    me = lax.axis_index("expert").astype(jnp.int32).reshape(1)
    rep = lax.axis_index("replica").astype(jnp.int32)
    y, x, core = rep >> 2, (rep >> 1) & 1, rep & 1
    step = jnp.arange(16, dtype=jnp.int32)
    hop = jnp.where(step < 8, step >> 1, step & 3)
    flip = jnp.where(step < 8, step & 1, (step < 12).astype(jnp.int32))
    tbl = ((y + (3 - hop) * (1 - 2 * core)) & 3) * 4 + (x ^ flip) * 2 + core

    def over_replica(label, value, perm):
        with jax.named_scope(label):
            return lax.ppermute(value, "replica", perm)

    def to_z(label, value, dz):
        with jax.named_scope(label):
            return lax.ppermute(value, "expert", along_z(dz))

    packed = call(
        pack_kernel,
        "pack",
        [pl.BlockSpec(memory_space=pltpu.HBM)] * 4,
        bf16_like(2 * TOK + META, D),
        (tokens, cotangent, expert_ids.T, gates.T),
        scratch=[
            pltpu.VMEM((2, TOK), jnp.int32),
            pltpu.VMEM((2, TOK), F32),
            pltpu.SemaphoreType.DMA((4,)),
        ],
        limit=63 * 1024 * 1024,
    )
    with jax.named_scope("packed"):
        partner = lax.ppermute(packed, "expert", PARTNER)
    sent = dispatch("own_slots", False, me, packed)
    from_own = [sent[0]] + [to_z("own_rows", sent[dz], dz) for dz in range(1, 4)]
    sent = dispatch("partner_slots", True, me, partner)
    firsts = [sent[0]] + [to_z("partner_rows0", sent[dz], dz) for dz in range(1, 4)]
    rests = [sent[4]] + [to_z("partner_rows12", sent[4 + dz], dz) for dz in range(1, 4)]

    weights = (w_gate, w_up, w_down)
    own0 = join("join0", 1, from_own + firsts, ())
    oth0 = over_replica("core_rows0", own0, CORE)
    far0, *sums = expert("expert0_first", 0, 0, tbl, 0, (2,), False, own0, oth0, weights)
    second0 = over_replica("ring0_1", far0, RING)
    own12 = join("join12", 2, from_own + rests, (far0,))
    oth12 = over_replica("core_rows12", own12, CORE)
    mid0, near0, home0, ret0, swap0 = expert(
        "expert0_rest", 0, 0, tbl, 2, (2, 2, 2), True, own0, oth0, weights, sums, (own12,)
    )
    mid0, swap0, second0 = lax.optimization_barrier((mid0, swap0, second0))
    second0 = add(mid0, second0)
    third0 = over_replica("ring0_2", second0, RING)
    swap0 = over_replica("core_back0", swap0, CORE)
    cross1a, cross1b, *mine1, ret1, swap1 = expert(
        "expert1", 1, 0, tbl, 8, (2, 2, 1, 1, 1, 1), True, own12, oth12, weights, (), (second0,)
    )
    cross1a, swap1, third0 = lax.optimization_barrier((cross1a, swap1, third0))
    third0 = add(near0, third0)
    last0 = over_replica("ring0_3", third0, RING)
    crossed1a = over_replica("cross1a", cross1a, ACROSS)
    swap1 = over_replica("core_back1", swap1, CORE)
    far2, *sums = expert(
        "expert2_first", 2, 1, tbl, 0, (2,), False, own12, oth12, weights, (), (third0, ret1)
    )
    second2 = over_replica("ring2_1", far2, RING)
    back01 = back("back01", me, (ret0, swap0, ret1, swap1), (far2,))
    with jax.named_scope("rows_back01"):
        rows01 = lax.all_to_all(
            back01, "expert", 0, 0, axis_index_groups=[[0, 2, 4, 6], [1, 3, 5, 7]], tiled=True
        )
    mid2, near2, home2, ret2, swap2 = expert(
        "expert2_rest", 2, 1, tbl, 2, (2, 2, 2), True, own12, oth12, weights, sums, (back01,)
    )
    mid2, swap2, second2, last0, crossed1a = lax.optimization_barrier(
        (mid2, swap2, second2, last0, crossed1a)
    )
    swap2 = over_replica("core_back2", swap2, CORE)
    third = ring_sums(
        "ring_sums_2",
        [((0, 0), (1, 0)), ((0, 1), (1, 1)), ((2, 0), (3, 0))],
        (mid2, second2, mine1[0], crossed1a),
    )
    third = over_replica("ring2_2", third, RING)
    crossed1b = over_replica("cross1b", cross1b, ACROSS)
    back2 = back("back2", me, (ret2, swap2))
    rows2 = [back2[0]] + [to_z("rows_back2", back2[dz], 4 - dz) for dz in range(1, 4)]
    fourth = ring_sums(
        "ring_sums_3",
        [((0, 0), (1, 0)), ((0, 1), (1, 1)), ((2, 0), (3, 1), (1, 2))],
        (near2, third, mine1[1], crossed1a),
    )
    fourth = over_replica("ring2_3", fourth, RING)
    rows01, *rows2 = lax.optimization_barrier((rows01, *rows2))
    last0 = lax.optimization_barrier((last0, fourth))[0]
    scratch = [pltpu.VMEM((4 * LOCAL * CAP, D), BF16)] * 2
    theirs = call(
        partner_kernel, "partner_sums", [SMEM] + [VMEM] * 6, bf16_like(2, TOK, D),
        (me, partner, rows01, *rows2), 3 * 10**6, scratch,
    )
    with jax.named_scope("partner_out"):
        others = lax.ppermute(theirs, "expert", PARTNER)
    across0 = over_replica("across0", add(home0[1], last0[1]), ACROSS)
    crossed1b, last = lax.optimization_barrier((crossed1b, fourth))
    across2 = over_replica("across2", add(home2[1], last[1]), ACROSS)
    ring1 = over_replica("ring1_3", add(mine1[2][0], crossed1b[0], last[2]), RING)
    mixed, token_grad = call(
        combine_kernel, "combine", [SMEM] + [VMEM] * 7, [bf16_like(TOK, D)] * 2,
        (me, packed, others, rows01, *rows2), 3 * 10**6, scratch,
    )
    parts = [add(home0[0], last0[0]), across0]
    parts += [add(mine1[3][0], crossed1b[1]), ring1]
    parts += [add(home2[0], last[0]), across2]
    gate_grad, up_grad, down_grad = call(
        finish_kernel, "finish", [VMEM] * len(parts),
        [bf16_like(LOCAL, D, BLK), bf16_like(LOCAL, D, BLK), bf16_like(LOCAL, BLK, D)],
        parts, 4 * 10**6,
    )
    return mixed, token_grad, gate_grad, up_grad, down_grad


def solution(mesh):
    tokens = P(("expert", "replica"), None)
    return jax.shard_map(
        local,
        mesh=mesh,
        in_specs=(tokens,) * 4 + (P("expert", None, None),) * 3,
        out_specs=(tokens,) * 2
        + (P("expert", None, "replica"), P("expert", None, "replica"), P("expert", "replica", None)),
        check_vma=False,
    )
```

```python
import functools

import jax
import jax.numpy as jnp
from jax import lax
from jax.experimental import pallas as pl
from jax.experimental.pallas import tpu as pltpu
from jax.sharding import PartitionSpec as P

CAP = 48
LOCAL = 3
SOURCES = 8
ROWS = SOURCES * CAP
D = 512
TOK = 256
BLK = 128
META = 16
F32 = jnp.float32
BF16 = jnp.bfloat16
VMEM_LIMIT = 32 * 1024 * 1024
EXPERT_LIMIT = 44 * 1024 * 1024
COST = {
    "ring_sums": 0,
    "partner_sums": 20,
    "expert0_first": 20,
    "expert0_rest": 20,
    "expert1": 20,
    "expert2_first": 4,
    "expert2_rest": 4,
}
VMEM = pl.BlockSpec(memory_space=pltpu.VMEM)
SMEM = pl.BlockSpec(memory_space=pltpu.SMEM)


def dot(a, b, ca=1, cb=0):
    return lax.dot_general(a, b, (((ca,), (cb,)), ((), ())), preferred_element_type=F32)


def bf16_like(*shape):
    return jax.ShapeDtypeStruct(shape, BF16)


def call(kernel, name, in_specs, out_shape, args, nbytes=10**6, scratch=(), limit=VMEM_LIMIT):
    return pl.pallas_call(
        kernel,
        in_specs=in_specs,
        out_specs=jax.tree.map(lambda _: VMEM, out_shape),
        out_shape=out_shape,
        scratch_shapes=list(scratch),
        compiler_params=pltpu.CompilerParams(vmem_limit_bytes=limit),
        cost_estimate=pl.CostEstimate(
            flops=COST.get(name, 0) * 10**9, bytes_accessed=nbytes, transcendentals=0
        ),
        name=name,
    )(*args)


def along_z(dz):
    return [(z * 2 + h, ((z + dz) % 4) * 2 + h) for z in range(4) for h in range(2)]


PARTNER = [(e, e ^ 1) for e in range(8)]
CORE = [(r, r ^ 1) for r in range(16)]
ACROSS = [(r, r ^ 2) for r in range(16)]
RING = [(r, (r + (4 if r % 2 == 0 else 12)) % 16) for r in range(16)]


def pack_kernel(tokens_ref, cot_ref, ids_ref, gates_ref, out_ref, ids_s, gates_s, sems):
    copies = [
        pltpu.make_async_copy(src, dst, sems.at[n])
        for n, (src, dst) in enumerate(
            (
                (ids_ref, ids_s),
                (gates_ref, gates_s),
                (tokens_ref, out_ref.at[pl.ds(0, TOK)]),
                (cot_ref, out_ref.at[pl.ds(TOK, TOK)]),
            )
        )
    ]
    for copy in copies:
        copy.start()
    copies[0].wait()
    copies[1].wait()
    gates = gates_s[...]
    high = gates.astype(BF16).astype(F32)
    middle = (gates - high).astype(BF16).astype(F32)
    low = gates - high - middle
    meta = jnp.concatenate(
        [ids_s[...].astype(F32), high, middle, low, jnp.zeros((META - 8, TOK), F32)], axis=0
    )
    out_ref[2 * TOK :] = jnp.concatenate([meta, jnp.zeros_like(meta)], axis=1).astype(BF16)
    copies[2].wait()
    copies[3].wait()


def read_meta(packed_ref):
    meta = packed_ref[2 * TOK :, 0:TOK].astype(F32)
    gates = meta[2:4] + meta[4:6] + meta[6:8]
    return meta[0:2], gates


def dispatch_kernel(split, me_ref, packed_ref, *out_refs):
    z, h = me_ref[0] >> 1, me_ref[0] & 1
    ids, gates = read_meta(packed_ref)
    count = 4 * LOCAL
    index = lax.broadcasted_iota(jnp.int32, (16, TOK), 0)
    want = (((z + (index & 3)) & 3) * 2 + h) * LOCAL + (index >> 2)
    want = jnp.where(index < count, want, -1).astype(F32)
    hit0 = ids[0:1] == want
    hit1 = ids[1:2] == want
    hit = jnp.where(hit0 | hit1, 1.0, 0.0).astype(F32)
    gate = jnp.where(hit0, gates[0:1], jnp.where(hit1, gates[1:2], 0.0))
    earlier = lax.broadcasted_iota(jnp.int32, (TOK, TOK), 0) < lax.broadcasted_iota(
        jnp.int32, (TOK, TOK), 1
    )
    before = dot(hit.astype(BF16), jnp.where(earlier, 1.0, 0.0).astype(BF16))
    place = jnp.where(hit > 0.0, before, -1.0).astype(jnp.int32)
    slot = lax.broadcasted_iota(jnp.int32, (CAP, TOK), 0)
    for j in range(LOCAL):
        picks, weights = [], []
        for n in range(j * 4, j * 4 + 4):
            sel = slot == place[n : n + 1]
            picks.append(jnp.where(sel, 1.0, 0.0).astype(BF16))
            weights.append(jnp.sum(jnp.where(sel, gate[n : n + 1], 0.0), axis=1, keepdims=True))
        pick = jnp.concatenate(picks, axis=0)
        weight = jnp.concatenate(weights, axis=0)
        rows = dot(pick, packed_ref[0:TOK]).astype(BF16)
        grads = (weight * dot(pick, packed_ref[TOK : 2 * TOK])).astype(BF16)
        for dz in range(4):
            part = slice(dz * CAP, (dz + 1) * CAP)
            ref, at = out_refs[dz], j
            if split:
                ref, at = (out_refs[dz], 0) if j == 0 else (out_refs[4 + dz], j - 1)
            ref[at, 0] = rows[part]
            ref[at, 1] = grads[part]


def dispatch(name, split, me, packed):
    out = [bf16_like(n, 2, CAP, D) for n in ((1, 2) if split else (3,)) for _ in range(4)]
    kernel = functools.partial(dispatch_kernel, split)
    return call(kernel, name, [SMEM, VMEM], out, (me, packed), 3 * 10**6)


def join_kernel(count, *refs):
    ins, out_ref = refs[:SOURCES], refs[-1]
    for n, ref in enumerate(ins):
        skip = ref.shape[0] - count
        for j in range(count):
            out_ref[j, n] = ref[skip + j if count > 1 else 0]


def join(name, count, pieces, after):
    specs = [VMEM] * SOURCES + [pl.BlockSpec(memory_space=pl.ANY)] * len(after)
    out = bf16_like(count, SOURCES, 2, CAP, D)
    return call(functools.partial(join_kernel, count), name, specs, out, (*pieces, *after), 10**6)


def expert_kernel(j, at, base, counts, has_sums, ends, n_after, tbl_ref, own_ref, oth_ref, *refs):
    weights, refs = refs[:3], refs[3:]
    if has_sums:
        sums, refs = refs[:2], refs[2:]
    refs = refs[n_after:]
    chunks, refs = refs[: len(counts)], refs[len(counts) :]
    results, (x_s, g_s, xt_s, gt_s, wg_s, wu_s, wd_s, sems, *acc) = refs[:2], refs[2:]
    eo_s, ig_s = acc if ends else results
    flat = [ref.at[n] for ref, count in zip(chunks, counts) for n in range(count)]
    steps = len(flat) // 2

    def fetch(i):
        slot, copies = i % 2, []
        for k in range(2):
            block = pl.ds(pl.multiple_of(tbl_ref[base + 2 * i + k] * BLK, BLK), BLK)
            here = pl.ds(k * BLK, BLK)
            pairs = (
                (weights[0].at[j, :, block], wg_s.at[slot, :, here]),
                (weights[1].at[j, :, block], wu_s.at[slot, :, here]),
                (weights[2].at[j, block, :], wd_s.at[slot, here, :]),
            )
            for n, (src, dst) in enumerate(pairs):
                copies.append(pltpu.make_async_copy(src, dst, sems.at[slot, 3 * k + n]))
        return copies

    for copy in fetch(0):
        copy.start()
    for k, ref in enumerate((own_ref, oth_ref)):
        x_s[k * ROWS : (k + 1) * ROWS, :] = ref[at, :, 0].reshape(ROWS, D)
        g_s[k * ROWS : (k + 1) * ROWS, :] = ref[at, :, 1].reshape(ROWS, D)
    xt_s[...] = x_s[...].T
    gt_s[...] = g_s[...].T
    for i in range(steps):
        if i + 1 < steps:
            for copy in fetch(i + 1):
                copy.start()
        for copy in fetch(i):
            copy.wait()
        wg, wu, wd = wg_s[i % 2], wu_s[i % 2], wd_s[i % 2]
        acts = []
        for half in range(2):
            part = slice(half * ROWS, (half + 1) * ROWS)
            x, g = x_s[part], g_s[part]
            pre_gate = dot(x, wg)
            pre_up = dot(x, wu)
            grad_hidden = dot(g, wd, 1, 1)
            sig = jax.nn.sigmoid(pre_gate)
            silu = pre_gate * sig
            hidden = (silu * pre_up).astype(BF16)
            grad_gate = (grad_hidden * pre_up * sig * (1.0 + pre_gate * (1.0 - sig))).astype(BF16)
            grad_up = (grad_hidden * silu).astype(BF16)
            acts.append((grad_gate, grad_up, hidden))
            out_rows = dot(hidden, wd)
            in_rows = dot(grad_gate, wg, 1, 1) + dot(grad_up, wu, 1, 1)
            if i > 0 or has_sums:
                before = (eo_s, ig_s) if i > 0 else sums
                out_rows = before[0][part] + out_rows
                in_rows = before[1][part] + in_rows
            eo_s[part] = out_rows
            ig_s[part] = in_rows
        for k, rows_t in enumerate((xt_s, xt_s, gt_s)):
            act = jnp.concatenate([acts[0][k], acts[1][k]], axis=0)
            grad = dot(rows_t[...], act).astype(BF16)
            for lane in range(2):
                flat[2 * i + lane][k * D : (k + 1) * D, :] = grad[:, lane * BLK : (lane + 1) * BLK]
    if ends:
        for k, ref in enumerate(results):
            ref[0] = eo_s[k * ROWS : (k + 1) * ROWS, :].astype(BF16)
            ref[1] = ig_s[k * ROWS : (k + 1) * ROWS, :].astype(BF16)


def expert(name, j, at, tbl, base, counts, ends, own, oth, weights, sums=(), after=()):
    rows = 2 * ROWS
    out = [bf16_like(count, 3 * D, BLK) for count in counts]
    scratch = [pltpu.VMEM((rows, D), BF16)] * 2 + [pltpu.VMEM((D, rows), BF16)] * 2
    scratch += [pltpu.VMEM((2, D, 2 * BLK), BF16)] * 2 + [pltpu.VMEM((2, 2 * BLK, D), BF16)]
    scratch += [pltpu.SemaphoreType.DMA((2, 6))]
    if ends:
        out += [bf16_like(2, ROWS, D)] * 2
        scratch += [pltpu.VMEM((rows, D), F32)] * 2
    else:
        out += [jax.ShapeDtypeStruct((rows, D), F32)] * 2
    anywhere = pl.BlockSpec(memory_space=pl.ANY)
    kernel = functools.partial(
        expert_kernel, j, at, base, counts, bool(sums), ends, len(after)
    )
    return pl.pallas_call(
        kernel,
        in_specs=[SMEM, VMEM, VMEM] + [anywhere] * 3 + [VMEM] * len(sums) + [anywhere] * len(after),
        out_specs=[VMEM] * len(out),
        scratch_shapes=scratch,
        out_shape=out,
        compiler_params=pltpu.CompilerParams(vmem_limit_bytes=EXPERT_LIMIT),
        cost_estimate=pl.CostEstimate(
            flops=COST[name] * 10**9, bytes_accessed=10**6, transcendentals=0
        ),
        name=name,
    )(tbl, own, oth, *weights, *sums, *after)


def sums_kernel(terms, *refs):
    out_ref = refs[-1]
    for n, pairs in enumerate(terms):
        total = refs[pairs[0][0]][pairs[0][1]].astype(F32)
        for ref, index in pairs[1:]:
            total = total + refs[ref][index].astype(F32)
        out_ref[n] = total.astype(BF16)


def ring_sums(name, terms, args):
    out = bf16_like(len(terms), 3 * D, BLK)
    return call(functools.partial(sums_kernel, terms), name, [VMEM] * len(args), out, args, 3 * 10**6)


def back_kernel(count, n_after, *refs):
    ins, outs = refs[: 2 * count], refs[2 * count + n_after :]
    for n in range(SOURCES):
        for j in range(count):
            for k in range(2):
                rows = slice(n * CAP, (n + 1) * CAP)
                total = ins[2 * j][k, rows].astype(F32) + ins[2 * j + 1][k, rows].astype(F32)
                outs[n & 3][j, n >> 2, k] = total.astype(BF16)


def back(name, pairs, after=()):
    count = len(pairs) // 2
    out = [bf16_like(count, 2, 2, CAP, D)] * 4
    specs = [VMEM] * len(pairs) + [pl.BlockSpec(memory_space=pl.ANY)] * len(after)
    return call(functools.partial(back_kernel, count, len(after)), name, specs, out, (*pairs, *after))


def token_sums(side, me_ref, packed_ref, rows, out_s, in_s):
    z, h = me_ref[0] >> 1, me_ref[0] & 1
    for dz in range(4):
        for j in range(LOCAL):
            n = j * 4 + dz
            ref, at = (rows[dz], 0) if j == 0 else (rows[4 + dz], j - 1)
            for k, dst in enumerate((out_s, in_s)):
                dst[n * CAP : (n + 1) * CAP, :] = ref[at, side, k]
    ids, gates = read_meta(packed_ref)
    columns = jnp.concatenate([ids, gates, jnp.zeros((4, TOK), F32)], axis=0).T
    lane = lax.broadcasted_iota(jnp.int32, (TOK, 128), 1)
    want = (((z + (lane & 3)) & 3) * 2 + h) * LOCAL + (lane >> 2)
    want = jnp.where(lane < 4 * LOCAL, want, -1).astype(F32)
    hits = [columns[:, k : k + 1] == want for k in range(2)]
    either = jnp.where(hits[0] | hits[1], 1.0, 0.0).astype(BF16)
    earlier = lax.broadcasted_iota(jnp.int32, (TOK, TOK), 1) < lax.broadcasted_iota(
        jnp.int32, (TOK, TOK), 0
    )
    before = dot(jnp.where(earlier, 1.0, 0.0).astype(BF16), either)
    code = before + (lane * CAP + 1).astype(F32)
    slots = lax.broadcasted_iota(jnp.int32, (TOK, 4 * LOCAL * CAP), 1)
    picks = []
    for k in range(2):
        slot = jnp.sum(jnp.where(hits[k], code, 0.0), axis=1, keepdims=True).astype(jnp.int32) - 1
        picks.append(jnp.where(slots == slot, 1.0, 0.0).astype(BF16))
    mixed = columns[:, 2:3] * dot(picks[0], out_s[...]) + columns[:, 3:4] * dot(picks[1], out_s[...])
    return mixed, dot(picks[0] + picks[1], in_s[...])


def partner_kernel(me_ref, packed_ref, *refs):
    rows, (out_ref, out_s, in_s) = refs[:-3], refs[-3:]
    mixed, grad = token_sums(1, me_ref, packed_ref, rows, out_s, in_s)
    out_ref[0] = mixed.astype(BF16)
    out_ref[1] = grad.astype(BF16)


def combine_kernel(me_ref, packed_ref, other_ref, *refs):
    rows, (mixed_ref, grad_ref, out_s, in_s) = refs[:-4], refs[-4:]
    mixed, grad = token_sums(0, me_ref, packed_ref, rows, out_s, in_s)
    mixed_ref[...] = (mixed + other_ref[0].astype(F32)).astype(BF16)
    grad_ref[...] = (grad + other_ref[1].astype(F32)).astype(BF16)


def finish_kernel(*refs):
    ins, outs = refs[: 2 * LOCAL], refs[2 * LOCAL :]
    for j in range(LOCAL):
        total = (ins[2 * j][...].astype(F32) + ins[2 * j + 1][...].astype(F32)).astype(BF16)
        outs[0][j] = total[0:D]
        outs[1][j] = total[D : 2 * D]
        outs[2][j] = total[2 * D :].T


def add(*terms):
    return functools.reduce(lambda a, b: a + b, [t.astype(F32) for t in terms]).astype(BF16)


def local(tokens, expert_ids, gates, cotangent, w_gate, w_up, w_down):
    me = lax.axis_index("expert").astype(jnp.int32).reshape(1)
    rep = lax.axis_index("replica").astype(jnp.int32)
    y, x, core = rep >> 2, (rep >> 1) & 1, rep & 1
    step = jnp.arange(16, dtype=jnp.int32)
    hop = jnp.where(step < 8, step >> 1, step & 3)
    flip = jnp.where(step < 8, step & 1, (step < 12).astype(jnp.int32))
    tbl = ((y + (3 - hop) * (1 - 2 * core)) & 3) * 4 + (x ^ flip) * 2 + core

    def over_replica(label, value, perm):
        with jax.named_scope(label):
            return lax.ppermute(value, "replica", perm)

    def to_z(label, value, dz):
        with jax.named_scope(label):
            return lax.ppermute(value, "expert", along_z(dz))

    packed = call(
        pack_kernel,
        "pack",
        [pl.BlockSpec(memory_space=pltpu.HBM)] * 4,
        bf16_like(2 * TOK + META, D),
        (tokens, cotangent, expert_ids.T, gates.T),
        scratch=[
            pltpu.VMEM((2, TOK), jnp.int32),
            pltpu.VMEM((2, TOK), F32),
            pltpu.SemaphoreType.DMA((4,)),
        ],
        limit=63 * 1024 * 1024,
    )
    with jax.named_scope("packed"):
        partner = lax.ppermute(packed, "expert", PARTNER)
    sent = dispatch("own_slots", False, me, packed)
    from_own = [sent[0]] + [to_z("own_rows", sent[dz], dz) for dz in range(1, 4)]
    sent = dispatch("partner_slots", True, me, partner)
    firsts = [sent[0]] + [to_z("partner_rows0", sent[dz], dz) for dz in range(1, 4)]
    rests = [sent[4]] + [to_z("partner_rows12", sent[4 + dz], dz) for dz in range(1, 4)]

    weights = (w_gate, w_up, w_down)
    own0 = join("join0", 1, from_own + firsts, ())
    oth0 = over_replica("core_rows0", own0, CORE)
    far0, *sums = expert("expert0_first", 0, 0, tbl, 0, (2,), False, own0, oth0, weights)
    second0 = over_replica("ring0_1", far0, RING)
    own12 = join("join12", 2, from_own + rests, (far0,))
    oth12 = over_replica("core_rows12", own12, CORE)
    mid0, near0, home0, ret0, swap0 = expert(
        "expert0_rest", 0, 0, tbl, 2, (2, 2, 2), True, own0, oth0, weights, sums, (own12,)
    )
    mid0, swap0, second0 = lax.optimization_barrier((mid0, swap0, second0))
    second0 = add(mid0, second0)
    third0 = over_replica("ring0_2", second0, RING)
    swap0 = over_replica("core_back0", swap0, CORE)
    cross1, *mine1, ret1, swap1 = expert(
        "expert1", 1, 0, tbl, 8, (4, 1, 1, 1, 1), True, own12, oth12, weights, (), (second0,)
    )
    cross1, swap1, third0 = lax.optimization_barrier((cross1, swap1, third0))
    third0 = add(near0, third0)
    last0 = over_replica("ring0_3", third0, RING)
    crossed1 = over_replica("cross1", cross1, ACROSS)
    swap1 = over_replica("core_back1", swap1, CORE)
    far2, *sums = expert(
        "expert2_first", 2, 1, tbl, 0, (2,), False, own12, oth12, weights, (), (third0, ret1)
    )
    second2 = over_replica("ring2_1", far2, RING)
    back0 = back("back0", (ret0, swap0), (far2,))
    rows0 = [back0[0]] + [to_z("rows_back0", back0[dz], 4 - dz) for dz in range(1, 4)]
    across0 = add(home0[1], last0[1])
    mid2, near2, home2, ret2, swap2 = expert(
        "expert2_rest", 2, 1, tbl, 2, (2, 2, 2), True, own12, oth12, weights, sums,
        (back0[0], across0),
    )
    mid2, swap2, second2, *rows0 = lax.optimization_barrier((mid2, swap2, second2, *rows0))
    swap2 = over_replica("core_back2", swap2, CORE)
    third2 = over_replica("ring2_2", add(mid2, second2), RING)
    back12 = back("back12", (ret1, swap1, ret2, swap2))
    rows12 = [back12[0]] + [to_z("rows_back12", back12[dz], 4 - dz) for dz in range(1, 4)]
    third2, crossed1, across0, _ = lax.optimization_barrier((third2, crossed1, across0, back12[0]))
    third = ring_sums(
        "ring_sums",
        [((0, 0), (1, 0)), ((0, 1), (1, 1)), ((2, 0), (3, 0))],
        (near2, third2, mine1[0], crossed1),
    )
    third = over_replica("ring2_3", third, RING)
    across0 = over_replica("across0", across0, ACROSS)
    rows = rows0 + rows12
    scratch = [pltpu.VMEM((4 * LOCAL * CAP, D), BF16)] * 2
    theirs = call(
        partner_kernel, "partner_sums", [SMEM] + [VMEM] * 9, bf16_like(2, TOK, D),
        (me, partner, *rows), 3 * 10**6, scratch,
    )
    third, _ = lax.optimization_barrier((third, theirs))
    with jax.named_scope("partner_out"):
        others = lax.ppermute(theirs, "expert", PARTNER)
    across2 = over_replica("across2", add(home2[1], third[1]), ACROSS)
    ring1 = over_replica("ring1_2", add(mine1[1][0], crossed1[1], third[2]), RING)
    ring1 = over_replica("ring1_3", add(mine1[2][0], crossed1[2], ring1), RING)
    mixed, token_grad = call(
        combine_kernel, "combine", [SMEM] + [VMEM] * 10, [bf16_like(TOK, D)] * 2,
        (me, packed, others, *rows), 3 * 10**6, scratch,
    )
    parts = [add(home0[0], last0[0]), across0]
    parts += [add(mine1[3][0], crossed1[3]), ring1]
    parts += [add(home2[0], third[0]), across2]
    gate_grad, up_grad, down_grad = call(
        finish_kernel, "finish", [VMEM] * len(parts),
        [bf16_like(LOCAL, D, BLK), bf16_like(LOCAL, D, BLK), bf16_like(LOCAL, BLK, D)],
        parts, 4 * 10**6,
    )
    return mixed, token_grad, gate_grad, up_grad, down_grad


def solution(mesh):
    tokens = P(("expert", "replica"), None)
    return jax.shard_map(
        local,
        mesh=mesh,
        in_specs=(tokens,) * 4 + (P("expert", None, None),) * 3,
        out_specs=(tokens,) * 2
        + (P("expert", None, "replica"), P("expert", None, "replica"), P("expert", "replica", None)),
        check_vma=False,
    )
```

```python
import functools

import jax
import jax.numpy as jnp
from jax import lax
from jax.experimental import pallas as pl
from jax.experimental.pallas import tpu as pltpu
from jax.sharding import PartitionSpec as P

CAP = 48
LOCAL = 3
SOURCES = 8
ROWS = SOURCES * CAP
D = 512
TOK = 256
BLK = 128
META = 16
F32 = jnp.float32
BF16 = jnp.bfloat16
VMEM_LIMIT = 32 * 1024 * 1024
EXPERT_LIMIT = 44 * 1024 * 1024
COST = {
    "ring_sums": 0,
    "partner_sums": 20,
    "own_sums": 20,
    "expert0_first": 20,
    "expert0_rest": 20,
    "expert1": 20,
    "expert2_first": 4,
    "expert2_rest": 4,
}
VMEM = pl.BlockSpec(memory_space=pltpu.VMEM)
SMEM = pl.BlockSpec(memory_space=pltpu.SMEM)


def dot(a, b, ca=1, cb=0):
    return lax.dot_general(a, b, (((ca,), (cb,)), ((), ())), preferred_element_type=F32)


def bf16_like(*shape):
    return jax.ShapeDtypeStruct(shape, BF16)


def call(kernel, name, in_specs, out_shape, args, nbytes=10**6, scratch=(), limit=VMEM_LIMIT):
    return pl.pallas_call(
        kernel,
        in_specs=in_specs,
        out_specs=jax.tree.map(lambda _: VMEM, out_shape),
        out_shape=out_shape,
        scratch_shapes=list(scratch),
        compiler_params=pltpu.CompilerParams(vmem_limit_bytes=limit),
        cost_estimate=pl.CostEstimate(
            flops=COST.get(name, 0) * 10**9, bytes_accessed=nbytes, transcendentals=0
        ),
        name=name,
    )(*args)


def along_z(dz):
    return [(z * 2 + h, ((z + dz) % 4) * 2 + h) for z in range(4) for h in range(2)]


PARTNER = [(e, e ^ 1) for e in range(8)]
CORE = [(r, r ^ 1) for r in range(16)]
ACROSS = [(r, r ^ 2) for r in range(16)]
RING = [(r, (r + (4 if r % 2 == 0 else 12)) % 16) for r in range(16)]


def pack_kernel(tokens_ref, cot_ref, ids_ref, gates_ref, out_ref, ids_s, gates_s, sems):
    copies = [
        pltpu.make_async_copy(src, dst, sems.at[n])
        for n, (src, dst) in enumerate(
            (
                (ids_ref, ids_s),
                (gates_ref, gates_s),
                (tokens_ref, out_ref.at[pl.ds(0, TOK)]),
                (cot_ref, out_ref.at[pl.ds(TOK, TOK)]),
            )
        )
    ]
    for copy in copies:
        copy.start()
    copies[0].wait()
    copies[1].wait()
    gates = gates_s[...]
    high = gates.astype(BF16).astype(F32)
    middle = (gates - high).astype(BF16).astype(F32)
    low = gates - high - middle
    meta = jnp.concatenate(
        [ids_s[...].astype(F32), high, middle, low, jnp.zeros((META - 8, TOK), F32)], axis=0
    )
    out_ref[2 * TOK :] = jnp.concatenate([meta, jnp.zeros_like(meta)], axis=1).astype(BF16)
    copies[2].wait()
    copies[3].wait()


def read_meta(packed_ref):
    meta = packed_ref[2 * TOK :, 0:TOK].astype(F32)
    gates = meta[2:4] + meta[4:6] + meta[6:8]
    return meta[0:2], gates


def dispatch_kernel(split, me_ref, packed_ref, *out_refs):
    z, h = me_ref[0] >> 1, me_ref[0] & 1
    ids, gates = read_meta(packed_ref)
    count = 4 * LOCAL
    index = lax.broadcasted_iota(jnp.int32, (16, TOK), 0)
    want = (((z + (index & 3)) & 3) * 2 + h) * LOCAL + (index >> 2)
    want = jnp.where(index < count, want, -1).astype(F32)
    hit0 = ids[0:1] == want
    hit1 = ids[1:2] == want
    hit = jnp.where(hit0 | hit1, 1.0, 0.0).astype(F32)
    gate = jnp.where(hit0, gates[0:1], jnp.where(hit1, gates[1:2], 0.0))
    earlier = lax.broadcasted_iota(jnp.int32, (TOK, TOK), 0) < lax.broadcasted_iota(
        jnp.int32, (TOK, TOK), 1
    )
    before = dot(hit.astype(BF16), jnp.where(earlier, 1.0, 0.0).astype(BF16))
    place = jnp.where(hit > 0.0, before, -1.0).astype(jnp.int32)
    slot = lax.broadcasted_iota(jnp.int32, (CAP, TOK), 0)
    for j in range(LOCAL):
        picks, weights = [], []
        for n in range(j * 4, j * 4 + 4):
            sel = slot == place[n : n + 1]
            picks.append(jnp.where(sel, 1.0, 0.0).astype(BF16))
            weights.append(jnp.sum(jnp.where(sel, gate[n : n + 1], 0.0), axis=1, keepdims=True))
        pick = jnp.concatenate(picks, axis=0)
        weight = jnp.concatenate(weights, axis=0)
        rows = dot(pick, packed_ref[0:TOK]).astype(BF16)
        grads = (weight * dot(pick, packed_ref[TOK : 2 * TOK])).astype(BF16)
        for dz in range(4):
            part = slice(dz * CAP, (dz + 1) * CAP)
            ref, at = out_refs[dz], j
            if split:
                ref, at = (out_refs[dz], 0) if j == 0 else (out_refs[4 + dz], j - 1)
            ref[at, 0] = rows[part]
            ref[at, 1] = grads[part]


def dispatch(name, split, me, packed):
    out = [bf16_like(n, 2, CAP, D) for n in ((1, 2) if split else (3,)) for _ in range(4)]
    kernel = functools.partial(dispatch_kernel, split)
    return call(kernel, name, [SMEM, VMEM], out, (me, packed), 3 * 10**6)


def join_kernel(count, *refs):
    ins, out_ref = refs[:SOURCES], refs[-1]
    for n, ref in enumerate(ins):
        skip = ref.shape[0] - count
        for j in range(count):
            out_ref[j, n] = ref[skip + j if count > 1 else 0]


def join(name, count, pieces, after):
    specs = [VMEM] * SOURCES + [pl.BlockSpec(memory_space=pl.ANY)] * len(after)
    out = bf16_like(count, SOURCES, 2, CAP, D)
    return call(functools.partial(join_kernel, count), name, specs, out, (*pieces, *after), 10**6)


def expert_kernel(j, at, base, counts, has_sums, ends, n_after, tbl_ref, own_ref, oth_ref, *refs):
    weights, refs = refs[:3], refs[3:]
    if has_sums:
        sums, refs = refs[:2], refs[2:]
    refs = refs[n_after:]
    chunks, refs = refs[: len(counts)], refs[len(counts) :]
    results, (x_s, g_s, xt_s, gt_s, wg_s, wu_s, wd_s, sems, *acc) = refs[:2], refs[2:]
    eo_s, ig_s = acc if ends else results
    flat = [ref.at[n] for ref, count in zip(chunks, counts) for n in range(count)]
    steps = len(flat) // 2

    def fetch(i):
        slot, copies = i % 2, []
        for k in range(2):
            block = pl.ds(pl.multiple_of(tbl_ref[base + 2 * i + k] * BLK, BLK), BLK)
            here = pl.ds(k * BLK, BLK)
            pairs = (
                (weights[0].at[j, :, block], wg_s.at[slot, :, here]),
                (weights[1].at[j, :, block], wu_s.at[slot, :, here]),
                (weights[2].at[j, block, :], wd_s.at[slot, here, :]),
            )
            for n, (src, dst) in enumerate(pairs):
                copies.append(pltpu.make_async_copy(src, dst, sems.at[slot, 3 * k + n]))
        return copies

    for copy in fetch(0):
        copy.start()
    for k, ref in enumerate((own_ref, oth_ref)):
        x_s[k * ROWS : (k + 1) * ROWS, :] = ref[at, :, 0].reshape(ROWS, D)
        g_s[k * ROWS : (k + 1) * ROWS, :] = ref[at, :, 1].reshape(ROWS, D)
    xt_s[...] = x_s[...].T
    gt_s[...] = g_s[...].T
    for i in range(steps):
        if i + 1 < steps:
            for copy in fetch(i + 1):
                copy.start()
        for copy in fetch(i):
            copy.wait()
        wg, wu, wd = wg_s[i % 2], wu_s[i % 2], wd_s[i % 2]
        acts = []
        for half in range(2):
            part = slice(half * ROWS, (half + 1) * ROWS)
            x, g = x_s[part], g_s[part]
            pre_gate = dot(x, wg)
            pre_up = dot(x, wu)
            grad_hidden = dot(g, wd, 1, 1)
            sig = jax.nn.sigmoid(pre_gate)
            silu = pre_gate * sig
            hidden = (silu * pre_up).astype(BF16)
            grad_gate = (grad_hidden * pre_up * sig * (1.0 + pre_gate * (1.0 - sig))).astype(BF16)
            grad_up = (grad_hidden * silu).astype(BF16)
            acts.append((grad_gate, grad_up, hidden))
            out_rows = dot(hidden, wd)
            in_rows = dot(grad_gate, wg, 1, 1) + dot(grad_up, wu, 1, 1)
            if i > 0 or has_sums:
                before = (eo_s, ig_s) if i > 0 else sums
                out_rows = before[0][part] + out_rows
                in_rows = before[1][part] + in_rows
            eo_s[part] = out_rows
            ig_s[part] = in_rows
        for k, rows_t in enumerate((xt_s, xt_s, gt_s)):
            act = jnp.concatenate([acts[0][k], acts[1][k]], axis=0)
            grad = dot(rows_t[...], act).astype(BF16)
            for lane in range(2):
                flat[2 * i + lane][k * D : (k + 1) * D, :] = grad[:, lane * BLK : (lane + 1) * BLK]
    if ends:
        for k, ref in enumerate(results):
            ref[0] = eo_s[k * ROWS : (k + 1) * ROWS, :].astype(BF16)
            ref[1] = ig_s[k * ROWS : (k + 1) * ROWS, :].astype(BF16)


def expert(name, j, at, tbl, base, counts, ends, own, oth, weights, sums=(), after=()):
    rows = 2 * ROWS
    out = [bf16_like(count, 3 * D, BLK) for count in counts]
    scratch = [pltpu.VMEM((rows, D), BF16)] * 2 + [pltpu.VMEM((D, rows), BF16)] * 2
    scratch += [pltpu.VMEM((2, D, 2 * BLK), BF16)] * 2 + [pltpu.VMEM((2, 2 * BLK, D), BF16)]
    scratch += [pltpu.SemaphoreType.DMA((2, 6))]
    if ends:
        out += [bf16_like(2, ROWS, D)] * 2
        scratch += [pltpu.VMEM((rows, D), F32)] * 2
    else:
        out += [jax.ShapeDtypeStruct((rows, D), F32)] * 2
    anywhere = pl.BlockSpec(memory_space=pl.ANY)
    kernel = functools.partial(
        expert_kernel, j, at, base, counts, bool(sums), ends, len(after)
    )
    return pl.pallas_call(
        kernel,
        in_specs=[SMEM, VMEM, VMEM] + [anywhere] * 3 + [VMEM] * len(sums) + [anywhere] * len(after),
        out_specs=[VMEM] * len(out),
        scratch_shapes=scratch,
        out_shape=out,
        compiler_params=pltpu.CompilerParams(vmem_limit_bytes=EXPERT_LIMIT),
        cost_estimate=pl.CostEstimate(
            flops=COST[name] * 10**9, bytes_accessed=10**6, transcendentals=0
        ),
        name=name,
    )(tbl, own, oth, *weights, *sums, *after)


def sums_kernel(terms, *refs):
    out_ref = refs[-1]
    for n, pairs in enumerate(terms):
        total = refs[pairs[0][0]][pairs[0][1]].astype(F32)
        for ref, index in pairs[1:]:
            total = total + refs[ref][index].astype(F32)
        out_ref[n] = total.astype(BF16)


def ring_sums(name, terms, args):
    out = bf16_like(len(terms), 3 * D, BLK)
    return call(functools.partial(sums_kernel, terms), name, [VMEM] * len(args), out, args, 3 * 10**6)


def back_kernel(count, n_after, *refs):
    ins, outs = refs[: 2 * count], refs[2 * count + n_after :]
    for n in range(SOURCES):
        for j in range(count):
            for k in range(2):
                rows = slice(n * CAP, (n + 1) * CAP)
                total = ins[2 * j][k, rows].astype(F32) + ins[2 * j + 1][k, rows].astype(F32)
                outs[n & 3][j, n >> 2, k] = total.astype(BF16)


def back(name, pairs, after=()):
    count = len(pairs) // 2
    out = [bf16_like(count, 2, 2, CAP, D)] * 4
    specs = [VMEM] * len(pairs) + [pl.BlockSpec(memory_space=pl.ANY)] * len(after)
    return call(functools.partial(back_kernel, count, len(after)), name, specs, out, (*pairs, *after))


def token_sums(side, me_ref, packed_ref, rows, out_s, in_s):
    z, h = me_ref[0] >> 1, me_ref[0] & 1
    for dz in range(4):
        for j in range(LOCAL):
            n = j * 4 + dz
            ref, at = (rows[dz], 0) if j == 0 else (rows[4 + dz], j - 1)
            for k, dst in enumerate((out_s, in_s)):
                dst[n * CAP : (n + 1) * CAP, :] = ref[at, side, k]
    ids, gates = read_meta(packed_ref)
    columns = jnp.concatenate([ids, gates, jnp.zeros((4, TOK), F32)], axis=0).T
    lane = lax.broadcasted_iota(jnp.int32, (TOK, 128), 1)
    want = (((z + (lane & 3)) & 3) * 2 + h) * LOCAL + (lane >> 2)
    want = jnp.where(lane < 4 * LOCAL, want, -1).astype(F32)
    hits = [columns[:, k : k + 1] == want for k in range(2)]
    either = jnp.where(hits[0] | hits[1], 1.0, 0.0).astype(BF16)
    earlier = lax.broadcasted_iota(jnp.int32, (TOK, TOK), 1) < lax.broadcasted_iota(
        jnp.int32, (TOK, TOK), 0
    )
    before = dot(jnp.where(earlier, 1.0, 0.0).astype(BF16), either)
    code = before + (lane * CAP + 1).astype(F32)
    slots = lax.broadcasted_iota(jnp.int32, (TOK, 4 * LOCAL * CAP), 1)
    picks = []
    for k in range(2):
        slot = jnp.sum(jnp.where(hits[k], code, 0.0), axis=1, keepdims=True).astype(jnp.int32) - 1
        picks.append(jnp.where(slots == slot, 1.0, 0.0).astype(BF16))
    mixed = columns[:, 2:3] * dot(picks[0], out_s[...]) + columns[:, 3:4] * dot(picks[1], out_s[...])
    return mixed, dot(picks[0] + picks[1], in_s[...])


def sides_kernel(side, me_ref, packed_ref, *refs):
    rows, (out_ref, out_s, in_s) = refs[:8], refs[-3:]
    mixed, grad = token_sums(side, me_ref, packed_ref, rows, out_s, in_s)
    out_ref[0] = mixed.astype(out_ref.dtype)
    out_ref[1] = grad.astype(out_ref.dtype)


def token_outputs(name, side, dtype, me, packed, rows, after=()):
    specs = [SMEM] + [VMEM] * 9 + [pl.BlockSpec(memory_space=pl.ANY)] * len(after)
    out = jax.ShapeDtypeStruct((2, TOK, D), dtype)
    scratch = [pltpu.VMEM((4 * LOCAL * CAP, D), BF16)] * 2
    kernel = functools.partial(sides_kernel, side)
    return call(kernel, name, specs, out, (me, packed, *rows, *after), 3 * 10**6, scratch)


def finish_kernel(*refs):
    ins, outs = refs[: 2 * LOCAL], refs[2 * LOCAL :]
    for j in range(LOCAL):
        total = (ins[2 * j][...].astype(F32) + ins[2 * j + 1][...].astype(F32)).astype(BF16)
        outs[0][j] = total[0:D]
        outs[1][j] = total[D : 2 * D]
        outs[2][j] = total[2 * D :].T


def add(*terms):
    return functools.reduce(lambda a, b: a + b, [t.astype(F32) for t in terms]).astype(BF16)


def local(tokens, expert_ids, gates, cotangent, w_gate, w_up, w_down):
    me = lax.axis_index("expert").astype(jnp.int32).reshape(1)
    rep = lax.axis_index("replica").astype(jnp.int32)
    y, x, core = rep >> 2, (rep >> 1) & 1, rep & 1
    step = jnp.arange(16, dtype=jnp.int32)
    hop = jnp.where(step < 8, step >> 1, step & 3)
    flip = jnp.where(step < 8, step & 1, (step < 12).astype(jnp.int32))
    tbl = ((y + (3 - hop) * (1 - 2 * core)) & 3) * 4 + (x ^ flip) * 2 + core

    def over_replica(label, value, perm):
        with jax.named_scope(label):
            return lax.ppermute(value, "replica", perm)

    def to_z(label, value, dz):
        with jax.named_scope(label):
            return lax.ppermute(value, "expert", along_z(dz))

    packed = call(
        pack_kernel,
        "pack",
        [pl.BlockSpec(memory_space=pltpu.HBM)] * 4,
        bf16_like(2 * TOK + META, D),
        (tokens, cotangent, expert_ids.T, gates.T),
        scratch=[
            pltpu.VMEM((2, TOK), jnp.int32),
            pltpu.VMEM((2, TOK), F32),
            pltpu.SemaphoreType.DMA((4,)),
        ],
        limit=65000 * 1024,
    )
    with jax.named_scope("packed"):
        partner = lax.ppermute(packed, "expert", PARTNER)
    sent = dispatch("own_slots", False, me, packed)
    from_own = [sent[0]] + [to_z("own_rows", sent[dz], dz) for dz in range(1, 4)]
    sent = dispatch("partner_slots", True, me, partner)
    firsts = [sent[0]] + [to_z("partner_rows0", sent[dz], dz) for dz in range(1, 4)]
    rests = [sent[4]] + [to_z("partner_rows12", sent[4 + dz], dz) for dz in range(1, 4)]

    weights = (w_gate, w_up, w_down)
    own0 = join("join0", 1, from_own + firsts, ())
    oth0 = over_replica("core_rows0", own0, CORE)
    far0, *sums = expert("expert0_first", 0, 0, tbl, 0, (2,), False, own0, oth0, weights)
    second0 = over_replica("ring0_1", far0, RING)
    own12 = join("join12", 2, from_own + rests, (far0,))
    oth12 = over_replica("core_rows12", own12, CORE)
    mid0, near0, home0, ret0, swap0 = expert(
        "expert0_rest", 0, 0, tbl, 2, (2, 2, 2), True, own0, oth0, weights, sums, (own12,)
    )
    mid0, swap0, second0 = lax.optimization_barrier((mid0, swap0, second0))
    second0 = add(mid0, second0)
    third0 = over_replica("ring0_2", second0, RING)
    swap0 = over_replica("core_back0", swap0, CORE)
    cross1, *mine1, ret1, swap1 = expert(
        "expert1", 1, 0, tbl, 8, (4, 1, 1, 1, 1), True, own12, oth12, weights, (), (second0,)
    )
    cross1, swap1, third0 = lax.optimization_barrier((cross1, swap1, third0))
    third0 = add(near0, third0)
    last0 = over_replica("ring0_3", third0, RING)
    crossed1 = over_replica("cross1", cross1, ACROSS)
    swap1 = over_replica("core_back1", swap1, CORE)
    far2, *sums = expert(
        "expert2_first", 2, 1, tbl, 0, (2,), False, own12, oth12, weights, (), (third0, ret1)
    )
    second2 = over_replica("ring2_1", far2, RING)
    back0 = back("back0", (ret0, swap0), (far2,))
    rows0 = [back0[0]] + [to_z("rows_back0", back0[dz], 4 - dz) for dz in range(1, 4)]
    across0 = add(home0[1], last0[1])
    mid2, near2, home2, ret2, swap2 = expert(
        "expert2_rest", 2, 1, tbl, 2, (2, 2, 2), True, own12, oth12, weights, sums,
        (back0[0], across0),
    )
    mid2, swap2, second2, *rows0 = lax.optimization_barrier((mid2, swap2, second2, *rows0))
    swap2 = over_replica("core_back2", swap2, CORE)
    third2 = over_replica("ring2_2", add(mid2, second2), RING)
    back12 = back("back12", (ret1, swap1, ret2, swap2))
    rows12 = [back12[0]] + [to_z("rows_back12", back12[dz], 4 - dz) for dz in range(1, 4)]
    third2, crossed1, across0, _ = lax.optimization_barrier((third2, crossed1, across0, back12[0]))
    third = ring_sums(
        "ring_sums",
        [((0, 0), (1, 0)), ((0, 1), (1, 1)), ((2, 0), (3, 0))],
        (near2, third2, mine1[0], crossed1),
    )
    third = over_replica("ring2_3", third, RING)
    across0 = over_replica("across0", across0, ACROSS)
    rows = rows0 + rows12
    theirs = token_outputs("partner_sums", 1, BF16, me, partner, rows)
    with jax.named_scope("partner_out"):
        others = lax.ppermute(theirs, "expert", PARTNER)
    mine = token_outputs("own_sums", 0, F32, me, packed, rows, (theirs,))
    third, across0, mine = lax.optimization_barrier((third, across0, mine))
    across2 = over_replica("across2", add(home2[1], third[1]), ACROSS)
    ring1 = over_replica("ring1_2", add(mine1[1][0], crossed1[1], third[2]), RING)
    ring1, others = lax.optimization_barrier((ring1, others))
    ring1 = over_replica("ring1_3", add(mine1[2][0], crossed1[2], ring1), RING)
    mixed, token_grad = add(mine[0], others[0]), add(mine[1], others[1])
    parts = [add(home0[0], last0[0]), across0]
    parts += [add(mine1[3][0], crossed1[3]), ring1]
    parts += [add(home2[0], third[0]), across2]
    gate_grad, up_grad, down_grad = call(
        finish_kernel, "finish", [VMEM] * len(parts),
        [bf16_like(LOCAL, D, BLK), bf16_like(LOCAL, D, BLK), bf16_like(LOCAL, BLK, D)],
        parts, 4 * 10**6,
    )
    return mixed, token_grad, gate_grad, up_grad, down_grad


def solution(mesh):
    tokens = P(("expert", "replica"), None)
    return jax.shard_map(
        local,
        mesh=mesh,
        in_specs=(tokens,) * 4 + (P("expert", None, None),) * 3,
        out_specs=(tokens,) * 2
        + (P("expert", None, "replica"), P("expert", None, "replica"), P("expert", "replica", None)),
        check_vma=False,
    )
```

```python
import functools

import jax
import jax.numpy as jnp
from jax import lax
from jax.experimental import pallas as pl
from jax.experimental.pallas import tpu as pltpu
from jax.sharding import PartitionSpec as P

CAP = 48
LOCAL = 3
SOURCES = 8
ROWS = SOURCES * CAP
D = 512
TOK = 256
BLK = 128
META = 16
F32 = jnp.float32
BF16 = jnp.bfloat16
VMEM_LIMIT = 32 * 1024 * 1024
EXPERT_LIMIT = 44 * 1024 * 1024
COST = {
    "ring_sums": 0,
    "partner_sums": 20,
    "own_sums": 20,
    "expert0_first": 20,
    "expert0_rest": 20,
    "expert1": 20,
    "expert2_first": 4,
    "expert2_rest": 4,
}
VMEM = pl.BlockSpec(memory_space=pltpu.VMEM)
SMEM = pl.BlockSpec(memory_space=pltpu.SMEM)


def dot(a, b, ca=1, cb=0):
    return lax.dot_general(a, b, (((ca,), (cb,)), ((), ())), preferred_element_type=F32)


def bf16_like(*shape):
    return jax.ShapeDtypeStruct(shape, BF16)


def call(kernel, name, in_specs, out_shape, args, nbytes=10**6, scratch=(), limit=VMEM_LIMIT):
    return pl.pallas_call(
        kernel,
        in_specs=in_specs,
        out_specs=jax.tree.map(lambda _: VMEM, out_shape),
        out_shape=out_shape,
        scratch_shapes=list(scratch),
        compiler_params=pltpu.CompilerParams(vmem_limit_bytes=limit),
        cost_estimate=pl.CostEstimate(
            flops=COST.get(name, 0) * 10**9, bytes_accessed=nbytes, transcendentals=0
        ),
        name=name,
    )(*args)


def along_z(dz):
    return [(z * 2 + h, ((z + dz) % 4) * 2 + h) for z in range(4) for h in range(2)]


PARTNER = [(e, e ^ 1) for e in range(8)]
CORE = [(r, r ^ 1) for r in range(16)]
ACROSS = [(r, r ^ 2) for r in range(16)]
RING = [(r, (r + (4 if r % 2 == 0 else 12)) % 16) for r in range(16)]


def pack_kernel(tokens_ref, cot_ref, ids_ref, gates_ref, out_ref, ids_s, gates_s, sems):
    copies = [
        pltpu.make_async_copy(src, dst, sems.at[n])
        for n, (src, dst) in enumerate(
            (
                (ids_ref, ids_s),
                (gates_ref, gates_s),
                (tokens_ref, out_ref.at[pl.ds(0, TOK)]),
                (cot_ref, out_ref.at[pl.ds(TOK, TOK)]),
            )
        )
    ]
    for copy in copies:
        copy.start()
    copies[0].wait()
    copies[1].wait()
    gates = gates_s[...]
    high = gates.astype(BF16).astype(F32)
    middle = (gates - high).astype(BF16).astype(F32)
    low = gates - high - middle
    meta = jnp.concatenate(
        [ids_s[...].astype(F32), high, middle, low, jnp.zeros((META - 8, TOK), F32)], axis=0
    )
    out_ref[2 * TOK :] = jnp.concatenate([meta, jnp.zeros_like(meta)], axis=1).astype(BF16)
    copies[2].wait()
    copies[3].wait()


def read_meta(packed_ref):
    meta = packed_ref[2 * TOK :, 0:TOK].astype(F32)
    gates = meta[2:4] + meta[4:6] + meta[6:8]
    return meta[0:2], gates


def dispatch_kernel(split, me_ref, packed_ref, *out_refs):
    z, h = me_ref[0] >> 1, me_ref[0] & 1
    ids, gates = read_meta(packed_ref)
    count = 4 * LOCAL
    index = lax.broadcasted_iota(jnp.int32, (16, TOK), 0)
    want = (((z + (index & 3)) & 3) * 2 + h) * LOCAL + (index >> 2)
    want = jnp.where(index < count, want, -1).astype(F32)
    hit0 = ids[0:1] == want
    hit1 = ids[1:2] == want
    hit = jnp.where(hit0 | hit1, 1.0, 0.0).astype(F32)
    gate = jnp.where(hit0, gates[0:1], jnp.where(hit1, gates[1:2], 0.0))
    earlier = lax.broadcasted_iota(jnp.int32, (TOK, TOK), 0) < lax.broadcasted_iota(
        jnp.int32, (TOK, TOK), 1
    )
    before = dot(hit.astype(BF16), jnp.where(earlier, 1.0, 0.0).astype(BF16))
    place = jnp.where(hit > 0.0, before, -1.0).astype(jnp.int32)
    slot = lax.broadcasted_iota(jnp.int32, (CAP, TOK), 0)
    for j in range(LOCAL):
        picks, weights = [], []
        for n in range(j * 4, j * 4 + 4):
            sel = slot == place[n : n + 1]
            picks.append(jnp.where(sel, 1.0, 0.0).astype(BF16))
            weights.append(jnp.sum(jnp.where(sel, gate[n : n + 1], 0.0), axis=1, keepdims=True))
        pick = jnp.concatenate(picks, axis=0)
        weight = jnp.concatenate(weights, axis=0)
        rows = dot(pick, packed_ref[0:TOK]).astype(BF16)
        grads = (weight * dot(pick, packed_ref[TOK : 2 * TOK])).astype(BF16)
        for dz in range(4):
            part = slice(dz * CAP, (dz + 1) * CAP)
            ref, at = out_refs[dz], j
            if split:
                ref, at = (out_refs[dz], 0) if j == 0 else (out_refs[4 + dz], j - 1)
            ref[at, 0] = rows[part]
            ref[at, 1] = grads[part]


def dispatch(name, split, me, packed):
    out = [bf16_like(n, 2, CAP, D) for n in ((1, 2) if split else (3,)) for _ in range(4)]
    kernel = functools.partial(dispatch_kernel, split)
    return call(kernel, name, [SMEM, VMEM], out, (me, packed), 3 * 10**6)


def join_kernel(count, *refs):
    ins, out_ref = refs[:SOURCES], refs[-1]
    for n, ref in enumerate(ins):
        skip = ref.shape[0] - count
        for j in range(count):
            out_ref[j, n] = ref[skip + j if count > 1 else 0]


def join(name, count, pieces, after):
    specs = [VMEM] * SOURCES + [pl.BlockSpec(memory_space=pl.ANY)] * len(after)
    out = bf16_like(count, SOURCES, 2, CAP, D)
    return call(functools.partial(join_kernel, count), name, specs, out, (*pieces, *after), 10**6)


def expert_kernel(j, at, base, counts, has_sums, ends, n_after, tbl_ref, own_ref, oth_ref, *refs):
    weights, refs = refs[:3], refs[3:]
    if has_sums:
        sums, refs = refs[:2], refs[2:]
    refs = refs[n_after:]
    chunks, refs = refs[: len(counts)], refs[len(counts) :]
    results, (x_s, g_s, xt_s, gt_s, wg_s, wu_s, wd_s, sems, *acc) = refs[:2], refs[2:]
    eo_s, ig_s = acc if ends else results
    flat = [ref.at[n] for ref, count in zip(chunks, counts) for n in range(count)]
    steps = len(flat) // 2

    def fetch(i):
        slot, copies = i % 2, []
        for k in range(2):
            block = pl.ds(pl.multiple_of(tbl_ref[base + 2 * i + k] * BLK, BLK), BLK)
            here = pl.ds(k * BLK, BLK)
            pairs = (
                (weights[0].at[j, :, block], wg_s.at[slot, :, here]),
                (weights[1].at[j, :, block], wu_s.at[slot, :, here]),
                (weights[2].at[j, block, :], wd_s.at[slot, here, :]),
            )
            for n, (src, dst) in enumerate(pairs):
                copies.append(pltpu.make_async_copy(src, dst, sems.at[slot, 3 * k + n]))
        return copies

    for copy in fetch(0):
        copy.start()
    for k, ref in enumerate((own_ref, oth_ref)):
        x_s[k * ROWS : (k + 1) * ROWS, :] = ref[at, :, 0].reshape(ROWS, D)
        g_s[k * ROWS : (k + 1) * ROWS, :] = ref[at, :, 1].reshape(ROWS, D)
    xt_s[...] = x_s[...].T
    gt_s[...] = g_s[...].T
    for i in range(steps):
        if i + 1 < steps:
            for copy in fetch(i + 1):
                copy.start()
        for copy in fetch(i):
            copy.wait()
        wg, wu, wd = wg_s[i % 2], wu_s[i % 2], wd_s[i % 2]
        acts = []
        for half in range(2):
            part = slice(half * ROWS, (half + 1) * ROWS)
            x, g = x_s[part], g_s[part]
            pre_gate = dot(x, wg)
            pre_up = dot(x, wu)
            grad_hidden = dot(g, wd, 1, 1)
            sig = jax.nn.sigmoid(pre_gate)
            silu = pre_gate * sig
            hidden = (silu * pre_up).astype(BF16)
            grad_gate = (grad_hidden * pre_up * sig * (1.0 + pre_gate * (1.0 - sig))).astype(BF16)
            grad_up = (grad_hidden * silu).astype(BF16)
            acts.append((grad_gate, grad_up, hidden))
            out_rows = dot(hidden, wd)
            in_rows = dot(grad_gate, wg, 1, 1) + dot(grad_up, wu, 1, 1)
            if i > 0 or has_sums:
                before = (eo_s, ig_s) if i > 0 else sums
                out_rows = before[0][part] + out_rows
                in_rows = before[1][part] + in_rows
            eo_s[part] = out_rows
            ig_s[part] = in_rows
        for k, rows_t in enumerate((xt_s, xt_s, gt_s)):
            act = jnp.concatenate([acts[0][k], acts[1][k]], axis=0)
            grad = dot(rows_t[...], act).astype(BF16)
            for lane in range(2):
                flat[2 * i + lane][k * D : (k + 1) * D, :] = grad[:, lane * BLK : (lane + 1) * BLK]
    if ends:
        for k, ref in enumerate(results):
            ref[0] = eo_s[k * ROWS : (k + 1) * ROWS, :].astype(BF16)
            ref[1] = ig_s[k * ROWS : (k + 1) * ROWS, :].astype(BF16)


def expert(name, j, at, tbl, base, counts, ends, own, oth, weights, sums=(), after=()):
    rows = 2 * ROWS
    out = [bf16_like(count, 3 * D, BLK) for count in counts]
    scratch = [pltpu.VMEM((rows, D), BF16)] * 2 + [pltpu.VMEM((D, rows), BF16)] * 2
    scratch += [pltpu.VMEM((2, D, 2 * BLK), BF16)] * 2 + [pltpu.VMEM((2, 2 * BLK, D), BF16)]
    scratch += [pltpu.SemaphoreType.DMA((2, 6))]
    if ends:
        out += [bf16_like(2, ROWS, D)] * 2
        scratch += [pltpu.VMEM((rows, D), F32)] * 2
    else:
        out += [jax.ShapeDtypeStruct((rows, D), F32)] * 2
    anywhere = pl.BlockSpec(memory_space=pl.ANY)
    kernel = functools.partial(
        expert_kernel, j, at, base, counts, bool(sums), ends, len(after)
    )
    return pl.pallas_call(
        kernel,
        in_specs=[SMEM, VMEM, VMEM] + [anywhere] * 3 + [VMEM] * len(sums) + [anywhere] * len(after),
        out_specs=[VMEM] * len(out),
        scratch_shapes=scratch,
        out_shape=out,
        compiler_params=pltpu.CompilerParams(vmem_limit_bytes=EXPERT_LIMIT),
        cost_estimate=pl.CostEstimate(
            flops=COST[name] * 10**9, bytes_accessed=10**6, transcendentals=0
        ),
        name=name,
    )(tbl, own, oth, *weights, *sums, *after)


def sums_kernel(terms, *refs):
    out_ref = refs[-1]
    for n, pairs in enumerate(terms):
        total = refs[pairs[0][0]][pairs[0][1]].astype(F32)
        for ref, index in pairs[1:]:
            total = total + refs[ref][index].astype(F32)
        out_ref[n] = total.astype(BF16)


def ring_sums(name, terms, args):
    out = bf16_like(len(terms), 3 * D, BLK)
    return call(functools.partial(sums_kernel, terms), name, [VMEM] * len(args), out, args, 3 * 10**6)


def back_kernel(count, n_after, *refs):
    ins, outs = refs[: 2 * count], refs[2 * count + n_after :]
    for n in range(SOURCES):
        for j in range(count):
            for k in range(2):
                rows = slice(n * CAP, (n + 1) * CAP)
                total = ins[2 * j][k, rows].astype(F32) + ins[2 * j + 1][k, rows].astype(F32)
                outs[n & 3][j, n >> 2, k] = total.astype(BF16)


def back(name, pairs, after=()):
    count = len(pairs) // 2
    out = [bf16_like(count, 2, 2, CAP, D)] * 4
    specs = [VMEM] * len(pairs) + [pl.BlockSpec(memory_space=pl.ANY)] * len(after)
    return call(functools.partial(back_kernel, count, len(after)), name, specs, out, (*pairs, *after))


def token_sums(side, me_ref, packed_ref, rows, out_s, in_s):
    z, h = me_ref[0] >> 1, me_ref[0] & 1
    for dz in range(4):
        for j in range(LOCAL):
            n = j * 4 + dz
            ref, at = (rows[dz], j) if j < LOCAL - 1 else (rows[4 + dz], 0)
            for k, dst in enumerate((out_s, in_s)):
                dst[n * CAP : (n + 1) * CAP, :] = ref[at, side, k]
    ids, gates = read_meta(packed_ref)
    columns = jnp.concatenate([ids, gates, jnp.zeros((4, TOK), F32)], axis=0).T
    lane = lax.broadcasted_iota(jnp.int32, (TOK, 128), 1)
    want = (((z + (lane & 3)) & 3) * 2 + h) * LOCAL + (lane >> 2)
    want = jnp.where(lane < 4 * LOCAL, want, -1).astype(F32)
    hits = [columns[:, k : k + 1] == want for k in range(2)]
    either = jnp.where(hits[0] | hits[1], 1.0, 0.0).astype(BF16)
    earlier = lax.broadcasted_iota(jnp.int32, (TOK, TOK), 1) < lax.broadcasted_iota(
        jnp.int32, (TOK, TOK), 0
    )
    before = dot(jnp.where(earlier, 1.0, 0.0).astype(BF16), either)
    code = before + (lane * CAP + 1).astype(F32)
    slots = lax.broadcasted_iota(jnp.int32, (TOK, 4 * LOCAL * CAP), 1)
    picks = []
    for k in range(2):
        slot = jnp.sum(jnp.where(hits[k], code, 0.0), axis=1, keepdims=True).astype(jnp.int32) - 1
        picks.append(jnp.where(slots == slot, 1.0, 0.0).astype(BF16))
    mixed = columns[:, 2:3] * dot(picks[0], out_s[...]) + columns[:, 3:4] * dot(picks[1], out_s[...])
    return mixed, dot(picks[0] + picks[1], in_s[...])


def sides_kernel(side, me_ref, packed_ref, *refs):
    rows, (out_ref, out_s, in_s) = refs[:8], refs[-3:]
    mixed, grad = token_sums(side, me_ref, packed_ref, rows, out_s, in_s)
    out_ref[0] = mixed.astype(out_ref.dtype)
    out_ref[1] = grad.astype(out_ref.dtype)


def token_outputs(name, side, dtype, me, packed, rows, after=()):
    specs = [SMEM] + [VMEM] * 9 + [pl.BlockSpec(memory_space=pl.ANY)] * len(after)
    out = jax.ShapeDtypeStruct((2, TOK, D), dtype)
    scratch = [pltpu.VMEM((4 * LOCAL * CAP, D), BF16)] * 2
    kernel = functools.partial(sides_kernel, side)
    return call(kernel, name, specs, out, (me, packed, *rows, *after), 3 * 10**6, scratch)


def finish_kernel(*refs):
    ins, outs = refs[: 2 * LOCAL], refs[2 * LOCAL :]
    for j in range(LOCAL):
        total = (ins[2 * j][...].astype(F32) + ins[2 * j + 1][...].astype(F32)).astype(BF16)
        outs[0][j] = total[0:D]
        outs[1][j] = total[D : 2 * D]
        outs[2][j] = total[2 * D :].T


def add(*terms):
    return functools.reduce(lambda a, b: a + b, [t.astype(F32) for t in terms]).astype(BF16)


def local(tokens, expert_ids, gates, cotangent, w_gate, w_up, w_down):
    me = lax.axis_index("expert").astype(jnp.int32).reshape(1)
    rep = lax.axis_index("replica").astype(jnp.int32)
    y, x, core = rep >> 2, (rep >> 1) & 1, rep & 1
    step = jnp.arange(16, dtype=jnp.int32)
    hop = jnp.where(step < 8, step >> 1, step & 3)
    flip = jnp.where(step < 8, step & 1, (step < 12).astype(jnp.int32))
    tbl = ((y + (3 - hop) * (1 - 2 * core)) & 3) * 4 + (x ^ flip) * 2 + core

    def over_replica(label, value, perm):
        with jax.named_scope(label):
            return lax.ppermute(value, "replica", perm)

    def to_z(label, value, dz):
        with jax.named_scope(label):
            return lax.ppermute(value, "expert", along_z(dz))

    packed = call(
        pack_kernel,
        "pack",
        [pl.BlockSpec(memory_space=pltpu.HBM)] * 4,
        bf16_like(2 * TOK + META, D),
        (tokens, cotangent, expert_ids.T, gates.T),
        scratch=[
            pltpu.VMEM((2, TOK), jnp.int32),
            pltpu.VMEM((2, TOK), F32),
            pltpu.SemaphoreType.DMA((4,)),
        ],
        limit=65000 * 1024,
    )
    with jax.named_scope("packed"):
        partner = lax.ppermute(packed, "expert", PARTNER)
    sent = dispatch("own_slots", False, me, packed)
    from_own = [sent[0]] + [to_z("own_rows", sent[dz], dz) for dz in range(1, 4)]
    sent = dispatch("partner_slots", True, me, partner)
    firsts = [sent[0]] + [to_z("partner_rows0", sent[dz], dz) for dz in range(1, 4)]
    rests = [sent[4]] + [to_z("partner_rows12", sent[4 + dz], dz) for dz in range(1, 4)]

    weights = (w_gate, w_up, w_down)
    own0 = join("join0", 1, from_own + firsts, ())
    oth0 = over_replica("core_rows0", own0, CORE)
    far0, *sums = expert("expert0_first", 0, 0, tbl, 0, (2,), False, own0, oth0, weights)
    second0 = over_replica("ring0_1", far0, RING)
    own12 = join("join12", 2, from_own + rests, (far0,))
    oth12 = over_replica("core_rows12", own12, CORE)
    mid0, near0, home0, ret0, swap0 = expert(
        "expert0_rest", 0, 0, tbl, 2, (2, 2, 2), True, own0, oth0, weights, sums, (own12,)
    )
    mid0, swap0, second0 = lax.optimization_barrier((mid0, swap0, second0))
    second0 = add(mid0, second0)
    third0 = over_replica("ring0_2", second0, RING)
    swap0 = over_replica("core_back0", swap0, CORE)
    cross1, *mine1, ret1, swap1 = expert(
        "expert1", 1, 0, tbl, 8, (4, 1, 1, 1, 1), True, own12, oth12, weights, (), (second0,)
    )
    cross1, swap1, third0 = lax.optimization_barrier((cross1, swap1, third0))
    third0 = add(near0, third0)
    last0 = over_replica("ring0_3", third0, RING)
    crossed1 = over_replica("cross1", cross1, ACROSS)
    swap1 = over_replica("core_back1", swap1, CORE)
    far2, *sums = expert(
        "expert2_first", 2, 1, tbl, 0, (2,), False, own12, oth12, weights, (), (third0, ret1)
    )
    second2 = over_replica("ring2_1", far2, RING)
    back01 = back("back01", (ret0, swap0, ret1, swap1), (far2,))
    rows01 = [back01[0]] + [to_z("rows_back01", back01[dz], 4 - dz) for dz in range(1, 4)]
    across0 = add(home0[1], last0[1])
    mid2, near2, home2, ret2, swap2 = expert(
        "expert2_rest", 2, 1, tbl, 2, (2, 2, 2), True, own12, oth12, weights, sums,
        (back01[0], across0),
    )
    mid2, swap2, second2, *rows01 = lax.optimization_barrier((mid2, swap2, second2, *rows01))
    swap2 = over_replica("core_back2", swap2, CORE)
    third2 = over_replica("ring2_2", add(mid2, second2), RING)
    back2 = back("back2", (ret2, swap2))
    rows2 = [back2[0]] + [to_z("rows_back2", back2[dz], 4 - dz) for dz in range(1, 4)]
    third2, crossed1, across0, _ = lax.optimization_barrier((third2, crossed1, across0, back2[0]))
    third = ring_sums(
        "ring_sums",
        [((0, 0), (1, 0)), ((0, 1), (1, 1)), ((2, 0), (3, 0))],
        (near2, third2, mine1[0], crossed1),
    )
    third = over_replica("ring2_3", third, RING)
    across0 = over_replica("across0", across0, ACROSS)
    rows = rows01 + rows2
    theirs = token_outputs("partner_sums", 1, BF16, me, partner, rows)
    with jax.named_scope("partner_out"):
        others = lax.ppermute(theirs, "expert", PARTNER)
    mine = token_outputs("own_sums", 0, F32, me, packed, rows, (theirs,))
    third, across0, mine = lax.optimization_barrier((third, across0, mine))
    across2 = over_replica("across2", add(home2[1], third[1]), ACROSS)
    ring1 = over_replica("ring1_2", add(mine1[1][0], crossed1[1], third[2]), RING)
    ring1, others = lax.optimization_barrier((ring1, others))
    ring1 = over_replica("ring1_3", add(mine1[2][0], crossed1[2], ring1), RING)
    mixed, token_grad = add(mine[0], others[0]), add(mine[1], others[1])
    parts = [add(home0[0], last0[0]), across0]
    parts += [add(mine1[3][0], crossed1[3]), ring1]
    parts += [add(home2[0], third[0]), across2]
    gate_grad, up_grad, down_grad = call(
        finish_kernel, "finish", [VMEM] * len(parts),
        [bf16_like(LOCAL, D, BLK), bf16_like(LOCAL, D, BLK), bf16_like(LOCAL, BLK, D)],
        parts, 4 * 10**6,
    )
    return mixed, token_grad, gate_grad, up_grad, down_grad


def solution(mesh):
    tokens = P(("expert", "replica"), None)
    return jax.shard_map(
        local,
        mesh=mesh,
        in_specs=(tokens,) * 4 + (P("expert", None, None),) * 3,
        out_specs=(tokens,) * 2
        + (P("expert", None, "replica"), P("expert", None, "replica"), P("expert", "replica", None)),
        check_vma=False,
    )
```

```python
import functools

import jax
import jax.numpy as jnp
from jax import lax
from jax.experimental import pallas as pl
from jax.experimental.pallas import tpu as pltpu
from jax.sharding import PartitionSpec as P

CAP = 48
LOCAL = 3
SOURCES = 8
ROWS = SOURCES * CAP
D = 512
TOK = 256
BLK = 128
META = 16
F32 = jnp.float32
BF16 = jnp.bfloat16
VMEM_LIMIT = 32 * 1024 * 1024
EXPERT_LIMIT = 44 * 1024 * 1024
COST = {
    "ring_sums": 0,
    "partner_sums": 20,
    "own_sums": 20,
    "expert0_first": 20,
    "expert0_rest": 20,
    "expert1": 20,
    "expert2_first": 4,
    "expert2_rest": 4,
}
VMEM = pl.BlockSpec(memory_space=pltpu.VMEM)
SMEM = pl.BlockSpec(memory_space=pltpu.SMEM)


def dot(a, b, ca=1, cb=0):
    return lax.dot_general(a, b, (((ca,), (cb,)), ((), ())), preferred_element_type=F32)


def bf16_like(*shape):
    return jax.ShapeDtypeStruct(shape, BF16)


def call(kernel, name, in_specs, out_shape, args, nbytes=10**6, scratch=(), limit=VMEM_LIMIT):
    return pl.pallas_call(
        kernel,
        in_specs=in_specs,
        out_specs=jax.tree.map(lambda _: VMEM, out_shape),
        out_shape=out_shape,
        scratch_shapes=list(scratch),
        compiler_params=pltpu.CompilerParams(vmem_limit_bytes=limit),
        cost_estimate=pl.CostEstimate(
            flops=COST.get(name, 0) * 10**9, bytes_accessed=nbytes, transcendentals=0
        ),
        name=name,
    )(*args)


def along_z(dz):
    return [(z * 2 + h, ((z + dz) % 4) * 2 + h) for z in range(4) for h in range(2)]


PARTNER = [(e, e ^ 1) for e in range(8)]
CORE = [(r, r ^ 1) for r in range(16)]
ACROSS = [(r, r ^ 2) for r in range(16)]
RING = [(r, (r + (4 if r % 2 == 0 else 12)) % 16) for r in range(16)]
OTHER_WAY = [(b, a) for a, b in RING]


def pack_kernel(tokens_ref, cot_ref, ids_ref, gates_ref, out_ref, ids_s, gates_s, sems):
    copies = [
        pltpu.make_async_copy(src, dst, sems.at[n])
        for n, (src, dst) in enumerate(
            (
                (ids_ref, ids_s),
                (gates_ref, gates_s),
                (tokens_ref, out_ref.at[pl.ds(0, TOK)]),
                (cot_ref, out_ref.at[pl.ds(TOK, TOK)]),
            )
        )
    ]
    for copy in copies:
        copy.start()
    copies[0].wait()
    copies[1].wait()
    gates = gates_s[...]
    high = gates.astype(BF16).astype(F32)
    middle = (gates - high).astype(BF16).astype(F32)
    low = gates - high - middle
    meta = jnp.concatenate(
        [ids_s[...].astype(F32), high, middle, low, jnp.zeros((META - 8, TOK), F32)], axis=0
    )
    out_ref[2 * TOK :] = jnp.concatenate([meta, jnp.zeros_like(meta)], axis=1).astype(BF16)
    copies[2].wait()
    copies[3].wait()


def read_meta(packed_ref):
    meta = packed_ref[2 * TOK :, 0:TOK].astype(F32)
    gates = meta[2:4] + meta[4:6] + meta[6:8]
    return meta[0:2], gates


def dispatch_kernel(split, me_ref, packed_ref, *out_refs):
    z, h = me_ref[0] >> 1, me_ref[0] & 1
    ids, gates = read_meta(packed_ref)
    count = 4 * LOCAL
    index = lax.broadcasted_iota(jnp.int32, (16, TOK), 0)
    want = (((z + (index & 3)) & 3) * 2 + h) * LOCAL + (index >> 2)
    want = jnp.where(index < count, want, -1).astype(F32)
    hit0 = ids[0:1] == want
    hit1 = ids[1:2] == want
    hit = jnp.where(hit0 | hit1, 1.0, 0.0).astype(F32)
    gate = jnp.where(hit0, gates[0:1], jnp.where(hit1, gates[1:2], 0.0))
    earlier = lax.broadcasted_iota(jnp.int32, (TOK, TOK), 0) < lax.broadcasted_iota(
        jnp.int32, (TOK, TOK), 1
    )
    before = dot(hit.astype(BF16), jnp.where(earlier, 1.0, 0.0).astype(BF16))
    place = jnp.where(hit > 0.0, before, -1.0).astype(jnp.int32)
    slot = lax.broadcasted_iota(jnp.int32, (CAP, TOK), 0)
    for j in range(LOCAL):
        picks, weights = [], []
        for n in range(j * 4, j * 4 + 4):
            sel = slot == place[n : n + 1]
            picks.append(jnp.where(sel, 1.0, 0.0).astype(BF16))
            weights.append(jnp.sum(jnp.where(sel, gate[n : n + 1], 0.0), axis=1, keepdims=True))
        pick = jnp.concatenate(picks, axis=0)
        weight = jnp.concatenate(weights, axis=0)
        rows = dot(pick, packed_ref[0:TOK]).astype(BF16)
        grads = (weight * dot(pick, packed_ref[TOK : 2 * TOK])).astype(BF16)
        for dz in range(4):
            part = slice(dz * CAP, (dz + 1) * CAP)
            ref, at = out_refs[dz], j
            if split:
                ref, at = (out_refs[dz], 0) if j == 0 else (out_refs[4 + dz], j - 1)
            ref[at, 0] = rows[part]
            ref[at, 1] = grads[part]


def dispatch(name, split, me, packed):
    out = [bf16_like(n, 2, CAP, D) for n in ((1, 2) if split else (3,)) for _ in range(4)]
    kernel = functools.partial(dispatch_kernel, split)
    return call(kernel, name, [SMEM, VMEM], out, (me, packed), 3 * 10**6)


def join_kernel(count, *refs):
    ins, out_ref = refs[:SOURCES], refs[-1]
    for n, ref in enumerate(ins):
        skip = ref.shape[0] - count
        for j in range(count):
            out_ref[j, n] = ref[skip + j if count > 1 else 0]


def join(name, count, pieces, after):
    specs = [VMEM] * SOURCES + [pl.BlockSpec(memory_space=pl.ANY)] * len(after)
    out = bf16_like(count, SOURCES, 2, CAP, D)
    return call(functools.partial(join_kernel, count), name, specs, out, (*pieces, *after), 10**6)


def expert_kernel(j, at, base, counts, has_sums, ends, n_after, tbl_ref, own_ref, oth_ref, *refs):
    weights, refs = refs[:3], refs[3:]
    if has_sums:
        sums, refs = refs[:2], refs[2:]
    refs = refs[n_after:]
    chunks, refs = refs[: len(counts)], refs[len(counts) :]
    results, (x_s, g_s, xt_s, gt_s, wg_s, wu_s, wd_s, sems, *acc) = refs[:2], refs[2:]
    eo_s, ig_s = acc if ends else results
    flat = [ref.at[n] for ref, count in zip(chunks, counts) for n in range(count)]
    steps = len(flat) // 2

    def fetch(i):
        slot, copies = i % 2, []
        for k in range(2):
            block = pl.ds(pl.multiple_of(tbl_ref[base + 2 * i + k] * BLK, BLK), BLK)
            here = pl.ds(k * BLK, BLK)
            pairs = (
                (weights[0].at[j, :, block], wg_s.at[slot, :, here]),
                (weights[1].at[j, :, block], wu_s.at[slot, :, here]),
                (weights[2].at[j, block, :], wd_s.at[slot, here, :]),
            )
            for n, (src, dst) in enumerate(pairs):
                copies.append(pltpu.make_async_copy(src, dst, sems.at[slot, 3 * k + n]))
        return copies

    for copy in fetch(0):
        copy.start()
    for k, ref in enumerate((own_ref, oth_ref)):
        x_s[k * ROWS : (k + 1) * ROWS, :] = ref[at, :, 0].reshape(ROWS, D)
        g_s[k * ROWS : (k + 1) * ROWS, :] = ref[at, :, 1].reshape(ROWS, D)
    xt_s[...] = x_s[...].T
    gt_s[...] = g_s[...].T
    for i in range(steps):
        if i + 1 < steps:
            for copy in fetch(i + 1):
                copy.start()
        for copy in fetch(i):
            copy.wait()
        wg, wu, wd = wg_s[i % 2], wu_s[i % 2], wd_s[i % 2]
        acts = []
        for half in range(2):
            part = slice(half * ROWS, (half + 1) * ROWS)
            x, g = x_s[part], g_s[part]
            pre_gate = dot(x, wg)
            pre_up = dot(x, wu)
            grad_hidden = dot(g, wd, 1, 1)
            sig = jax.nn.sigmoid(pre_gate)
            silu = pre_gate * sig
            hidden = (silu * pre_up).astype(BF16)
            grad_gate = (grad_hidden * pre_up * sig * (1.0 + pre_gate * (1.0 - sig))).astype(BF16)
            grad_up = (grad_hidden * silu).astype(BF16)
            acts.append((grad_gate, grad_up, hidden))
            out_rows = dot(hidden, wd)
            in_rows = dot(grad_gate, wg, 1, 1) + dot(grad_up, wu, 1, 1)
            if i > 0 or has_sums:
                before = (eo_s, ig_s) if i > 0 else sums
                out_rows = before[0][part] + out_rows
                in_rows = before[1][part] + in_rows
            eo_s[part] = out_rows
            ig_s[part] = in_rows
        for k, rows_t in enumerate((xt_s, xt_s, gt_s)):
            act = jnp.concatenate([acts[0][k], acts[1][k]], axis=0)
            grad = dot(rows_t[...], act).astype(BF16)
            for lane in range(2):
                flat[2 * i + lane][k * D : (k + 1) * D, :] = grad[:, lane * BLK : (lane + 1) * BLK]
    if ends:
        for k, ref in enumerate(results):
            ref[0] = eo_s[k * ROWS : (k + 1) * ROWS, :].astype(BF16)
            ref[1] = ig_s[k * ROWS : (k + 1) * ROWS, :].astype(BF16)


def expert(name, j, at, tbl, base, counts, ends, own, oth, weights, sums=(), after=()):
    rows = 2 * ROWS
    out = [bf16_like(count, 3 * D, BLK) for count in counts]
    scratch = [pltpu.VMEM((rows, D), BF16)] * 2 + [pltpu.VMEM((D, rows), BF16)] * 2
    scratch += [pltpu.VMEM((2, D, 2 * BLK), BF16)] * 2 + [pltpu.VMEM((2, 2 * BLK, D), BF16)]
    scratch += [pltpu.SemaphoreType.DMA((2, 6))]
    if ends:
        out += [bf16_like(2, ROWS, D)] * 2
        scratch += [pltpu.VMEM((rows, D), F32)] * 2
    else:
        out += [jax.ShapeDtypeStruct((rows, D), F32)] * 2
    anywhere = pl.BlockSpec(memory_space=pl.ANY)
    kernel = functools.partial(
        expert_kernel, j, at, base, counts, bool(sums), ends, len(after)
    )
    return pl.pallas_call(
        kernel,
        in_specs=[SMEM, VMEM, VMEM] + [anywhere] * 3 + [VMEM] * len(sums) + [anywhere] * len(after),
        out_specs=[VMEM] * len(out),
        scratch_shapes=scratch,
        out_shape=out,
        compiler_params=pltpu.CompilerParams(vmem_limit_bytes=EXPERT_LIMIT),
        cost_estimate=pl.CostEstimate(
            flops=COST[name] * 10**9, bytes_accessed=10**6, transcendentals=0
        ),
        name=name,
    )(tbl, own, oth, *weights, *sums, *after)


def sums_kernel(terms, *refs):
    out_ref = refs[-1]
    for n, pairs in enumerate(terms):
        total = refs[pairs[0][0]][pairs[0][1]].astype(F32)
        for ref, index in pairs[1:]:
            total = total + refs[ref][index].astype(F32)
        out_ref[n] = total.astype(BF16)


def ring_sums(name, terms, args):
    out = bf16_like(len(terms), 3 * D, BLK)
    return call(functools.partial(sums_kernel, terms), name, [VMEM] * len(args), out, args, 3 * 10**6)


def back_kernel(count, n_after, *refs):
    ins, outs = refs[: 2 * count], refs[2 * count + n_after :]
    for n in range(SOURCES):
        for j in range(count):
            for k in range(2):
                rows = slice(n * CAP, (n + 1) * CAP)
                total = ins[2 * j][k, rows].astype(F32) + ins[2 * j + 1][k, rows].astype(F32)
                outs[n & 3][j, n >> 2, k] = total.astype(BF16)


def back(name, pairs, after=()):
    count = len(pairs) // 2
    out = [bf16_like(count, 2, 2, CAP, D)] * 4
    specs = [VMEM] * len(pairs) + [pl.BlockSpec(memory_space=pl.ANY)] * len(after)
    return call(functools.partial(back_kernel, count, len(after)), name, specs, out, (*pairs, *after))


def token_sums(side, me_ref, packed_ref, rows, out_s, in_s):
    z, h = me_ref[0] >> 1, me_ref[0] & 1
    for dz in range(4):
        for j in range(LOCAL):
            n = j * 4 + dz
            ref, at = (rows[dz], 0) if j == 0 else (rows[4 + dz], j - 1)
            for k, dst in enumerate((out_s, in_s)):
                dst[n * CAP : (n + 1) * CAP, :] = ref[at, side, k]
    ids, gates = read_meta(packed_ref)
    columns = jnp.concatenate([ids, gates, jnp.zeros((4, TOK), F32)], axis=0).T
    lane = lax.broadcasted_iota(jnp.int32, (TOK, 128), 1)
    want = (((z + (lane & 3)) & 3) * 2 + h) * LOCAL + (lane >> 2)
    want = jnp.where(lane < 4 * LOCAL, want, -1).astype(F32)
    hits = [columns[:, k : k + 1] == want for k in range(2)]
    either = jnp.where(hits[0] | hits[1], 1.0, 0.0).astype(BF16)
    earlier = lax.broadcasted_iota(jnp.int32, (TOK, TOK), 1) < lax.broadcasted_iota(
        jnp.int32, (TOK, TOK), 0
    )
    before = dot(jnp.where(earlier, 1.0, 0.0).astype(BF16), either)
    code = before + (lane * CAP + 1).astype(F32)
    slots = lax.broadcasted_iota(jnp.int32, (TOK, 4 * LOCAL * CAP), 1)
    picks = []
    for k in range(2):
        slot = jnp.sum(jnp.where(hits[k], code, 0.0), axis=1, keepdims=True).astype(jnp.int32) - 1
        picks.append(jnp.where(slots == slot, 1.0, 0.0).astype(BF16))
    mixed = columns[:, 2:3] * dot(picks[0], out_s[...]) + columns[:, 3:4] * dot(picks[1], out_s[...])
    return mixed, dot(picks[0] + picks[1], in_s[...])


def sides_kernel(side, me_ref, packed_ref, *refs):
    rows, (out_ref, out_s, in_s) = refs[:8], refs[-3:]
    mixed, grad = token_sums(side, me_ref, packed_ref, rows, out_s, in_s)
    out_ref[0] = mixed.astype(out_ref.dtype)
    out_ref[1] = grad.astype(out_ref.dtype)


def token_outputs(name, side, dtype, me, packed, rows, after=()):
    specs = [SMEM] + [VMEM] * 9 + [pl.BlockSpec(memory_space=pl.ANY)] * len(after)
    out = jax.ShapeDtypeStruct((2, TOK, D), dtype)
    scratch = [pltpu.VMEM((4 * LOCAL * CAP, D), BF16)] * 2
    kernel = functools.partial(sides_kernel, side)
    return call(kernel, name, specs, out, (me, packed, *rows, *after), 3 * 10**6, scratch)


def finish_kernel(*refs):
    ins, outs = refs[: 2 * LOCAL], refs[2 * LOCAL :]
    for j in range(LOCAL):
        total = (ins[2 * j][...].astype(F32) + ins[2 * j + 1][...].astype(F32)).astype(BF16)
        outs[0][j] = total[0:D]
        outs[1][j] = total[D : 2 * D]
        outs[2][j] = total[2 * D :].T


def add(*terms):
    return functools.reduce(lambda a, b: a + b, [t.astype(F32) for t in terms]).astype(BF16)


def local(tokens, expert_ids, gates, cotangent, w_gate, w_up, w_down):
    me = lax.axis_index("expert").astype(jnp.int32).reshape(1)
    rep = lax.axis_index("replica").astype(jnp.int32)
    y, x, core = rep >> 2, (rep >> 1) & 1, rep & 1
    step = jnp.arange(16, dtype=jnp.int32)
    hop = jnp.where(step < 8, step >> 1, step & 3)
    flip = jnp.where(step < 8, step & 1, (step < 12).astype(jnp.int32))
    tbl = ((y + (3 - hop) * (1 - 2 * core)) & 3) * 4 + (x ^ flip) * 2 + core

    def over_replica(label, value, perm):
        with jax.named_scope(label):
            return lax.ppermute(value, "replica", perm)

    def to_z(label, value, dz):
        with jax.named_scope(label):
            return lax.ppermute(value, "expert", along_z(dz))

    packed = call(
        pack_kernel,
        "pack",
        [pl.BlockSpec(memory_space=pltpu.HBM)] * 4,
        bf16_like(2 * TOK + META, D),
        (tokens, cotangent, expert_ids.T, gates.T),
        scratch=[
            pltpu.VMEM((2, TOK), jnp.int32),
            pltpu.VMEM((2, TOK), F32),
            pltpu.SemaphoreType.DMA((4,)),
        ],
        limit=65000 * 1024,
    )
    with jax.named_scope("packed"):
        partner = lax.ppermute(packed, "expert", PARTNER)
    sent = dispatch("own_slots", False, me, packed)
    from_own = [sent[0]] + [to_z("own_rows", sent[dz], dz) for dz in range(1, 4)]
    sent = dispatch("partner_slots", True, me, partner)
    firsts = [sent[0]] + [to_z("partner_rows0", sent[dz], dz) for dz in range(1, 4)]
    rests = [sent[4]] + [to_z("partner_rows12", sent[4 + dz], dz) for dz in range(1, 4)]

    weights = (w_gate, w_up, w_down)
    own0 = join("join0", 1, from_own + firsts, ())
    oth0 = over_replica("core_rows0", own0, CORE)
    far0, *sums = expert("expert0_first", 0, 0, tbl, 0, (2,), False, own0, oth0, weights)
    second0 = over_replica("ring0_1", far0, RING)
    own12 = join("join12", 2, from_own + rests, (far0,))
    oth12 = over_replica("core_rows12", own12, CORE)
    mid0, near0, home0, ret0, swap0 = expert(
        "expert0_rest", 0, 0, tbl, 2, (2, 2, 2), True, own0, oth0, weights, sums, (own12,)
    )
    mid0, swap0, second0 = lax.optimization_barrier((mid0, swap0, second0))
    second0 = add(mid0, second0)
    third0 = over_replica("ring0_2", second0, RING)
    swap0 = over_replica("core_back0", swap0, CORE)
    cross1, *mine1, ret1, swap1 = expert(
        "expert1", 1, 0, tbl, 8, (4, 1, 1, 1, 1), True, own12, oth12, weights, (), (second0,)
    )
    cross1, swap1, third0 = lax.optimization_barrier((cross1, swap1, third0))
    third0 = add(near0, third0)
    last0 = over_replica("ring0_3", third0, RING)
    crossed1 = over_replica("cross1", cross1, ACROSS)
    swap1 = over_replica("core_back1", swap1, CORE)
    far2, *sums = expert(
        "expert2_first", 2, 1, tbl, 0, (2,), False, own12, oth12, weights, (), (third0, ret1)
    )
    second2 = over_replica("ring2_1", far2, RING)
    back0 = back("back0", (ret0, swap0), (far2,))
    rows0 = [back0[0]] + [to_z("rows_back0", back0[dz], 4 - dz) for dz in range(1, 4)]
    across0 = add(home0[1], last0[1])
    mid2, near2, home2, ret2, swap2 = expert(
        "expert2_rest", 2, 1, tbl, 2, (2, 2, 2), True, own12, oth12, weights, sums,
        (back0[0], across0),
    )
    mid2, swap2, second2, *rows0 = lax.optimization_barrier((mid2, swap2, second2, *rows0))
    swap2 = over_replica("core_back2", swap2, CORE)
    third2 = over_replica("ring2_2", add(mid2, second2), RING)
    back12 = back("back12", (ret1, swap1, ret2, swap2))
    rows12 = [back12[0]] + [to_z("rows_back12", back12[dz], 4 - dz) for dz in range(1, 4)]
    third2, crossed1, across0, _ = lax.optimization_barrier((third2, crossed1, across0, back12[0]))
    third = ring_sums(
        "ring_sums",
        [((0, 0), (1, 0)), ((0, 1), (1, 1)), ((2, 0), (3, 1))],
        (near2, third2, mine1[1], crossed1),
    )
    third = over_replica("ring2_3", third, RING)
    across0 = over_replica("across0", across0, ACROSS)
    rows = rows0 + rows12
    theirs = token_outputs("partner_sums", 1, BF16, me, partner, rows)
    with jax.named_scope("partner_out"):
        others = lax.ppermute(theirs, "expert", PARTNER)
    mine = token_outputs("own_sums", 0, F32, me, packed, rows, (theirs,))
    third, across0, mine = lax.optimization_barrier((third, across0, mine))
    across2 = over_replica("across2", add(home2[1], third[1]), ACROSS)
    ring1 = over_replica("ring1_2", add(mine1[2][0], crossed1[2], third[2]), RING)
    far1 = over_replica("ring1_far", add(mine1[0][0], crossed1[0]), OTHER_WAY)
    ring1, others = lax.optimization_barrier((ring1, others))
    mixed, token_grad = add(mine[0], others[0]), add(mine[1], others[1])
    parts = [add(home0[0], last0[0]), across0]
    parts += [add(mine1[3][0], crossed1[3], far1), ring1]
    parts += [add(home2[0], third[0]), across2]
    gate_grad, up_grad, down_grad = call(
        finish_kernel, "finish", [VMEM] * len(parts),
        [bf16_like(LOCAL, D, BLK), bf16_like(LOCAL, D, BLK), bf16_like(LOCAL, BLK, D)],
        parts, 4 * 10**6,
    )
    return mixed, token_grad, gate_grad, up_grad, down_grad


def solution(mesh):
    tokens = P(("expert", "replica"), None)
    return jax.shard_map(
        local,
        mesh=mesh,
        in_specs=(tokens,) * 4 + (P("expert", None, None),) * 3,
        out_specs=(tokens,) * 2
        + (P("expert", None, "replica"), P("expert", None, "replica"), P("expert", "replica", None)),
        check_vma=False,
    )
```

```python
import functools

import jax
import jax.numpy as jnp
from jax import lax
from jax.experimental import pallas as pl
from jax.experimental.pallas import tpu as pltpu
from jax.sharding import PartitionSpec as P

CAP = 48
LOCAL = 3
SOURCES = 8
ROWS = SOURCES * CAP
D = 512
TOK = 256
BLK = 128
META = 16
F32 = jnp.float32
BF16 = jnp.bfloat16
VMEM_LIMIT = 32 * 1024 * 1024
EXPERT_LIMIT = 44 * 1024 * 1024
COST = {
    "ring_sums": 0,
    "partner_sums": 20,
    "own_sums": 20,
    "expert0_first": 20,
    "expert0_rest": 20,
    "expert1": 20,
    "expert2_first": 4,
    "expert2_rest": 4,
}
VMEM = pl.BlockSpec(memory_space=pltpu.VMEM)
SMEM = pl.BlockSpec(memory_space=pltpu.SMEM)


def dot(a, b, ca=1, cb=0):
    return lax.dot_general(a, b, (((ca,), (cb,)), ((), ())), preferred_element_type=F32)


def bf16_like(*shape):
    return jax.ShapeDtypeStruct(shape, BF16)


def call(kernel, name, in_specs, out_shape, args, nbytes=10**6, scratch=(), limit=VMEM_LIMIT):
    return pl.pallas_call(
        kernel,
        in_specs=in_specs,
        out_specs=jax.tree.map(lambda _: VMEM, out_shape),
        out_shape=out_shape,
        scratch_shapes=list(scratch),
        compiler_params=pltpu.CompilerParams(vmem_limit_bytes=limit),
        cost_estimate=pl.CostEstimate(
            flops=COST.get(name, 0) * 10**9, bytes_accessed=nbytes, transcendentals=0
        ),
        name=name,
    )(*args)


def along_z(dz):
    return [(z * 2 + h, ((z + dz) % 4) * 2 + h) for z in range(4) for h in range(2)]


Z_ORDER = (0, 2, 1, 3)
PARTNER = [(e, e ^ 1) for e in range(8)]
CORE = [(r, r ^ 1) for r in range(16)]
ACROSS = [(r, r ^ 2) for r in range(16)]
RING = [(r, (r + (4 if r % 2 == 0 else 12)) % 16) for r in range(16)]
OTHER_WAY = [(b, a) for a, b in RING]


def pack_kernel(tokens_ref, cot_ref, ids_ref, gates_ref, out_ref, ids_s, gates_s, sems):
    copies = [
        pltpu.make_async_copy(src, dst, sems.at[n])
        for n, (src, dst) in enumerate(
            (
                (ids_ref, ids_s),
                (gates_ref, gates_s),
                (tokens_ref, out_ref.at[pl.ds(0, TOK)]),
                (cot_ref, out_ref.at[pl.ds(TOK, TOK)]),
            )
        )
    ]
    for copy in copies:
        copy.start()
    copies[0].wait()
    copies[1].wait()
    gates = gates_s[...]
    high = gates.astype(BF16).astype(F32)
    middle = (gates - high).astype(BF16).astype(F32)
    low = gates - high - middle
    meta = jnp.concatenate(
        [ids_s[...].astype(F32), high, middle, low, jnp.zeros((META - 8, TOK), F32)], axis=0
    )
    out_ref[2 * TOK :] = jnp.concatenate([meta, jnp.zeros_like(meta)], axis=1).astype(BF16)
    copies[2].wait()
    copies[3].wait()


def read_meta(packed_ref):
    meta = packed_ref[2 * TOK :, 0:TOK].astype(F32)
    gates = meta[2:4] + meta[4:6] + meta[6:8]
    return meta[0:2], gates


def dispatch_kernel(split, me_ref, packed_ref, *out_refs):
    z, h = me_ref[0] >> 1, me_ref[0] & 1
    ids, gates = read_meta(packed_ref)
    count = 4 * LOCAL
    index = lax.broadcasted_iota(jnp.int32, (16, TOK), 0)
    want = (((z + (index & 3)) & 3) * 2 + h) * LOCAL + (index >> 2)
    want = jnp.where(index < count, want, -1).astype(F32)
    hit0 = ids[0:1] == want
    hit1 = ids[1:2] == want
    hit = jnp.where(hit0 | hit1, 1.0, 0.0).astype(F32)
    gate = jnp.where(hit0, gates[0:1], jnp.where(hit1, gates[1:2], 0.0))
    earlier = lax.broadcasted_iota(jnp.int32, (TOK, TOK), 0) < lax.broadcasted_iota(
        jnp.int32, (TOK, TOK), 1
    )
    before = dot(hit.astype(BF16), jnp.where(earlier, 1.0, 0.0).astype(BF16))
    place = jnp.where(hit > 0.0, before, -1.0).astype(jnp.int32)
    slot = lax.broadcasted_iota(jnp.int32, (CAP, TOK), 0)
    for j in range(LOCAL):
        picks, weights = [], []
        for n in range(j * 4, j * 4 + 4):
            sel = slot == place[n : n + 1]
            picks.append(jnp.where(sel, 1.0, 0.0).astype(BF16))
            weights.append(jnp.sum(jnp.where(sel, gate[n : n + 1], 0.0), axis=1, keepdims=True))
        pick = jnp.concatenate(picks, axis=0)
        weight = jnp.concatenate(weights, axis=0)
        rows = dot(pick, packed_ref[0:TOK]).astype(BF16)
        grads = (weight * dot(pick, packed_ref[TOK : 2 * TOK])).astype(BF16)
        for dz in range(4):
            part = slice(dz * CAP, (dz + 1) * CAP)
            turn = Z_ORDER.index(dz)
            ref, at = out_refs[turn], j
            if split:
                ref, at = (out_refs[turn], 0) if j == 0 else (out_refs[4 + turn], j - 1)
            ref[at, 0] = rows[part]
            ref[at, 1] = grads[part]


def dispatch(name, split, me, packed):
    out = [bf16_like(n, 2, CAP, D) for n in ((1, 2) if split else (3,)) for _ in range(4)]
    kernel = functools.partial(dispatch_kernel, split)
    return call(kernel, name, [SMEM, VMEM], out, (me, packed), 3 * 10**6)


def join_kernel(count, *refs):
    ins, out_ref = refs[:SOURCES], refs[-1]
    for n, ref in zip([side * 4 + dz for side in range(2) for dz in Z_ORDER], ins):
        skip = ref.shape[0] - count
        for j in range(count):
            out_ref[j, n] = ref[skip + j if count > 1 else 0]


def join(name, count, pieces, after):
    specs = [VMEM] * SOURCES + [pl.BlockSpec(memory_space=pl.ANY)] * len(after)
    out = bf16_like(count, SOURCES, 2, CAP, D)
    args = [pieces[side * 4 + dz] for side in range(2) for dz in Z_ORDER] + list(after)
    return call(functools.partial(join_kernel, count), name, specs, out, args, 10**6)


def expert_kernel(j, at, base, counts, has_sums, ends, n_after, tbl_ref, own_ref, oth_ref, *refs):
    weights, refs = refs[:3], refs[3:]
    if has_sums:
        sums, refs = refs[:2], refs[2:]
    refs = refs[n_after:]
    chunks, refs = refs[: len(counts)], refs[len(counts) :]
    results, (x_s, g_s, xt_s, gt_s, wg_s, wu_s, wd_s, sems, *acc) = refs[:2], refs[2:]
    eo_s, ig_s = acc if ends else results
    flat = [ref.at[n] for ref, count in zip(chunks, counts) for n in range(count)]
    steps = len(flat) // 2

    def fetch(i):
        slot, copies = i % 2, []
        for k in range(2):
            block = pl.ds(pl.multiple_of(tbl_ref[base + 2 * i + k] * BLK, BLK), BLK)
            here = pl.ds(k * BLK, BLK)
            pairs = (
                (weights[0].at[j, :, block], wg_s.at[slot, :, here]),
                (weights[1].at[j, :, block], wu_s.at[slot, :, here]),
                (weights[2].at[j, block, :], wd_s.at[slot, here, :]),
            )
            for n, (src, dst) in enumerate(pairs):
                copies.append(pltpu.make_async_copy(src, dst, sems.at[slot, 3 * k + n]))
        return copies

    for copy in fetch(0):
        copy.start()
    for k, ref in enumerate((own_ref, oth_ref)):
        x_s[k * ROWS : (k + 1) * ROWS, :] = ref[at, :, 0].reshape(ROWS, D)
        g_s[k * ROWS : (k + 1) * ROWS, :] = ref[at, :, 1].reshape(ROWS, D)
    xt_s[...] = x_s[...].T
    gt_s[...] = g_s[...].T
    for i in range(steps):
        if i + 1 < steps:
            for copy in fetch(i + 1):
                copy.start()
        for copy in fetch(i):
            copy.wait()
        wg, wu, wd = wg_s[i % 2], wu_s[i % 2], wd_s[i % 2]
        acts = []
        for half in range(2):
            part = slice(half * ROWS, (half + 1) * ROWS)
            x, g = x_s[part], g_s[part]
            pre_gate = dot(x, wg)
            pre_up = dot(x, wu)
            grad_hidden = dot(g, wd, 1, 1)
            sig = jax.nn.sigmoid(pre_gate)
            silu = pre_gate * sig
            hidden = (silu * pre_up).astype(BF16)
            grad_gate = (grad_hidden * pre_up * sig * (1.0 + pre_gate * (1.0 - sig))).astype(BF16)
            grad_up = (grad_hidden * silu).astype(BF16)
            acts.append((grad_gate, grad_up, hidden))
            out_rows = dot(hidden, wd)
            in_rows = dot(grad_gate, wg, 1, 1) + dot(grad_up, wu, 1, 1)
            if i > 0 or has_sums:
                before = (eo_s, ig_s) if i > 0 else sums
                out_rows = before[0][part] + out_rows
                in_rows = before[1][part] + in_rows
            eo_s[part] = out_rows
            ig_s[part] = in_rows
        for k, rows_t in enumerate((xt_s, xt_s, gt_s)):
            act = jnp.concatenate([acts[0][k], acts[1][k]], axis=0)
            grad = dot(rows_t[...], act).astype(BF16)
            for lane in range(2):
                flat[2 * i + lane][k * D : (k + 1) * D, :] = grad[:, lane * BLK : (lane + 1) * BLK]
    if ends:
        for k, ref in enumerate(results):
            ref[0] = eo_s[k * ROWS : (k + 1) * ROWS, :].astype(BF16)
            ref[1] = ig_s[k * ROWS : (k + 1) * ROWS, :].astype(BF16)


def expert(name, j, at, tbl, base, counts, ends, own, oth, weights, sums=(), after=()):
    rows = 2 * ROWS
    out = [bf16_like(count, 3 * D, BLK) for count in counts]
    scratch = [pltpu.VMEM((rows, D), BF16)] * 2 + [pltpu.VMEM((D, rows), BF16)] * 2
    scratch += [pltpu.VMEM((2, D, 2 * BLK), BF16)] * 2 + [pltpu.VMEM((2, 2 * BLK, D), BF16)]
    scratch += [pltpu.SemaphoreType.DMA((2, 6))]
    if ends:
        out += [bf16_like(2, ROWS, D)] * 2
        scratch += [pltpu.VMEM((rows, D), F32)] * 2
    else:
        out += [jax.ShapeDtypeStruct((rows, D), F32)] * 2
    anywhere = pl.BlockSpec(memory_space=pl.ANY)
    kernel = functools.partial(
        expert_kernel, j, at, base, counts, bool(sums), ends, len(after)
    )
    return pl.pallas_call(
        kernel,
        in_specs=[SMEM, VMEM, VMEM] + [anywhere] * 3 + [VMEM] * len(sums) + [anywhere] * len(after),
        out_specs=[VMEM] * len(out),
        scratch_shapes=scratch,
        out_shape=out,
        compiler_params=pltpu.CompilerParams(vmem_limit_bytes=EXPERT_LIMIT),
        cost_estimate=pl.CostEstimate(
            flops=COST[name] * 10**9, bytes_accessed=10**6, transcendentals=0
        ),
        name=name,
    )(tbl, own, oth, *weights, *sums, *after)


def sums_kernel(terms, *refs):
    out_ref = refs[-1]
    for n, pairs in enumerate(terms):
        total = refs[pairs[0][0]][pairs[0][1]].astype(F32)
        for ref, index in pairs[1:]:
            total = total + refs[ref][index].astype(F32)
        out_ref[n] = total.astype(BF16)


def ring_sums(name, terms, args):
    out = bf16_like(len(terms), 3 * D, BLK)
    return call(functools.partial(sums_kernel, terms), name, [VMEM] * len(args), out, args, 3 * 10**6)


def back_kernel(count, n_after, *refs):
    ins, outs = refs[: 2 * count], refs[2 * count + n_after :]
    for n in range(SOURCES):
        for j in range(count):
            for k in range(2):
                rows = slice(n * CAP, (n + 1) * CAP)
                total = ins[2 * j][k, rows].astype(F32) + ins[2 * j + 1][k, rows].astype(F32)
                outs[n & 3][j, n >> 2, k] = total.astype(BF16)


def back(name, pairs, after=()):
    count = len(pairs) // 2
    out = [bf16_like(count, 2, 2, CAP, D)] * 4
    specs = [VMEM] * len(pairs) + [pl.BlockSpec(memory_space=pl.ANY)] * len(after)
    return call(functools.partial(back_kernel, count, len(after)), name, specs, out, (*pairs, *after))


def token_sums(side, me_ref, packed_ref, rows, out_s, in_s):
    z, h = me_ref[0] >> 1, me_ref[0] & 1
    for dz in range(4):
        for j in range(LOCAL):
            n = j * 4 + dz
            ref, at = (rows[dz], 0) if j == 0 else (rows[4 + dz], j - 1)
            for k, dst in enumerate((out_s, in_s)):
                dst[n * CAP : (n + 1) * CAP, :] = ref[at, side, k]
    ids, gates = read_meta(packed_ref)
    columns = jnp.concatenate([ids, gates, jnp.zeros((4, TOK), F32)], axis=0).T
    lane = lax.broadcasted_iota(jnp.int32, (TOK, 128), 1)
    want = (((z + (lane & 3)) & 3) * 2 + h) * LOCAL + (lane >> 2)
    want = jnp.where(lane < 4 * LOCAL, want, -1).astype(F32)
    hits = [columns[:, k : k + 1] == want for k in range(2)]
    either = jnp.where(hits[0] | hits[1], 1.0, 0.0).astype(BF16)
    earlier = lax.broadcasted_iota(jnp.int32, (TOK, TOK), 1) < lax.broadcasted_iota(
        jnp.int32, (TOK, TOK), 0
    )
    before = dot(jnp.where(earlier, 1.0, 0.0).astype(BF16), either)
    code = before + (lane * CAP + 1).astype(F32)
    slots = lax.broadcasted_iota(jnp.int32, (TOK, 4 * LOCAL * CAP), 1)
    picks = []
    for k in range(2):
        slot = jnp.sum(jnp.where(hits[k], code, 0.0), axis=1, keepdims=True).astype(jnp.int32) - 1
        picks.append(jnp.where(slots == slot, 1.0, 0.0).astype(BF16))
    mixed = columns[:, 2:3] * dot(picks[0], out_s[...]) + columns[:, 3:4] * dot(picks[1], out_s[...])
    return mixed, dot(picks[0] + picks[1], in_s[...])


def sides_kernel(side, me_ref, packed_ref, *refs):
    rows, (out_ref, out_s, in_s) = refs[:8], refs[-3:]
    mixed, grad = token_sums(side, me_ref, packed_ref, rows, out_s, in_s)
    out_ref[0] = mixed.astype(out_ref.dtype)
    out_ref[1] = grad.astype(out_ref.dtype)


def token_outputs(name, side, dtype, me, packed, rows, after=()):
    specs = [SMEM] + [VMEM] * 9 + [pl.BlockSpec(memory_space=pl.ANY)] * len(after)
    out = jax.ShapeDtypeStruct((2, TOK, D), dtype)
    scratch = [pltpu.VMEM((4 * LOCAL * CAP, D), BF16)] * 2
    kernel = functools.partial(sides_kernel, side)
    return call(kernel, name, specs, out, (me, packed, *rows, *after), 3 * 10**6, scratch)


def finish_kernel(*refs):
    ins, outs = refs[: 2 * LOCAL], refs[2 * LOCAL :]
    for j in range(LOCAL):
        total = (ins[2 * j][...].astype(F32) + ins[2 * j + 1][...].astype(F32)).astype(BF16)
        outs[0][j] = total[0:D]
        outs[1][j] = total[D : 2 * D]
        outs[2][j] = total[2 * D :].T


def add(*terms):
    return functools.reduce(lambda a, b: a + b, [t.astype(F32) for t in terms]).astype(BF16)


def local(tokens, expert_ids, gates, cotangent, w_gate, w_up, w_down):
    me = lax.axis_index("expert").astype(jnp.int32).reshape(1)
    rep = lax.axis_index("replica").astype(jnp.int32)
    y, x, core = rep >> 2, (rep >> 1) & 1, rep & 1
    step = jnp.arange(16, dtype=jnp.int32)
    hop = jnp.where(step < 8, step >> 1, step & 3)
    flip = jnp.where(step < 8, step & 1, (step < 12).astype(jnp.int32))
    tbl = ((y + (3 - hop) * (1 - 2 * core)) & 3) * 4 + (x ^ flip) * 2 + core

    def over_replica(label, value, perm):
        with jax.named_scope(label):
            return lax.ppermute(value, "replica", perm)

    def to_z(label, value, dz):
        with jax.named_scope(label):
            return lax.ppermute(value, "expert", along_z(dz))

    def all_to_z(label, values):
        there = {dz: to_z(label, value, dz) if dz else value for dz, value in zip(Z_ORDER, values)}
        return [there[dz] for dz in range(4)]

    packed = call(
        pack_kernel,
        "pack",
        [pl.BlockSpec(memory_space=pltpu.HBM)] * 4,
        bf16_like(2 * TOK + META, D),
        (tokens, cotangent, expert_ids.T, gates.T),
        scratch=[
            pltpu.VMEM((2, TOK), jnp.int32),
            pltpu.VMEM((2, TOK), F32),
            pltpu.SemaphoreType.DMA((4,)),
        ],
        limit=65000 * 1024,
    )
    with jax.named_scope("packed"):
        partner = lax.ppermute(packed, "expert", PARTNER)
    sent = dispatch("own_slots", False, me, packed)
    from_own = all_to_z("own_rows", sent)
    sent = dispatch("partner_slots", True, me, partner)
    firsts = all_to_z("partner_rows0", sent[:4])
    rests = all_to_z("partner_rows12", sent[4:])

    weights = (w_gate, w_up, w_down)
    own0 = join("join0", 1, from_own + firsts, ())
    oth0 = over_replica("core_rows0", own0, CORE)
    far0, *sums = expert("expert0_first", 0, 0, tbl, 0, (2,), False, own0, oth0, weights)
    second0 = over_replica("ring0_1", far0, RING)
    own12 = join("join12", 2, from_own + rests, (far0,))
    oth12 = over_replica("core_rows12", own12, CORE)
    mid0, near0, home0, ret0, swap0 = expert(
        "expert0_rest", 0, 0, tbl, 2, (2, 2, 2), True, own0, oth0, weights, sums, (own12,)
    )
    mid0, swap0, second0 = lax.optimization_barrier((mid0, swap0, second0))
    second0 = add(mid0, second0)
    third0 = over_replica("ring0_2", second0, RING)
    swap0 = over_replica("core_back0", swap0, CORE)
    cross1, *mine1, ret1, swap1 = expert(
        "expert1", 1, 0, tbl, 8, (4, 1, 1, 1, 1), True, own12, oth12, weights, (), (second0,)
    )
    cross1, swap1, third0 = lax.optimization_barrier((cross1, swap1, third0))
    third0 = add(near0, third0)
    last0 = over_replica("ring0_3", third0, RING)
    crossed1 = over_replica("cross1", cross1, ACROSS)
    swap1 = over_replica("core_back1", swap1, CORE)
    far2, *sums = expert(
        "expert2_first", 2, 1, tbl, 0, (2,), False, own12, oth12, weights, (), (third0, ret1)
    )
    second2 = over_replica("ring2_1", far2, RING)
    back0 = back("back0", (ret0, swap0), (far2,))
    rows0 = [back0[0]] + [to_z("rows_back0", back0[dz], 4 - dz) for dz in range(1, 4)]
    across0 = add(home0[1], last0[1])
    mid2, near2, home2, ret2, swap2 = expert(
        "expert2_rest", 2, 1, tbl, 2, (2, 2, 2), True, own12, oth12, weights, sums,
        (back0[0], across0),
    )
    mid2, swap2, second2, *rows0 = lax.optimization_barrier((mid2, swap2, second2, *rows0))
    swap2 = over_replica("core_back2", swap2, CORE)
    third2 = over_replica("ring2_2", add(mid2, second2), RING)
    back12 = back("back12", (ret1, swap1, ret2, swap2))
    rows12 = [back12[0]] + [to_z("rows_back12", back12[dz], 4 - dz) for dz in range(1, 4)]
    third2, crossed1, across0, _ = lax.optimization_barrier((third2, crossed1, across0, back12[0]))
    third = ring_sums(
        "ring_sums",
        [((0, 0), (1, 0)), ((0, 1), (1, 1)), ((2, 0), (3, 1))],
        (near2, third2, mine1[1], crossed1),
    )
    third = over_replica("ring2_3", third, RING)
    across0 = over_replica("across0", across0, ACROSS)
    rows = rows0 + rows12
    theirs = token_outputs("partner_sums", 1, BF16, me, partner, rows)
    with jax.named_scope("partner_out"):
        others = lax.ppermute(theirs, "expert", PARTNER)
    mine = token_outputs("own_sums", 0, F32, me, packed, rows, (theirs,))
    third, across0, mine = lax.optimization_barrier((third, across0, mine))
    across2 = over_replica("across2", add(home2[1], third[1]), ACROSS)
    ring1 = over_replica("ring1_2", add(mine1[2][0], crossed1[2], third[2]), RING)
    far1 = over_replica("ring1_far", add(mine1[0][0], crossed1[0]), OTHER_WAY)
    ring1, others = lax.optimization_barrier((ring1, others))
    mixed, token_grad = add(mine[0], others[0]), add(mine[1], others[1])
    parts = [add(home0[0], last0[0]), across0]
    parts += [add(mine1[3][0], crossed1[3], far1), ring1]
    parts += [add(home2[0], third[0]), across2]
    gate_grad, up_grad, down_grad = call(
        finish_kernel, "finish", [VMEM] * len(parts),
        [bf16_like(LOCAL, D, BLK), bf16_like(LOCAL, D, BLK), bf16_like(LOCAL, BLK, D)],
        parts, 4 * 10**6,
    )
    return mixed, token_grad, gate_grad, up_grad, down_grad


def solution(mesh):
    tokens = P(("expert", "replica"), None)
    return jax.shard_map(
        local,
        mesh=mesh,
        in_specs=(tokens,) * 4 + (P("expert", None, None),) * 3,
        out_specs=(tokens,) * 2
        + (P("expert", None, "replica"), P("expert", None, "replica"), P("expert", "replica", None)),
        check_vma=False,
    )
```

```python
import functools

import jax
import jax.numpy as jnp
from jax import lax
from jax.experimental import pallas as pl
from jax.experimental.pallas import tpu as pltpu
from jax.sharding import PartitionSpec as P

CAP = 48
LOCAL = 3
SOURCES = 8
ROWS = SOURCES * CAP
D = 512
TOK = 256
BLK = 128
META = 16
F32 = jnp.float32
BF16 = jnp.bfloat16
VMEM_LIMIT = 32 * 1024 * 1024
EXPERT_LIMIT = 44 * 1024 * 1024
COST = {
    "ring_sums": 0,
    "partner_sums": 20,
    "own_sums": 20,
    "expert0_first": 20,
    "expert0_rest": 20,
    "expert1": 20,
    "expert2_first": 4,
    "expert2_rest": 4,
}
VMEM = pl.BlockSpec(memory_space=pltpu.VMEM)
SMEM = pl.BlockSpec(memory_space=pltpu.SMEM)


def dot(a, b, ca=1, cb=0):
    return lax.dot_general(a, b, (((ca,), (cb,)), ((), ())), preferred_element_type=F32)


def bf16_like(*shape):
    return jax.ShapeDtypeStruct(shape, BF16)


def call(kernel, name, in_specs, out_shape, args, nbytes=10**6, scratch=(), limit=VMEM_LIMIT):
    return pl.pallas_call(
        kernel,
        in_specs=in_specs,
        out_specs=jax.tree.map(lambda _: VMEM, out_shape),
        out_shape=out_shape,
        scratch_shapes=list(scratch),
        compiler_params=pltpu.CompilerParams(vmem_limit_bytes=limit),
        cost_estimate=pl.CostEstimate(
            flops=COST.get(name, 0) * 10**9, bytes_accessed=nbytes, transcendentals=0
        ),
        name=name,
    )(*args)


def along_z(dz):
    return [(z * 2 + h, ((z + dz) % 4) * 2 + h) for z in range(4) for h in range(2)]


Z_BACK = (0, 2, 1, 3)
PARTNER = [(e, e ^ 1) for e in range(8)]
CORE = [(r, r ^ 1) for r in range(16)]
ACROSS = [(r, r ^ 2) for r in range(16)]
RING = [(r, (r + (4 if r % 2 == 0 else 12)) % 16) for r in range(16)]
OTHER_WAY = [(b, a) for a, b in RING]


def pack_kernel(tokens_ref, cot_ref, ids_ref, gates_ref, out_ref, ids_s, gates_s, sems):
    copies = [
        pltpu.make_async_copy(src, dst, sems.at[n])
        for n, (src, dst) in enumerate(
            (
                (ids_ref, ids_s),
                (gates_ref, gates_s),
                (tokens_ref, out_ref.at[pl.ds(0, TOK)]),
                (cot_ref, out_ref.at[pl.ds(TOK, TOK)]),
            )
        )
    ]
    for copy in copies:
        copy.start()
    copies[0].wait()
    copies[1].wait()
    gates = gates_s[...]
    high = gates.astype(BF16).astype(F32)
    middle = (gates - high).astype(BF16).astype(F32)
    low = gates - high - middle
    meta = jnp.concatenate(
        [ids_s[...].astype(F32), high, middle, low, jnp.zeros((META - 8, TOK), F32)], axis=0
    )
    out_ref[2 * TOK :] = jnp.concatenate([meta, jnp.zeros_like(meta)], axis=1).astype(BF16)
    copies[2].wait()
    copies[3].wait()


def read_meta(packed_ref):
    meta = packed_ref[2 * TOK :, 0:TOK].astype(F32)
    gates = meta[2:4] + meta[4:6] + meta[6:8]
    return meta[0:2], gates


def dispatch_kernel(split, me_ref, packed_ref, *out_refs):
    z, h = me_ref[0] >> 1, me_ref[0] & 1
    ids, gates = read_meta(packed_ref)
    count = 4 * LOCAL
    index = lax.broadcasted_iota(jnp.int32, (16, TOK), 0)
    want = (((z + (index & 3)) & 3) * 2 + h) * LOCAL + (index >> 2)
    want = jnp.where(index < count, want, -1).astype(F32)
    hit0 = ids[0:1] == want
    hit1 = ids[1:2] == want
    hit = jnp.where(hit0 | hit1, 1.0, 0.0).astype(F32)
    gate = jnp.where(hit0, gates[0:1], jnp.where(hit1, gates[1:2], 0.0))
    earlier = lax.broadcasted_iota(jnp.int32, (TOK, TOK), 0) < lax.broadcasted_iota(
        jnp.int32, (TOK, TOK), 1
    )
    before = dot(hit.astype(BF16), jnp.where(earlier, 1.0, 0.0).astype(BF16))
    place = jnp.where(hit > 0.0, before, -1.0).astype(jnp.int32)
    slot = lax.broadcasted_iota(jnp.int32, (CAP, TOK), 0)
    for j in range(LOCAL):
        picks, weights = [], []
        for n in range(j * 4, j * 4 + 4):
            sel = slot == place[n : n + 1]
            picks.append(jnp.where(sel, 1.0, 0.0).astype(BF16))
            weights.append(jnp.sum(jnp.where(sel, gate[n : n + 1], 0.0), axis=1, keepdims=True))
        pick = jnp.concatenate(picks, axis=0)
        weight = jnp.concatenate(weights, axis=0)
        rows = dot(pick, packed_ref[0:TOK]).astype(BF16)
        grads = (weight * dot(pick, packed_ref[TOK : 2 * TOK])).astype(BF16)
        for dz in range(4):
            part = slice(dz * CAP, (dz + 1) * CAP)
            ref, at = out_refs[dz], j
            if split:
                ref, at = (out_refs[dz], 0) if j == 0 else (out_refs[4 + dz], j - 1)
            ref[at, 0] = rows[part]
            ref[at, 1] = grads[part]


def dispatch(name, split, me, packed):
    out = [bf16_like(n, 2, CAP, D) for n in ((1, 2) if split else (3,)) for _ in range(4)]
    kernel = functools.partial(dispatch_kernel, split)
    return call(kernel, name, [SMEM, VMEM], out, (me, packed), 3 * 10**6)


def join_kernel(count, *refs):
    ins, out_ref = refs[:SOURCES], refs[-1]
    for n, ref in enumerate(ins):
        skip = ref.shape[0] - count
        for j in range(count):
            out_ref[j, n] = ref[skip + j if count > 1 else 0]


def join(name, count, pieces, after):
    specs = [VMEM] * SOURCES + [pl.BlockSpec(memory_space=pl.ANY)] * len(after)
    out = bf16_like(count, SOURCES, 2, CAP, D)
    return call(functools.partial(join_kernel, count), name, specs, out, (*pieces, *after), 10**6)


def expert_kernel(j, at, base, counts, has_sums, ends, n_after, tbl_ref, own_ref, oth_ref, *refs):
    weights, refs = refs[:3], refs[3:]
    if has_sums:
        sums, refs = refs[:2], refs[2:]
    refs = refs[n_after:]
    chunks, refs = refs[: len(counts)], refs[len(counts) :]
    results, (x_s, g_s, xt_s, gt_s, wg_s, wu_s, wd_s, sems, *acc) = refs[:2], refs[2:]
    eo_s, ig_s = acc if ends else results
    flat = [ref.at[n] for ref, count in zip(chunks, counts) for n in range(count)]
    steps = len(flat) // 2

    def fetch(i):
        slot, copies = i % 2, []
        for k in range(2):
            block = pl.ds(pl.multiple_of(tbl_ref[base + 2 * i + k] * BLK, BLK), BLK)
            here = pl.ds(k * BLK, BLK)
            pairs = (
                (weights[0].at[j, :, block], wg_s.at[slot, :, here]),
                (weights[1].at[j, :, block], wu_s.at[slot, :, here]),
                (weights[2].at[j, block, :], wd_s.at[slot, here, :]),
            )
            for n, (src, dst) in enumerate(pairs):
                copies.append(pltpu.make_async_copy(src, dst, sems.at[slot, 3 * k + n]))
        return copies

    for copy in fetch(0):
        copy.start()
    for k, ref in enumerate((own_ref, oth_ref)):
        x_s[k * ROWS : (k + 1) * ROWS, :] = ref[at, :, 0].reshape(ROWS, D)
        g_s[k * ROWS : (k + 1) * ROWS, :] = ref[at, :, 1].reshape(ROWS, D)
    xt_s[...] = x_s[...].T
    gt_s[...] = g_s[...].T
    for i in range(steps):
        if i + 1 < steps:
            for copy in fetch(i + 1):
                copy.start()
        for copy in fetch(i):
            copy.wait()
        wg, wu, wd = wg_s[i % 2], wu_s[i % 2], wd_s[i % 2]
        acts = []
        for half in range(2):
            part = slice(half * ROWS, (half + 1) * ROWS)
            x, g = x_s[part], g_s[part]
            pre_gate = dot(x, wg)
            pre_up = dot(x, wu)
            grad_hidden = dot(g, wd, 1, 1)
            sig = jax.nn.sigmoid(pre_gate)
            silu = pre_gate * sig
            hidden = (silu * pre_up).astype(BF16)
            grad_gate = (grad_hidden * pre_up * sig * (1.0 + pre_gate * (1.0 - sig))).astype(BF16)
            grad_up = (grad_hidden * silu).astype(BF16)
            acts.append((grad_gate, grad_up, hidden))
            out_rows = dot(hidden, wd)
            in_rows = dot(grad_gate, wg, 1, 1) + dot(grad_up, wu, 1, 1)
            if i > 0 or has_sums:
                before = (eo_s, ig_s) if i > 0 else sums
                out_rows = before[0][part] + out_rows
                in_rows = before[1][part] + in_rows
            eo_s[part] = out_rows
            ig_s[part] = in_rows
        for k, rows_t in enumerate((xt_s, xt_s, gt_s)):
            act = jnp.concatenate([acts[0][k], acts[1][k]], axis=0)
            grad = dot(rows_t[...], act).astype(BF16)
            for lane in range(2):
                flat[2 * i + lane][k * D : (k + 1) * D, :] = grad[:, lane * BLK : (lane + 1) * BLK]
    if ends:
        for k, ref in enumerate(results):
            ref[0] = eo_s[k * ROWS : (k + 1) * ROWS, :].astype(BF16)
            ref[1] = ig_s[k * ROWS : (k + 1) * ROWS, :].astype(BF16)


def expert(name, j, at, tbl, base, counts, ends, own, oth, weights, sums=(), after=()):
    rows = 2 * ROWS
    out = [bf16_like(count, 3 * D, BLK) for count in counts]
    scratch = [pltpu.VMEM((rows, D), BF16)] * 2 + [pltpu.VMEM((D, rows), BF16)] * 2
    scratch += [pltpu.VMEM((2, D, 2 * BLK), BF16)] * 2 + [pltpu.VMEM((2, 2 * BLK, D), BF16)]
    scratch += [pltpu.SemaphoreType.DMA((2, 6))]
    if ends:
        out += [bf16_like(2, ROWS, D)] * 2
        scratch += [pltpu.VMEM((rows, D), F32)] * 2
    else:
        out += [jax.ShapeDtypeStruct((rows, D), F32)] * 2
    anywhere = pl.BlockSpec(memory_space=pl.ANY)
    kernel = functools.partial(
        expert_kernel, j, at, base, counts, bool(sums), ends, len(after)
    )
    return pl.pallas_call(
        kernel,
        in_specs=[SMEM, VMEM, VMEM] + [anywhere] * 3 + [VMEM] * len(sums) + [anywhere] * len(after),
        out_specs=[VMEM] * len(out),
        scratch_shapes=scratch,
        out_shape=out,
        compiler_params=pltpu.CompilerParams(vmem_limit_bytes=EXPERT_LIMIT),
        cost_estimate=pl.CostEstimate(
            flops=COST[name] * 10**9, bytes_accessed=10**6, transcendentals=0
        ),
        name=name,
    )(tbl, own, oth, *weights, *sums, *after)


def sums_kernel(terms, *refs):
    out_ref = refs[-1]
    for n, pairs in enumerate(terms):
        total = refs[pairs[0][0]][pairs[0][1]].astype(F32)
        for ref, index in pairs[1:]:
            total = total + refs[ref][index].astype(F32)
        out_ref[n] = total.astype(BF16)


def ring_sums(name, terms, args):
    out = bf16_like(len(terms), 3 * D, BLK)
    return call(functools.partial(sums_kernel, terms), name, [VMEM] * len(args), out, args, 3 * 10**6)


def back_kernel(count, n_after, *refs):
    ins, outs = refs[: 2 * count], refs[2 * count + n_after :]
    for n in range(SOURCES):
        for j in range(count):
            for k in range(2):
                rows = slice(n * CAP, (n + 1) * CAP)
                total = ins[2 * j][k, rows].astype(F32) + ins[2 * j + 1][k, rows].astype(F32)
                outs[n & 3][j, n >> 2, k] = total.astype(BF16)


def back(name, pairs, after=()):
    count = len(pairs) // 2
    out = [bf16_like(count, 2, 2, CAP, D)] * 4
    specs = [VMEM] * len(pairs) + [pl.BlockSpec(memory_space=pl.ANY)] * len(after)
    return call(functools.partial(back_kernel, count, len(after)), name, specs, out, (*pairs, *after))


def token_sums(side, me_ref, packed_ref, rows, out_s, in_s):
    z, h = me_ref[0] >> 1, me_ref[0] & 1
    for dz in range(4):
        for j in range(LOCAL):
            n = j * 4 + dz
            turn = Z_BACK.index(dz)
            ref, at = (rows[turn], 0) if j == 0 else (rows[4 + turn], j - 1)
            for k, dst in enumerate((out_s, in_s)):
                dst[n * CAP : (n + 1) * CAP, :] = ref[at, side, k]
    ids, gates = read_meta(packed_ref)
    columns = jnp.concatenate([ids, gates, jnp.zeros((4, TOK), F32)], axis=0).T
    lane = lax.broadcasted_iota(jnp.int32, (TOK, 128), 1)
    want = (((z + (lane & 3)) & 3) * 2 + h) * LOCAL + (lane >> 2)
    want = jnp.where(lane < 4 * LOCAL, want, -1).astype(F32)
    hits = [columns[:, k : k + 1] == want for k in range(2)]
    either = jnp.where(hits[0] | hits[1], 1.0, 0.0).astype(BF16)
    earlier = lax.broadcasted_iota(jnp.int32, (TOK, TOK), 1) < lax.broadcasted_iota(
        jnp.int32, (TOK, TOK), 0
    )
    before = dot(jnp.where(earlier, 1.0, 0.0).astype(BF16), either)
    code = before + (lane * CAP + 1).astype(F32)
    slots = lax.broadcasted_iota(jnp.int32, (TOK, 4 * LOCAL * CAP), 1)
    picks = []
    for k in range(2):
        slot = jnp.sum(jnp.where(hits[k], code, 0.0), axis=1, keepdims=True).astype(jnp.int32) - 1
        picks.append(jnp.where(slots == slot, 1.0, 0.0).astype(BF16))
    mixed = columns[:, 2:3] * dot(picks[0], out_s[...]) + columns[:, 3:4] * dot(picks[1], out_s[...])
    return mixed, dot(picks[0] + picks[1], in_s[...])


def sides_kernel(side, me_ref, packed_ref, *refs):
    rows, (out_ref, out_s, in_s) = refs[:8], refs[-3:]
    mixed, grad = token_sums(side, me_ref, packed_ref, rows, out_s, in_s)
    out_ref[0] = mixed.astype(out_ref.dtype)
    out_ref[1] = grad.astype(out_ref.dtype)


def token_outputs(name, side, dtype, me, packed, rows, after=()):
    specs = [SMEM] + [VMEM] * 9 + [pl.BlockSpec(memory_space=pl.ANY)] * len(after)
    out = jax.ShapeDtypeStruct((2, TOK, D), dtype)
    scratch = [pltpu.VMEM((4 * LOCAL * CAP, D), BF16)] * 2
    kernel = functools.partial(sides_kernel, side)
    return call(kernel, name, specs, out, (me, packed, *rows, *after), 3 * 10**6, scratch)


def finish_kernel(*refs):
    ins, outs = refs[: 2 * LOCAL], refs[2 * LOCAL :]
    for j in range(LOCAL):
        total = (ins[2 * j][...].astype(F32) + ins[2 * j + 1][...].astype(F32)).astype(BF16)
        outs[0][j] = total[0:D]
        outs[1][j] = total[D : 2 * D]
        outs[2][j] = total[2 * D :].T


def add(*terms):
    return functools.reduce(lambda a, b: a + b, [t.astype(F32) for t in terms]).astype(BF16)


def local(tokens, expert_ids, gates, cotangent, w_gate, w_up, w_down):
    me = lax.axis_index("expert").astype(jnp.int32).reshape(1)
    rep = lax.axis_index("replica").astype(jnp.int32)
    y, x, core = rep >> 2, (rep >> 1) & 1, rep & 1
    step = jnp.arange(16, dtype=jnp.int32)
    hop = jnp.where(step < 8, step >> 1, step & 3)
    flip = jnp.where(step < 8, step & 1, (step < 12).astype(jnp.int32))
    tbl = ((y + (3 - hop) * (1 - 2 * core)) & 3) * 4 + (x ^ flip) * 2 + core

    def over_replica(label, value, perm):
        with jax.named_scope(label):
            return lax.ppermute(value, "replica", perm)

    def to_z(label, value, dz):
        with jax.named_scope(label):
            return lax.ppermute(value, "expert", along_z(dz))

    packed = call(
        pack_kernel,
        "pack",
        [pl.BlockSpec(memory_space=pltpu.HBM)] * 4,
        bf16_like(2 * TOK + META, D),
        (tokens, cotangent, expert_ids.T, gates.T),
        scratch=[
            pltpu.VMEM((2, TOK), jnp.int32),
            pltpu.VMEM((2, TOK), F32),
            pltpu.SemaphoreType.DMA((4,)),
        ],
        limit=65000 * 1024,
    )
    with jax.named_scope("packed"):
        partner = lax.ppermute(packed, "expert", PARTNER)
    sent = dispatch("own_slots", False, me, packed)
    from_own = [sent[0]] + [to_z("own_rows", sent[dz], dz) for dz in range(1, 4)]
    sent = dispatch("partner_slots", True, me, partner)
    firsts = [sent[0]] + [to_z("partner_rows0", sent[dz], dz) for dz in range(1, 4)]
    rests = [sent[4]] + [to_z("partner_rows12", sent[4 + dz], dz) for dz in range(1, 4)]

    weights = (w_gate, w_up, w_down)
    own0 = join("join0", 1, from_own + firsts, ())
    oth0 = over_replica("core_rows0", own0, CORE)
    far0, *sums = expert("expert0_first", 0, 0, tbl, 0, (2,), False, own0, oth0, weights)
    second0 = over_replica("ring0_1", far0, RING)
    own12 = join("join12", 2, from_own + rests, (far0,))
    oth12 = over_replica("core_rows12", own12, CORE)
    mid0, near0, home0, ret0, swap0 = expert(
        "expert0_rest", 0, 0, tbl, 2, (2, 2, 2), True, own0, oth0, weights, sums, (own12,)
    )
    mid0, swap0, second0 = lax.optimization_barrier((mid0, swap0, second0))
    second0 = add(mid0, second0)
    third0 = over_replica("ring0_2", second0, RING)
    swap0 = over_replica("core_back0", swap0, CORE)
    cross1, *mine1, ret1, swap1 = expert(
        "expert1", 1, 0, tbl, 8, (4, 1, 1, 1, 1), True, own12, oth12, weights, (), (second0,)
    )
    cross1, swap1, third0 = lax.optimization_barrier((cross1, swap1, third0))
    third0 = add(near0, third0)
    last0 = over_replica("ring0_3", third0, RING)
    crossed1 = over_replica("cross1", cross1, ACROSS)
    swap1 = over_replica("core_back1", swap1, CORE)
    far2, *sums = expert(
        "expert2_first", 2, 1, tbl, 0, (2,), False, own12, oth12, weights, (), (third0, ret1)
    )
    second2 = over_replica("ring2_1", far2, RING)
    back0 = back("back0", (ret0, swap0), (far2,))
    rows0 = [back0[0]] + [to_z("rows_back0", back0[dz], 4 - dz) for dz in range(1, 4)]
    across0 = add(home0[1], last0[1])
    mid2, near2, home2, ret2, swap2 = expert(
        "expert2_rest", 2, 1, tbl, 2, (2, 2, 2), True, own12, oth12, weights, sums,
        (back0[0], across0),
    )
    rows0 = [rows0[dz] for dz in Z_BACK]
    mid2, swap2, second2, *rows0 = lax.optimization_barrier((mid2, swap2, second2, *rows0))
    swap2 = over_replica("core_back2", swap2, CORE)
    third2 = over_replica("ring2_2", add(mid2, second2), RING)
    back12 = back("back12", (ret1, swap1, ret2, swap2))
    rows12 = [back12[0]] + [to_z("rows_back12", back12[dz], 4 - dz) for dz in range(1, 4)]
    third2, crossed1, across0, _ = lax.optimization_barrier((third2, crossed1, across0, back12[0]))
    third = ring_sums(
        "ring_sums",
        [((0, 0), (1, 0)), ((0, 1), (1, 1)), ((2, 0), (3, 1))],
        (near2, third2, mine1[1], crossed1),
    )
    third = over_replica("ring2_3", third, RING)
    across0 = over_replica("across0", across0, ACROSS)
    rows = rows0 + [rows12[dz] for dz in Z_BACK]
    theirs = token_outputs("partner_sums", 1, BF16, me, partner, rows)
    with jax.named_scope("partner_out"):
        others = lax.ppermute(theirs, "expert", PARTNER)
    mine = token_outputs("own_sums", 0, F32, me, packed, rows, (theirs,))
    third, across0, mine = lax.optimization_barrier((third, across0, mine))
    across2 = over_replica("across2", add(home2[1], third[1]), ACROSS)
    ring1 = over_replica("ring1_2", add(mine1[2][0], crossed1[2], third[2]), RING)
    far1 = over_replica("ring1_far", add(mine1[0][0], crossed1[0]), OTHER_WAY)
    ring1, others = lax.optimization_barrier((ring1, others))
    mixed, token_grad = add(mine[0], others[0]), add(mine[1], others[1])
    parts = [add(home0[0], last0[0]), across0]
    parts += [add(mine1[3][0], crossed1[3], far1), ring1]
    parts += [add(home2[0], third[0]), across2]
    gate_grad, up_grad, down_grad = call(
        finish_kernel, "finish", [VMEM] * len(parts),
        [bf16_like(LOCAL, D, BLK), bf16_like(LOCAL, D, BLK), bf16_like(LOCAL, BLK, D)],
        parts, 4 * 10**6,
    )
    return mixed, token_grad, gate_grad, up_grad, down_grad


def solution(mesh):
    tokens = P(("expert", "replica"), None)
    return jax.shard_map(
        local,
        mesh=mesh,
        in_specs=(tokens,) * 4 + (P("expert", None, None),) * 3,
        out_specs=(tokens,) * 2
        + (P("expert", None, "replica"), P("expert", None, "replica"), P("expert", "replica", None)),
        check_vma=False,
    )
```
